32 devices in a mesh: lat: 8 (over z, x), lon: 4 (over y, core).
Axes of the slice: x: 2, y: 2, z: 4, core: 2. Of those that a mesh axis runs over, the one named last changes fastest.
Arguments:
- observed: float32 [1024, 2048], P(('lat', 'lon')), may hold values from -12 to 12
- gauged: int32 [1024, 2048], P('lat', 'lon'), may hold values from 0 to 1, as said below
Outputs:
- coarsest_coeffs: float32 [128, 256], P('lat', 'lon')
- coarse_coeffs: float32 [256, 512], P('lat', 'lon')
- fine_coeffs: float32 [512, 1024], P('lat', 'lon')
- finest_coeffs: float32 [1024, 2048], P('lat', 'lon')
- imputed: float32 [1024, 2048], P(('lat', 'lon'))
The draws below stay inside these ranges and needn't reach their ends.
Inputs may be any that keep to these rules, and one draw needn't show every extreme that they name: 1 marks a gauged cell.
All inputs are finite; a program needn't handle non-finite values.
Results may differ from the reference program's by a relative error of at most 0.00029.
Values sent between devices are 32-bit elements; how exact they have to be, the bound alone decides.
No kernel may reach another device: no remote copies, remote signals or barrier semaphores. Data moves between devices by JAX's collectives and lax.ppermute only.
A program may use at most 64 MiB of HBM per device.

```python
import math
import jax
import jax.numpy as jnp
from jax import lax

LEVELS = 4
ITERS = 2
NLAT = 1024
NLON = 2048


def draw_observed(key, part):
    lon_frac = jnp.arange(NLON, dtype=jnp.float32)[None, :] / NLON
    amplitude = 0.3 * jnp.exp(jnp.log(10.0) * lon_frac)
    rough = jnp.clip(jax.random.normal(key, (NLAT, NLON), jnp.float32), -4.0, 4.0)
    return rough * amplitude


def draw_gauged(key, part):
    row_index = jnp.arange(NLAT, dtype=jnp.int32)[:, None]
    threshold = 200 + 600 * row_index // NLAT
    drawn = jax.random.randint(key, (NLAT, NLON), 0, 1000, dtype=jnp.int32)
    return (drawn < threshold).astype(jnp.int32)


def setup_inputs(seed: int = 0) -> dict:
    key_of = jax.random.split(jax.random.key(seed), 3)
    observed = draw_observed(jax.random.fold_in(key_of[2], 71), 0)
    gauged = draw_gauged(jax.random.fold_in(key_of[2], 71), 0)
    return {"observed": observed, "gauged": gauged}


highest = lax.Precision.HIGHEST
data_weight = 2.0
kappa_term = 5.0
level_scales = (0.02, 0.03, 0.05, 0.08)

def wendland(distance):
    remain = jnp.maximum(1.0 - distance, 0.0)
    return remain ** 6 * (35.0 * distance * distance + 18.0 * distance + 3.0) / 3.0

def weights_table(spacing):
    offsets = jnp.arange(spacing, dtype=jnp.int32)[:, None]
    shifts = jnp.arange(5, dtype=jnp.int32)[None, :] - 2
    numerator = jnp.abs(2 * offsets - 2 * spacing * shifts - (spacing - 1))
    return wendland(numerator.astype(jnp.float32) / (5.0 * spacing)) / math.sqrt(spacing)

def spread(coeffs, table, spacing):
    node_count = coeffs.shape[0]
    padded = jnp.pad(coeffs, ((2, 2), (0, 0)))
    result = jnp.zeros((node_count, spacing, coeffs.shape[1]), jnp.float32)
    for offset in range(5):
        result = result + table[:, offset][None, :, None] * padded[offset:offset + node_count][:, None, :]
    return result.reshape(node_count * spacing, coeffs.shape[1])

def collect(surface, table, spacing):
    node_count = surface.shape[0] // spacing
    blocks = surface.reshape(node_count, spacing, surface.shape[1])
    accum = jnp.zeros((node_count, surface.shape[1]), jnp.float32)
    for offset in range(5):
        summed = jnp.einsum('ntm,t->nm', blocks, table[:, offset], precision=highest)
        padded = jnp.pad(summed, ((2, 2), (0, 0)))
        accum = accum + padded[4 - offset:4 - offset + node_count]
    return accum

def synthesize(coeffs, spacings):
    surface = jnp.zeros((NLAT, NLON), jnp.float32)
    for level_idx in range(LEVELS):
        spacing = spacings[level_idx]
        table = weights_table(spacing)
        row_part = spread(coeffs[level_idx], table, spacing)
        surface = surface + spread(row_part.T, table, spacing).T
    return surface

def adjoint_all(misfit, spacings):
    result = []
    for level_idx in range(LEVELS):
        spacing = spacings[level_idx]
        table = weights_table(spacing)
        row_part = collect(misfit, table, spacing)
        result.append(collect(row_part.T, table, spacing).T)
    return result

def autoreg(coeffs):
    padded = jnp.pad(coeffs, 1)
    beside = padded[2:, 1:-1] + padded[:-2, 1:-1] + padded[1:-1, 2:] + padded[1:-1, :-2]
    return kappa_term * coeffs - beside

def apply_operator(coeffs, gauge_float, spacings):
    surface = synthesize(coeffs, spacings)
    backs = adjoint_all(data_weight * gauge_float * surface, spacings)
    curv_sum = data_weight * jnp.sum(gauge_float * surface * surface)
    images = []
    for level_idx in range(LEVELS):
        smoothed = autoreg(coeffs[level_idx])
        images.append(backs[level_idx] + level_scales[level_idx] * autoreg(smoothed))
        curv_sum = curv_sum + level_scales[level_idx] * jnp.sum(smoothed * smoothed)
    return (images, curv_sum)

def level_products(first, second):
    accum = jnp.float32(0.0)
    for level_idx in range(LEVELS):
        accum = accum + jnp.sum(first[level_idx] * second[level_idx])
    return accum

def reference(observed, gauged):
    spacings = [2 ** (LEVELS - 1 - level_idx) for level_idx in range(LEVELS)]
    gauge_float = gauged.astype(jnp.float32)
    right_side = adjoint_all(data_weight * gauge_float * observed, spacings)
    solution = [jnp.zeros_like(part_now) for part_now in right_side]
    residual = right_side
    search = right_side
    res_norm = level_products(residual, residual)
    for iteration in range(ITERS):
        images, curv_sum = apply_operator(search, gauge_float, spacings)
        step_size = res_norm / curv_sum
        solution = [solution[k] + step_size * search[k] for k in range(LEVELS)]
        if iteration + 1 < ITERS:
            residual = [residual[k] - step_size * images[k] for k in range(LEVELS)]
            new_norm = level_products(residual, residual)
            search = [residual[k] + new_norm / res_norm * search[k] for k in range(LEVELS)]
            res_norm = new_norm
    imputed = synthesize(solution, spacings)
    return (solution[0], solution[1], solution[2], solution[3], imputed)
```

```python
import math

import jax
import jax.numpy as jnp
import numpy as np
from jax import lax
from jax.experimental import pallas as pl
from jax.experimental.pallas import tpu as pltpu
from jax.sharding import PartitionSpec as P

LEVELS = 4
SPACINGS = tuple(2 ** (LEVELS - 1 - k) for k in range(LEVELS))
COARSE = LEVELS - 1
HALO = 64
INNER = 32
LANES = 128

data_weight = 2.0
kappa_term = 5.0
level_scales = (0.02, 0.03, 0.05, 0.08)

VMEM_LIMIT = 48 * 1024 * 1024


def wendland(distance):
    remain = np.maximum(1.0 - distance, 0.0)
    return remain**6 * (35.0 * distance * distance + 18.0 * distance + 3.0) / 3.0


def frame_index(total, tile, halo):
    place = np.arange(total)
    index = np.where(place < tile + halo, place, place - total)
    return index, (place < tile + halo) | (place >= total - halo)


def basis(cells, nodes, spacing):
    (cell, cell_ok), (node, node_ok) = cells, nodes
    numerator = np.abs(2 * cell[:, None] - 2 * spacing * node[None, :] - (spacing - 1))
    table = wendland(numerator / (5.0 * spacing)) / math.sqrt(spacing)
    return np.where(cell_ok[:, None] & node_ok[None, :], table, 0.0).astype(np.float32)


def halves(table):
    high = table.astype(jnp.bfloat16)
    low = (table - high.astype(np.float32)).astype(jnp.bfloat16)
    return np.stack([high, low])


def split(x):
    high = x.astype(jnp.bfloat16)
    return high, (x - high.astype(jnp.float32)).astype(jnp.bfloat16)


def dot(a, b, contract):
    return lax.dot_general(a, b, ((contract[0:1], contract[1:2]), ((), ())), preferred_element_type=jnp.float32)


def dot3(a, b, contract=(1, 0)):
    (ah, al), (bh, bl) = a, b
    return dot(ah, bh, contract) + (dot(ah, bl, contract) + dot(al, bh, contract))


TAPS = (float(wendland(np.float64(0.4))), float(wendland(np.float64(0.8))))


def shift(x, step, axis):
    return pltpu.roll(x, step % x.shape[axis], axis)


def smooth(x):
    for axis in (0, 1):
        near = shift(x, 1, axis) + shift(x, -1, axis)
        far = shift(x, 2, axis) + shift(x, -2, axis)
        x = x + (TAPS[0] * near + TAPS[1] * far)
    return x


def autoreg(x):
    beside = shift(x, 1, 0) + shift(x, -1, 0) + shift(x, 1, 1) + shift(x, -1, 1)
    return kappa_term * x - beside


def side_mask(total, tile, halo, at, last, dim):
    shape = (total, 1) if dim == 0 else (1, total)
    place = lax.broadcasted_iota(jnp.int32, shape, dim)
    after = (place < tile + halo) & (at < last)
    before = (place >= total - halo) & (at > 0)
    return ((place < tile) | after | before).astype(jnp.float32)


def fold(x):
    rows, cols = x.shape
    total = x[0:8]
    for r in range(8, rows, 8):
        total = total + x[r : r + 8]
    if cols < LANES:
        return jnp.concatenate([total, jnp.zeros((8, LANES - cols), jnp.float32)], axis=1)
    out = total[:, 0:LANES]
    for c in range(LANES, cols, LANES):
        out = out + total[:, c : c + LANES]
    return out


class Plan:
    def __init__(self, swath_shape, tile_shape, lat_total, lon_total):
        self.swath_rows, self.width = swath_shape
        self.rows, self.cols = tile_shape
        self.lat_total, self.lon_total = lat_total, lon_total
        self.row_frame = self.rows + 2 * HALO
        self.col_frame = self.cols + 2 * HALO
        self.inner_rows = self.rows + 2 * INNER
        self.node_rows = [self.row_frame // s for s in SPACINGS]
        self.node_cols = [-(-self.col_frame // (s * LANES)) * LANES for s in SPACINGS]
        self.row_starts = np.cumsum([0] + self.node_rows[:COARSE]).tolist()
        col_cells = frame_index(self.col_frame, self.cols, HALO)
        outer = frame_index(self.row_frame, self.rows, HALO)
        inner = frame_index(self.inner_rows, self.rows, INNER)
        col_tables, outer_rows, inner_rows = [], [], []
        for k in range(COARSE):
            s = SPACINGS[k]
            col_nodes = frame_index(self.node_cols[k], self.cols // s, HALO // s)
            row_nodes = frame_index(self.node_rows[k], self.rows // s, HALO // s)
            col_tables.append(halves(basis(col_cells, col_nodes, s)))
            outer_rows.append(basis(outer, row_nodes, s))
            inner_rows.append(basis(inner, row_nodes, s))
        outer_all = np.concatenate(outer_rows, axis=1)
        inner_all = np.concatenate(inner_rows, axis=1)
        self.tables = [
            *col_tables,
            halves(outer_all.T.copy()),
            halves(inner_all.T.copy()),
            halves(inner_all),
        ]


def call(kernel, outs, scratch=()):
    def run(*operands):
        return pl.pallas_call(
            kernel,
            out_shape=[jax.ShapeDtypeStruct(shape, jnp.float32) for shape in outs],
            in_specs=[pl.BlockSpec(memory_space=pltpu.VMEM)] * len(operands),
            out_specs=[pl.BlockSpec(memory_space=pltpu.VMEM)] * len(outs),
            scratch_shapes=list(scratch),
            compiler_params=pltpu.CompilerParams(vmem_limit_bytes=VMEM_LIMIT),
        )(*operands)

    return run


def pack(plan, observed, gauged):
    sr, width, cols, rows = plan.swath_rows, plan.width, plan.cols, plan.rows
    tiles = plan.col_frame // LANES

    def kernel(obs_ref, gauge_ref, own_ref, pair_ref, *rest):
        far_refs, odd_ref, wide = rest[:-2], rest[-2], rest[-1]
        at = lax.axis_index("lon")
        wide[:, 0:LANES] = jnp.zeros((sr, LANES), jnp.float32)
        wide[:, LANES : LANES + width] = obs_ref[...]
        wide[:, LANES + width :] = jnp.zeros((sr, LANES), jnp.float32)
        lane = lax.broadcasted_iota(jnp.int32, (sr, LANES), 1)

        def window(to):
            base = pl.multiple_of(to * cols, LANES)
            before = wide[:, pl.ds(base, LANES)]
            after = wide[:, pl.ds(base + LANES + cols, LANES)]
            return wide[:, pl.ds(base + LANES, cols)], jnp.where(lane < HALO, after, before)

        for k, ref in [(0, own_ref)] + list(enumerate(far_refs, 2)):
            main, sides = window(at ^ k)
            ref[:, 0:cols] = main
            ref[:, cols:] = sides
        main, sides = window(at ^ 1)
        for t in range(tiles - 1):
            pair_ref[t * sr : (t + 1) * sr, :] = main[:, t * LANES : (t + 1) * LANES]
        pair_ref[(tiles - 1) * sr : tiles * sr, :] = sides
        even = at % 2 == 0
        first = gauge_ref[:, 0:LANES].astype(jnp.float32)
        last = gauge_ref[:, cols - LANES :].astype(jnp.float32)
        pair_ref[tiles * sr :, :] = jnp.where(even, last, first)
        odd_ref[...] = jnp.where(even, first, last)

    outs = [(sr, plan.col_frame), (tiles * sr + rows, LANES)]
    outs += [(sr, plan.col_frame)] * (plan.lon_total - 2)
    outs += [(rows, LANES)]
    scratch = [pltpu.VMEM((sr, width + 2 * LANES), jnp.float32)]
    return call(kernel, outs, scratch)(observed, gauged)


def misfit(plan, own, pair, far, odd, gauged):
    sr, cols, rows = plan.swath_rows, plan.cols, plan.rows
    tiles = plan.col_frame // LANES

    def kernel(own_ref, pair_ref, odd_ref, gauge_ref, *rest):
        far_refs, (mis_ref, wt_ref, near_ref, next_ref) = rest[:-4], rest[-4:]
        at = lax.axis_index("lon")
        lat = lax.axis_index("lat")
        even = at % 2 == 0
        lane = lax.broadcasted_iota(jnp.int32, (rows, LANES), 1)
        from_pair = pair_ref[tiles * sr :, :]
        from_odd = odd_ref[...]
        right = jnp.where(even, from_pair, from_odd)
        left = jnp.where(even, from_odd, from_pair)
        wt_ref[:, 0:cols] = data_weight * gauge_ref[...].astype(jnp.float32)
        wt_ref[:, cols:] = data_weight * jnp.where(lane < HALO, right, left)

        def rows_of(k):
            return pl.ds(pl.multiple_of((at ^ k) * sr, sr), sr)

        for k, ref in [(0, own_ref)] + list(enumerate(far_refs, 2)):
            mis_ref[rows_of(k), :] = wt_ref[rows_of(k), :] * ref[...]
        for t in range(tiles):
            lanes = slice(t * LANES, (t + 1) * LANES)
            mis_ref[rows_of(1), lanes] = wt_ref[rows_of(1), lanes] * pair_ref[t * sr : (t + 1) * sr, :]
        up = lat % 2
        for ref, low in ((near_ref, 1 - up), (next_ref, up)):
            ref[0:HALO, :] = mis_ref[pl.ds(pl.multiple_of(low * (rows - HALO), 8), HALO), :]
            ref[HALO:, :] = wt_ref[pl.ds(pl.multiple_of(low * (rows - INNER), 8), INNER), :]

    outs = [(rows, plan.col_frame)] * 2 + [(HALO + INNER, plan.col_frame)] * 2
    return call(kernel, outs)(own, pair, odd, gauged, *far)


def operate(plan, mis, wt, near, following):
    rows, cols, sr, lon_total = plan.rows, plan.cols, plan.swath_rows, plan.lon_total
    starts = plan.row_starts
    inner_rows = plan.inner_rows
    n_tables = len(plan.tables)
    n_dev = plan.lat_total * lon_total

    def kernel(mis_ref, wt_ref, near_ref, next_ref, *rest):
        table_refs, out_refs = rest[:n_tables], rest[n_tables:]
        base_refs, image_refs = out_refs[:LEVELS], out_refs[LEVELS : 2 * LEVELS]
        surface_refs, part_ref = out_refs[2 * LEVELS : -1], out_refs[-1]
        lat = lax.axis_index("lat")
        lon = lax.axis_index("lon")
        even = lat % 2 == 0
        tables = [(ref[0], ref[1]) for ref in table_refs]
        col_tables, outer_t, inner_t, inner_s = tables[:COARSE], *tables[COARSE:]

        near_all, next_all = near_ref[...], next_ref[...]
        below = jnp.where(even, near_all, next_all)
        above = jnp.where(even, next_all, near_all)
        outer = jnp.concatenate([mis_ref[...], below[0:HALO], above[0:HALO]], axis=0)
        weight = jnp.concatenate([wt_ref[...], below[HALO:], above[HALO:]], axis=0)

        masks = []
        for k in range(LEVELS):
            s = SPACINGS[k]
            masks.append(
                side_mask(plan.node_rows[k], rows // s, HALO // s, lat, plan.lat_total - 1, 0)
                * side_mask(plan.node_cols[k], cols // s, HALO // s, lon, lon_total - 1, 1)
            )
        inner_mask = side_mask(inner_rows, rows, INNER, lat, plan.lat_total - 1, 0) * side_mask(
            plan.col_frame, cols, HALO, lon, lon_total - 1, 1
        )

        def collect(values, row_table):
            gathered = dot3(row_table, split(values))
            return [
                dot3(split(gathered[starts[k] : starts[k + 1]]), col_tables[k]) for k in range(COARSE)
            ]

        def spread(coeffs):
            return split(
                jnp.concatenate([dot3(split(coeffs[k]), col_tables[k], (1, 1)) for k in range(COARSE)], axis=0)
            )

        def cut(x):
            return jnp.concatenate([x[0 : rows + INNER], x[x.shape[0] - INNER :]], axis=0)

        base = collect(outer, outer_t)
        base = [base[k] * masks[k] for k in range(COARSE)]
        finest = smooth(outer) * masks[COARSE]
        surface = dot3(inner_s, spread(base)) + cut(smooth(finest))
        base.append(cut(finest))
        masks[COARSE] = inner_mask

        image = collect(weight * surface, inner_t)
        image.append(smooth(weight * surface))
        rough_base, rough_image = [], []
        for k in range(LEVELS):
            once = autoreg(base[k]) * masks[k]
            rough_base.append(once)
            image[k] = (image[k] + level_scales[k] * autoreg(once)) * masks[k]
            rough_image.append(autoreg(image[k]))
        tile_table = tuple(part[0:rows] for part in inner_s)
        second = dot3(tile_table, spread(image)) + smooth(image[COARSE])[0:rows]

        own = [(slice(0, rows // s), slice(0, cols // s)) for s in SPACINGS]
        b = [base[k][own[k]] for k in range(LEVELS)]
        ab = [image[k][own[k]] for k in range(LEVELS)]
        rb = [rough_base[k][own[k]] for k in range(LEVELS)]
        rab = [rough_image[k][own[k]] for k in range(LEVELS)]
        sb, sab = surface[0:rows, 0:cols], second[:, 0:cols]
        w = weight[0:rows, 0:cols]

        for k in range(LEVELS):
            base_refs[k][...] = b[k]
            image_refs[k][...] = ab[k]
        surface_refs[0][0:rows, :] = sb
        surface_refs[0][rows:, :] = sab
        for k in range(1, lon_total):
            take = pl.ds(pl.multiple_of((lon ^ k) * sr, sr), sr)
            surface_refs[k][0:sr, :] = surface_refs[0][take, :]
            take = pl.ds(pl.multiple_of(rows + (lon ^ k) * sr, sr), sr)
            surface_refs[k][sr:, :] = surface_refs[0][take, :]

        def inner(first, other):
            total = fold(first[0] * other[0])
            for k in range(1, LEVELS):
                total = total + fold(first[k] * other[k])
            return total

        def curvature(first, other, field, other_field):
            total = fold(w * field * other_field)
            for k in range(LEVELS):
                total = total + level_scales[k] * fold(first[k] * other[k])
            return total

        a0 = inner(b, b)
        a1 = curvature(rb, rb, sb, sb)
        top = jnp.sum(a0, keepdims=True)
        bottom = jnp.sum(a1, keepdims=True)
        tau = jnp.where(bottom > 0.0, top / jnp.where(bottom > 0.0, bottom, 1.0), 0.0)
        r = [b[k] - tau * ab[k] for k in range(LEVELS)]
        rr = [rb[k] - tau * rab[k] for k in range(LEVELS)]
        sr_field = sb - tau * sab
        blocks = [
            a0,
            a1,
            inner(r, r),
            inner(r, ab),
            inner(ab, ab),
            curvature(rr, rr, sr_field, sr_field),
            curvature(rr, rab, sr_field, sab),
            curvature(rab, rab, sab, sab),
            curvature(rr, rb, sr_field, sb),
            curvature(rab, rb, sab, sb),
        ]
        lines = [jnp.sum(block, axis=0, keepdims=True) for block in blocks]
        lane = lax.broadcasted_iota(jnp.int32, (1, LANES), 1)
        lines.append(jnp.where(lane == 0, tau, 0.0))
        lines.append(jnp.zeros((16 - len(lines), LANES), jnp.float32))
        sums = jnp.sum(jnp.concatenate(lines, axis=0), axis=1, keepdims=True)
        place = lax.broadcasted_iota(jnp.int32, (16, LANES), 0)
        lanes = lax.broadcasted_iota(jnp.int32, (16, LANES), 1)
        line = jnp.sum(jnp.where(place == lanes, sums, 0.0), axis=0, keepdims=True)
        part_ref[...] = jnp.broadcast_to(line, (n_dev, LANES))

    level_shapes = [(rows // s, cols // s) for s in SPACINGS]
    outs = level_shapes * 2 + [(2 * rows, cols)] + [(2 * sr, cols)] * (lon_total - 1) + [(n_dev, LANES)]
    tables = [jnp.asarray(t) for t in plan.tables]
    results = call(kernel, outs)(mis, wt, near, following, *tables)
    return results[:LEVELS], results[LEVELS : 2 * LEVELS], results[2 * LEVELS : -1], results[-1]


def finish(plan, parts, base, image, own_surface, far_surfaces):
    rows, cols, sr, lon_total = plan.rows, plan.cols, plan.swath_rows, plan.lon_total

    def kernel(part_ref, *rest):
        base_refs, image_refs = rest[:LEVELS], rest[LEVELS : 2 * LEVELS]
        own_ref, far_refs = rest[2 * LEVELS], rest[2 * LEVELS + 1 : 2 * LEVELS + lon_total]
        out_refs, swath_ref = rest[-LEVELS - 1 : -1], rest[-1]
        lon = lax.axis_index("lon")
        part = part_ref[...]
        lane = lax.broadcasted_iota(jnp.int32, part.shape, 1)

        def column(n):
            return jnp.sum(jnp.where(lane == n, part, 0.0), axis=1, keepdims=True)

        def total(values):
            return jnp.sum(values, axis=0, keepdims=True)

        a0, a1, p1, p2, p3, c1, c2, c3, c4, c5, tau = [column(n) for n in range(11)]
        sum0, sum1 = total(a0), total(a1)
        step = sum0 / sum1
        gap = tau - step
        norm = total(p1 + 2.0 * gap * p2 + gap * gap * p3)
        curv_res = total(c1 + 2.0 * gap * c2 + gap * gap * c3)
        curv_mix = total(c4 + gap * c5)
        ratio = norm / sum0
        curv = curv_res + 2.0 * ratio * curv_mix + ratio * ratio * sum1
        next_step = norm / curv
        alpha = step + next_step * (1.0 + ratio)
        beta = -next_step * step
        for k in range(LEVELS):
            out_refs[k][...] = alpha * base_refs[k][...] + beta * image_refs[k][...]
        take = pl.ds(pl.multiple_of(lon * sr, sr), sr)
        later = pl.ds(pl.multiple_of(rows + lon * sr, sr), sr)
        fields = [(own_ref[take, :], own_ref[later, :])]
        fields += [(ref[0:sr, :], ref[sr:, :]) for ref in far_refs]
        for k in range(lon_total):
            here = pl.ds(pl.multiple_of((lon ^ k) * cols, LANES), cols)
            swath_ref[:, here] = alpha * fields[k][0] + beta * fields[k][1]

    outs = [(rows // s, cols // s) for s in SPACINGS] + [(sr, plan.width)]
    return call(kernel, outs)(parts, *base, *image, own_surface, *far_surfaces)


def flip(x, axis, total, k):
    return lax.ppermute(x, axis, [(i, i ^ k) for i in range(total)])


def odd_swap(x, axis, total):
    pairs = [(i, i + 1) for i in range(1, total - 1, 2)]
    return lax.ppermute(x, axis, pairs + [(j, i) for i, j in pairs])


def body(observed, gauged):
    lat_total, lon_total = lax.axis_size("lat"), lax.axis_size("lon")
    plan = Plan(observed.shape, gauged.shape, lat_total, lon_total)
    own, pair, *far, odd = pack(plan, observed, gauged)
    far = [flip(x, "lon", lon_total, k) for k, x in enumerate(far, 2)]
    odd = odd_swap(odd, "lon", lon_total)
    pair = flip(pair, "lon", lon_total, 1)
    mis, wt, near, following = misfit(plan, own, pair, far, odd, gauged)
    following = odd_swap(following, "lat", lat_total)
    near = flip(near, "lat", lat_total, 1)
    base, image, surfaces, parts = operate(plan, mis, wt, near, following)
    far_surfaces = [flip(x, "lon", lon_total, k) for k, x in enumerate(surfaces[1:], 1)]
    parts = lax.all_to_all(parts, ("lat", "lon"), split_axis=0, concat_axis=0, tiled=True)
    return tuple(finish(plan, parts, base, image, surfaces[0], far_surfaces))


def solution(mesh):
    return jax.shard_map(
        body,
        mesh=mesh,
        in_specs=(P(("lat", "lon"), None), P("lat", "lon")),
        out_specs=(
            P("lat", "lon"),
            P("lat", "lon"),
            P("lat", "lon"),
            P("lat", "lon"),
            P(("lat", "lon"), None),
        ),
        check_vma=False,
    )
```

```python
import math

import jax
import jax.numpy as jnp
import numpy as np
from jax import lax
from jax.experimental import pallas as pl
from jax.experimental.pallas import tpu as pltpu
from jax.sharding import PartitionSpec as P

LEVELS = 4
SPACINGS = tuple(2 ** (LEVELS - 1 - k) for k in range(LEVELS))
COARSE = LEVELS - 1
HALO = 64
INNER = 32
RAW = 40
PART_ROWS = 8
LANES = 128

data_weight = 2.0
kappa_term = 5.0
level_scales = (0.02, 0.03, 0.05, 0.08)

MIB = 1024 * 1024


def wendland(distance, of=np):
    remain = of.maximum(1.0 - distance, 0.0)
    cube = remain * remain * remain
    return cube * cube * (35.0 * distance * distance + 18.0 * distance + 3.0) / 3.0


def frame_index(total, tile, halo):
    place = np.arange(total)
    index = np.where(place < tile + halo, place, place - total)
    return index, (place < tile + halo) | (place >= total - halo)


def basis(cells, nodes, spacing):
    (cell, cell_ok), (node, node_ok) = cells, nodes
    numerator = np.abs(2 * cell[:, None] - 2 * spacing * node[None, :] - (spacing - 1))
    table = wendland(numerator / (5.0 * spacing)) / math.sqrt(spacing)
    return np.where(cell_ok[:, None] & node_ok[None, :], table, 0.0).astype(np.float32)


def halves(table):
    high = table.astype(jnp.bfloat16)
    low = (table - high.astype(np.float32)).astype(jnp.bfloat16)
    return np.stack([high, low])


def split(x):
    high = x.astype(jnp.bfloat16)
    return high, (x - high.astype(jnp.float32)).astype(jnp.bfloat16)


def dot(a, b, contract):
    return lax.dot_general(a, b, ((contract[0:1], contract[1:2]), ((), ())), preferred_element_type=jnp.float32)


def dot3(a, b, contract=(1, 0)):
    (ah, al), (bh, bl) = a, b
    return dot(ah, bh, contract) + (dot(ah, bl, contract) + dot(al, bh, contract))


TAPS = (float(wendland(np.float64(0.4))), float(wendland(np.float64(0.8))))


def shift(x, step, axis):
    return pltpu.roll(x, step % x.shape[axis], axis)


def smooth(x):
    for axis in (0, 1):
        near = shift(x, 1, axis) + shift(x, -1, axis)
        far = shift(x, 2, axis) + shift(x, -2, axis)
        x = x + (TAPS[0] * near + TAPS[1] * far)
    return x


def autoreg(x):
    beside = shift(x, 1, 0) + shift(x, -1, 0) + shift(x, 1, 1) + shift(x, -1, 1)
    return kappa_term * x - beside


def side_mask(total, tile, halo, at, last, dim):
    shape = (total, 1) if dim == 0 else (1, total)
    place = lax.broadcasted_iota(jnp.int32, shape, dim)
    after = (place < tile + halo) & (at < last)
    before = (place >= total - halo) & (at > 0)
    return ((place < tile) | after | before).astype(jnp.float32)


def fold(x):
    rows, cols = x.shape
    total = x[0:8]
    for r in range(8, rows, 8):
        total = total + x[r : r + 8]
    if cols < LANES:
        return jnp.concatenate([total, jnp.zeros((8, LANES - cols), jnp.float32)], axis=1)
    out = total[:, 0:LANES]
    for c in range(LANES, cols, LANES):
        out = out + total[:, c : c + LANES]
    return out


class Plan:
    def __init__(self, swath_shape, tile_shape, lat_total, lon_total):
        self.swath_rows, self.width = swath_shape
        self.rows, self.cols = tile_shape
        self.lat_total, self.lon_total = lat_total, lon_total
        self.col_frame = self.cols + 2 * HALO
        self.outer_rows = self.rows + 2 * RAW
        self.inner_rows = self.rows + 2 * INNER
        self.node_rows = [(self.rows + 2 * HALO) // s for s in SPACINGS[:COARSE]] + [self.outer_rows]
        self.node_cols = [-(-self.col_frame // (s * LANES)) * LANES for s in SPACINGS]
        self.row_starts = np.cumsum([0] + self.node_rows[:COARSE]).tolist()
        self.col_starts = np.cumsum([0] + self.node_cols[:COARSE]).tolist()
        col_cells = frame_index(self.col_frame, self.cols, HALO)
        outer = frame_index(self.outer_rows, self.rows, RAW)
        inner = frame_index(self.inner_rows, self.rows, INNER)
        col_tables, outer_rows, inner_rows = [], [], []
        self.part_nodes, place_all = [], []
        for k in range(COARSE):
            s = SPACINGS[k]
            tile = self.rows // s
            col_nodes = frame_index(self.node_cols[k], self.cols // s, HALO // s)
            row_nodes = frame_index(self.node_rows[k], tile, HALO // s)
            col_tables.append(basis(col_cells, col_nodes, s))
            outer_rows.append(basis(outer, row_nodes, s))
            inner_rows.append(basis(inner, row_nodes, s))
            for away in range((RAW - 2 * s) // s, INNER // s + 2):
                self.part_nodes.append((s, away))
                at = self.row_starts[k]
                place_all.append((at + tile + away, at + self.node_rows[k] - 1 - away))
        nodes = self.row_starts[-1]
        joins = np.zeros((2 * PART_ROWS, nodes), np.float32)
        for n, (after_at, before_at) in enumerate(place_all):
            joins[n, after_at] = 1.0
            joins[PART_ROWS + n, before_at] = 1.0
        outer_all = np.concatenate([np.concatenate(outer_rows, axis=1), joins], axis=0)
        inner_all = np.concatenate(inner_rows, axis=1)
        row_tables = [outer_all.T, inner_all.T, inner_all]
        self.row_places, at = [], 0
        for table in row_tables:
            self.row_places.append((at, table.shape[0], table.shape[1]))
            at += table.shape[0]
        lanes = -(-max(t.shape[1] for t in row_tables) // LANES) * LANES
        col_all = np.concatenate(col_tables, axis=1)
        self.turned_start = self.col_starts[-1] + lanes
        whole = np.zeros((max(at, *col_all.shape), self.turned_start + self.col_frame), np.float32)
        whole[: self.col_frame, : self.col_starts[-1]] = col_all
        whole[: self.col_starts[-1], self.turned_start :] = col_all.T
        for (start, height, width), table in zip(self.row_places, row_tables):
            whole[start : start + height, self.col_starts[-1] : self.col_starts[-1] + width] = table
        self.tables = halves(whole)


def call(kernel, outs, limit, scratch=(), spaces=None):
    def run(*operands):
        in_spaces = spaces or [pltpu.VMEM] * len(operands)
        return pl.pallas_call(
            kernel,
            out_shape=[jax.ShapeDtypeStruct(shape, jnp.float32) for shape in outs],
            in_specs=[pl.BlockSpec(memory_space=space) for space in in_spaces],
            out_specs=[pl.BlockSpec(memory_space=pltpu.VMEM)] * len(outs),
            scratch_shapes=list(scratch),
            compiler_params=pltpu.CompilerParams(vmem_limit_bytes=limit * MIB),
        )(*operands)

    return run


def opposite(plan, observed):
    sr, width, cols, n = plan.swath_rows, plan.width, plan.cols, plan.lon_total

    def kernel(obs_ref, *out_refs):
        at = lax.axis_index("lon")
        for k, ref in enumerate(out_refs, 2):
            main, sides = window(plan, obs_ref, lax.rem(at + k, n))
            ref[:, 0:cols] = main
            ref[:, cols:] = sides

    return call(kernel, [(sr, plan.col_frame)] * (n - 3), 4)(observed)


def window(plan, obs_ref, to):
    sr, width, cols = plan.swath_rows, plan.width, plan.cols
    base = pl.multiple_of(to * cols, LANES)
    lane = lax.broadcasted_iota(jnp.int32, (sr, LANES), 1)
    before = obs_ref[:, pl.ds(pl.multiple_of(jnp.maximum(base - LANES, 0), LANES), LANES)]
    after = obs_ref[:, pl.ds(pl.multiple_of(jnp.minimum(base + cols, width - LANES), LANES), LANES)]
    before = jnp.where(to > 0, before, 0.0)
    after = jnp.where(to < plan.lon_total - 1, after, 0.0)
    return obs_ref[:, pl.ds(base, cols)], jnp.where(lane < HALO, after, before)


def beside(plan, observed, weight):
    sr, cols, rows, n = plan.swath_rows, plan.cols, plan.rows, plan.lon_total
    tiles = plan.col_frame // LANES

    def kernel(obs_ref, wt_ref, own_ref, right_ref, left_ref):
        at = lax.axis_index("lon")
        main, sides = window(plan, obs_ref, at)
        own_ref[:, 0:cols] = main
        own_ref[:, cols:] = sides
        half_lane = lax.broadcasted_iota(jnp.int32, (rows // 2, LANES), 1)
        for ref, k in ((right_ref, 1), (left_ref, n - 1)):
            main, sides = window(plan, obs_ref, lax.rem(at + k, n))
            for t in range(tiles - 1):
                ref[t * sr : (t + 1) * sr, :] = main[:, t * LANES : (t + 1) * LANES]
            ref[(tiles - 1) * sr : tiles * sr, :] = sides
            edge = wt_ref[:, cols - LANES :] if k == 1 else wt_ref[:, 0:LANES]
            kept = (half_lane >= HALO) if k == 1 else (half_lane < HALO)
            turned = pltpu.roll(edge[rows // 2 :], HALO, 1)
            ref[tiles * sr :, :] = jnp.where(kept, edge[0 : rows // 2], turned)

    side = (tiles * sr + rows // 2, LANES)
    outs = [(sr, plan.col_frame), side, side]
    return call(kernel, outs, 4)(observed, weight)


def misfit(plan, own, right, left, far, weight):
    sr, cols, rows, n = plan.swath_rows, plan.cols, plan.rows, plan.lon_total
    tiles = plan.col_frame // LANES

    def kernel(own_ref, right_ref, left_ref, wt_ref, *rest):
        far_refs, (mis_ref, side_ref, near_ref, next_ref) = rest[: n - 3], rest[n - 3 :]
        at = lax.axis_index("lon")
        lane = lax.broadcasted_iota(jnp.int32, (rows, LANES), 1)

        def side(ref, present):
            packed = ref[tiles * sr :, :]
            both = jnp.concatenate([packed, pltpu.roll(packed, HALO, 1)], axis=0)
            return jnp.where(present, both, 0.0)

        side_ref[...] = jnp.where(lane < HALO, side(left_ref, at < n - 1), side(right_ref, at > 0))

        for k, ref in enumerate((own_ref, right_ref, *far_refs, left_ref)):
            here = pl.ds(pl.multiple_of(lax.rem(at + (n - k), n) * sr, sr), sr)
            if k in (1, n - 1):
                for t in range(tiles - 1):
                    lanes = slice(t * LANES, (t + 1) * LANES)
                    mis_ref[here, lanes] = wt_ref[here, lanes] * ref[t * sr : (t + 1) * sr, :]
                mis_ref[here, cols:] = side_ref[here, :] * ref[(tiles - 1) * sr : tiles * sr, :]
            else:
                mis_ref[here, 0:cols] = wt_ref[here, :] * ref[:, 0:cols]
                mis_ref[here, cols:] = side_ref[here, :] * ref[:, cols:]

        up = lax.axis_index("lat") % 2
        depth = HALO - RAW
        shape = (PART_ROWS, depth)
        line = lax.broadcasted_iota(jnp.int32, shape, 0)
        cell = lax.broadcasted_iota(jnp.int32, shape, 1)
        for ref, low in ((near_ref, 1 - up), (next_ref, up)):
            far = mis_ref[pl.ds(pl.multiple_of(RAW + low * (rows - HALO - RAW), 8), depth), :]
            table = jnp.zeros(shape, jnp.float32)
            distance = jnp.where(low == 1, HALO - 1 - cell, RAW + cell)
            for m, (s, away) in enumerate(plan.part_nodes):
                numerator = jnp.abs(2 * distance - 2 * s * away - (s - 1)).astype(jnp.float32)
                table = jnp.where(line == m, wendland(numerator / (5.0 * s), jnp) / math.sqrt(s), table)
            ref[0:RAW, :] = mis_ref[pl.ds(pl.multiple_of(low * (rows - RAW), 8), RAW), :]
            ref[RAW : RAW + PART_ROWS, :] = jnp.dot(
                table, far, precision=lax.Precision.HIGHEST, preferred_element_type=jnp.float32
            )
            edge = pl.ds(pl.multiple_of(low * (rows - INNER), 8), INNER)
            ref[RAW + PART_ROWS :, 0:cols] = wt_ref[edge, :]
            ref[RAW + PART_ROWS :, cols:] = side_ref[edge, :]

    outs = [(rows, plan.col_frame), (rows, LANES)] + [(RAW + PART_ROWS + INNER, plan.col_frame)] * 2
    return call(kernel, outs, 4)(own, right, left, weight, *far)


def fetch(plan, after):
    def kernel(table_ref, after_ref, out_ref, sem):
        copy = pltpu.make_async_copy(table_ref, out_ref, sem)
        copy.start()
        copy.wait()

    table = jnp.asarray(plan.tables)
    return pl.pallas_call(
        kernel,
        out_shape=jax.ShapeDtypeStruct(table.shape, table.dtype),
        in_specs=[pl.BlockSpec(memory_space=pltpu.HBM), pl.BlockSpec(memory_space=pltpu.VMEM)],
        out_specs=pl.BlockSpec(memory_space=pltpu.VMEM),
        scratch_shapes=[pltpu.SemaphoreType.DMA],
        compiler_params=pltpu.CompilerParams(vmem_limit_bytes=MIB),
        cost_estimate=pl.CostEstimate(flops=0, bytes_accessed=2 * table.nbytes, transcendentals=0),
    )(table, after)


def operate(plan, mis, wt, side, near, following, tables):
    rows, cols, sr, lon_total = plan.rows, plan.cols, plan.swath_rows, plan.lon_total
    starts = plan.row_starts
    inner_rows = plan.inner_rows
    n_dev = plan.lat_total * lon_total

    def kernel(mis_ref, wt_ref, side_ref, near_ref, next_ref, table_ref, *out_refs):
        base_refs, image_refs = out_refs[:LEVELS], out_refs[LEVELS : 2 * LEVELS]
        surface_refs, part_ref = out_refs[2 * LEVELS : -1], out_refs[-1]
        lat = lax.axis_index("lat")
        lon = lax.axis_index("lon")
        even = lat % 2 == 0
        col_tables, turned_tables, row_tables = [], [], []
        for k in range(COARSE):
            places = slice(plan.col_starts[k], plan.col_starts[k + 1])
            turned_tables.append(tuple(table_ref[half, places, plan.turned_start :] for half in (0, 1)))
            lanes = slice(plan.col_starts[k], plan.col_starts[k + 1])
            col_tables.append(tuple(table_ref[half, 0 : plan.col_frame, lanes] for half in (0, 1)))
        for start, height, width in plan.row_places:
            lanes = slice(plan.col_starts[-1], plan.col_starts[-1] + width)
            row_tables.append(tuple(table_ref[half, start : start + height, lanes] for half in (0, 1)))
        outer_t, inner_t, inner_s = row_tables

        near_all, next_all = near_ref[...], next_ref[...]
        below = jnp.where(even, near_all, next_all)
        above = jnp.where(even, next_all, near_all)
        cells = jnp.concatenate([mis_ref[...], below[0:RAW], above[0:RAW]], axis=0)
        sums = slice(RAW, RAW + PART_ROWS)
        outer = jnp.concatenate([cells, below[sums], above[sums]], axis=0)
        own_weight = jnp.concatenate([wt_ref[...], side_ref[...]], axis=1)
        weight = jnp.concatenate([own_weight, below[RAW + PART_ROWS :], above[RAW + PART_ROWS :]], axis=0)

        masks = []
        for k in range(LEVELS):
            s = SPACINGS[k]
            masks.append(
                side_mask(plan.node_rows[k], rows // s, (HALO if k < COARSE else RAW) // s, lat, plan.lat_total - 1, 0)
                * side_mask(plan.node_cols[k], cols // s, HALO // s, lon, lon_total - 1, 1)
            )
        inner_mask = side_mask(inner_rows, rows, INNER, lat, plan.lat_total - 1, 0) * side_mask(
            plan.col_frame, cols, HALO, lon, lon_total - 1, 1
        )

        def collect(values, row_table):
            gathered = dot3(row_table, split(values))
            return [
                dot3(split(gathered[starts[k] : starts[k + 1]]), col_tables[k]) for k in range(COARSE)
            ]

        def spread(coeffs):
            return split(
                jnp.concatenate([dot3(split(coeffs[k]), turned_tables[k]) for k in range(COARSE)], axis=0)
            )

        def cut(x):
            return jnp.concatenate([x[0 : rows + INNER], x[x.shape[0] - INNER :]], axis=0)

        base = collect(outer, outer_t)
        base = [base[k] * masks[k] for k in range(COARSE)]
        finest = smooth(cells) * masks[COARSE]
        surface = dot3(inner_s, spread(base)) + cut(smooth(finest))
        base.append(cut(finest))
        masks[COARSE] = inner_mask

        image = collect(weight * surface, inner_t)
        image.append(smooth(weight * surface))
        rough_base, rough_image = [], []
        for k in range(LEVELS):
            once = autoreg(base[k]) * masks[k]
            rough_base.append(once)
            image[k] = (image[k] + level_scales[k] * autoreg(once)) * masks[k]
            rough_image.append(autoreg(image[k]))
        tile_table = tuple(part[0:rows] for part in inner_s)
        second = dot3(tile_table, spread(image)) + smooth(image[COARSE])[0:rows]

        own = [(slice(0, rows // s), slice(0, cols // s)) for s in SPACINGS]
        b = [base[k][own[k]] for k in range(LEVELS)]
        ab = [image[k][own[k]] for k in range(LEVELS)]
        rb = [rough_base[k][own[k]] for k in range(LEVELS)]
        rab = [rough_image[k][own[k]] for k in range(LEVELS)]
        sb, sab = surface[0:rows, 0:cols], second[:, 0:cols]
        w = weight[0:rows, 0:cols]

        for k in range(LEVELS):
            base_refs[k][...] = b[k]
            image_refs[k][...] = ab[k]
        surface_refs[0][0:rows, :] = sb
        surface_refs[0][rows:, :] = sab
        for k in range(1, lon_total):
            take = pl.ds(pl.multiple_of((lon ^ k) * sr, sr), sr)
            surface_refs[k][0:sr, :] = surface_refs[0][take, :]
            take = pl.ds(pl.multiple_of(rows + (lon ^ k) * sr, sr), sr)
            surface_refs[k][sr:, :] = surface_refs[0][take, :]

        def inner(first, other):
            total = fold(first[0] * other[0])
            for k in range(1, LEVELS):
                total = total + fold(first[k] * other[k])
            return total

        def curvature(first, other, field, other_field):
            total = fold(w * field * other_field)
            for k in range(LEVELS):
                total = total + level_scales[k] * fold(first[k] * other[k])
            return total

        a0 = inner(b, b)
        a1 = curvature(rb, rb, sb, sb)
        top = jnp.sum(a0, keepdims=True)
        bottom = jnp.sum(a1, keepdims=True)
        tau = jnp.where(bottom > 0.0, top / jnp.where(bottom > 0.0, bottom, 1.0), 0.0)
        r = [b[k] - tau * ab[k] for k in range(LEVELS)]
        rr = [rb[k] - tau * rab[k] for k in range(LEVELS)]
        sr_field = sb - tau * sab
        blocks = [
            a0,
            a1,
            inner(r, r),
            inner(r, ab),
            inner(ab, ab),
            curvature(rr, rr, sr_field, sr_field),
            curvature(rr, rab, sr_field, sab),
            curvature(rab, rab, sab, sab),
            curvature(rr, rb, sr_field, sb),
            curvature(rab, rb, sab, sb),
        ]
        lines = [jnp.sum(block, axis=0, keepdims=True) for block in blocks]
        lane = lax.broadcasted_iota(jnp.int32, (1, LANES), 1)
        lines.append(jnp.where(lane == 0, tau, 0.0))
        lines.append(jnp.zeros((16 - len(lines), LANES), jnp.float32))
        sums = jnp.sum(jnp.concatenate(lines, axis=0), axis=1, keepdims=True)
        place = lax.broadcasted_iota(jnp.int32, (16, LANES), 0)
        lanes = lax.broadcasted_iota(jnp.int32, (16, LANES), 1)
        line = jnp.sum(jnp.where(place == lanes, sums, 0.0), axis=0, keepdims=True)
        part_ref[...] = jnp.broadcast_to(line, (n_dev, LANES))

    level_shapes = [(rows // s, cols // s) for s in SPACINGS]
    outs = level_shapes * 2 + [(2 * rows, cols)] + [(2 * sr, cols)] * (lon_total - 1) + [(n_dev, LANES)]
    results = call(kernel, outs, 24)(mis, wt, side, near, following, tables)
    return results[:LEVELS], results[LEVELS : 2 * LEVELS], results[2 * LEVELS : -1], results[-1]


def finish(plan, parts, base, image, own_surface, far_surfaces):
    rows, cols, sr, lon_total = plan.rows, plan.cols, plan.swath_rows, plan.lon_total

    def kernel(part_ref, *rest):
        base_refs, image_refs = rest[:LEVELS], rest[LEVELS : 2 * LEVELS]
        own_ref, far_refs = rest[2 * LEVELS], rest[2 * LEVELS + 1 : 2 * LEVELS + lon_total]
        out_refs, swath_ref = rest[-LEVELS - 1 : -1], rest[-1]
        lon = lax.axis_index("lon")
        part = part_ref[...]
        lane = lax.broadcasted_iota(jnp.int32, part.shape, 1)

        def column(n):
            return jnp.sum(jnp.where(lane == n, part, 0.0), axis=1, keepdims=True)

        def total(values):
            return jnp.sum(values, axis=0, keepdims=True)

        a0, a1, p1, p2, p3, c1, c2, c3, c4, c5, tau = [column(n) for n in range(11)]
        sum0, sum1 = total(a0), total(a1)
        step = sum0 / sum1
        gap = tau - step
        norm = total(p1 + 2.0 * gap * p2 + gap * gap * p3)
        curv_res = total(c1 + 2.0 * gap * c2 + gap * gap * c3)
        curv_mix = total(c4 + gap * c5)
        ratio = norm / sum0
        curv = curv_res + 2.0 * ratio * curv_mix + ratio * ratio * sum1
        next_step = norm / curv
        alpha = step + next_step * (1.0 + ratio)
        beta = -next_step * step
        for k in range(LEVELS):
            out_refs[k][...] = alpha * base_refs[k][...] + beta * image_refs[k][...]
        take = pl.ds(pl.multiple_of(lon * sr, sr), sr)
        later = pl.ds(pl.multiple_of(rows + lon * sr, sr), sr)
        fields = [(own_ref[take, :], own_ref[later, :])]
        fields += [(ref[0:sr, :], ref[sr:, :]) for ref in far_refs]
        for k in range(lon_total):
            here = pl.ds(pl.multiple_of((lon ^ k) * cols, LANES), cols)
            swath_ref[:, here] = alpha * fields[k][0] + beta * fields[k][1]

    outs = [(rows // s, cols // s) for s in SPACINGS] + [(sr, plan.width)]
    return call(kernel, outs, 8)(parts, *base, *image, own_surface, *far_surfaces)


def turn(x, axis, total, k):
    return lax.ppermute(x, axis, [(i, (i + k) % total) for i in range(total)])


def flip(x, axis, total, k):
    return lax.ppermute(x, axis, [(i, i ^ k) for i in range(total)])


def odd_swap(x, axis, total):
    pairs = [(i, i + 1) for i in range(1, total - 1, 2)]
    return lax.ppermute(x, axis, pairs + [(j, i) for i, j in pairs])


def body(observed, gauged):
    lat_total, lon_total = lax.axis_size("lat"), lax.axis_size("lon")
    plan = Plan(observed.shape, gauged.shape, lat_total, lon_total)
    far = opposite(plan, observed)
    far = [turn(x, "lon", lon_total, k) for k, x in enumerate(far, 2)]
    weight = data_weight * gauged.astype(jnp.float32)
    own, right, left = beside(plan, observed, weight)
    right = turn(right, "lon", lon_total, 1)
    left = turn(left, "lon", lon_total, lon_total - 1)
    mis, side, near, following = misfit(plan, own, right, left, far, weight)
    tables = fetch(plan, side)
    near = flip(near, "lat", lat_total, 1)
    following = odd_swap(following, "lat", lat_total)
    base, image, surfaces, parts = operate(plan, mis, weight, side, near, following, tables)
    far_surfaces = [flip(x, "lon", lon_total, k) for k, x in enumerate(surfaces[1:], 1)]
    parts = lax.all_to_all(parts, ("lat", "lon"), split_axis=0, concat_axis=0, tiled=True)
    return tuple(finish(plan, parts, base, image, surfaces[0], far_surfaces))


def solution(mesh):
    return jax.shard_map(
        body,
        mesh=mesh,
        in_specs=(P(("lat", "lon"), None), P("lat", "lon")),
        out_specs=(
            P("lat", "lon"),
            P("lat", "lon"),
            P("lat", "lon"),
            P("lat", "lon"),
            P(("lat", "lon"), None),
        ),
        check_vma=False,
    )
```

```python
import math

import jax
import jax.numpy as jnp
import numpy as np
from jax import lax
from jax.experimental import pallas as pl
from jax.experimental.pallas import tpu as pltpu
from jax.sharding import PartitionSpec as P

LEVELS = 4
SPACINGS = tuple(2 ** (LEVELS - 1 - k) for k in range(LEVELS))
COARSE = LEVELS - 1
HALO = 64
INNER = 32
RAW = 40
PART_ROWS = 8
LANES = 128

data_weight = 2.0
kappa_term = 5.0
level_scales = (0.02, 0.03, 0.05, 0.08)

MIB = 1024 * 1024


def wendland(distance, of=np):
    remain = of.maximum(1.0 - distance, 0.0)
    cube = remain * remain * remain
    return cube * cube * (35.0 * distance * distance + 18.0 * distance + 3.0) / 3.0


def frame_index(total, tile, halo):
    place = np.arange(total)
    index = np.where(place < tile + halo, place, place - total)
    return index, (place < tile + halo) | (place >= total - halo)


def basis(cells, nodes, spacing):
    (cell, cell_ok), (node, node_ok) = cells, nodes
    numerator = np.abs(2 * cell[:, None] - 2 * spacing * node[None, :] - (spacing - 1))
    table = wendland(numerator / (5.0 * spacing)) / math.sqrt(spacing)
    return np.where(cell_ok[:, None] & node_ok[None, :], table, 0.0).astype(np.float32)


def halves(table):
    high = table.astype(jnp.bfloat16)
    low = (table - high.astype(np.float32)).astype(jnp.bfloat16)
    return np.stack([high, low])


def split(x):
    high = x.astype(jnp.bfloat16)
    return high, (x - high.astype(jnp.float32)).astype(jnp.bfloat16)


def dot(a, b, contract):
    return lax.dot_general(a, b, ((contract[0:1], contract[1:2]), ((), ())), preferred_element_type=jnp.float32)


def dot3(a, b, contract=(1, 0)):
    (ah, al), (bh, bl) = a, b
    n = ah.shape[0]
    both = dot(jnp.concatenate([ah, al], axis=0), bh, contract)
    return both[0:n] + (both[n:] + dot(ah, bl, contract))


TAPS = (float(wendland(np.float64(0.4))), float(wendland(np.float64(0.8))))


def shift(x, step, axis):
    return pltpu.roll(x, step % x.shape[axis], axis)


def smooth(x):
    for axis in (0, 1):
        near = shift(x, 1, axis) + shift(x, -1, axis)
        far = shift(x, 2, axis) + shift(x, -2, axis)
        x = x + (TAPS[0] * near + TAPS[1] * far)
    return x


def autoreg(x):
    beside = shift(x, 1, 0) + shift(x, -1, 0) + shift(x, 1, 1) + shift(x, -1, 1)
    return kappa_term * x - beside


def side_mask(total, tile, halo, at, last, dim):
    shape = (total, 1) if dim == 0 else (1, total)
    place = lax.broadcasted_iota(jnp.int32, shape, dim)
    after = (place < tile + halo) & (at < last)
    before = (place >= total - halo) & (at > 0)
    return ((place < tile) | after | before).astype(jnp.float32)


def fold(x):
    rows, cols = x.shape
    total = x[0:8]
    for r in range(8, rows, 8):
        total = total + x[r : r + 8]
    if cols < LANES:
        return jnp.concatenate([total, jnp.zeros((8, LANES - cols), jnp.float32)], axis=1)
    out = total[:, 0:LANES]
    for c in range(LANES, cols, LANES):
        out = out + total[:, c : c + LANES]
    return out


class Plan:
    def __init__(self, swath_shape, tile_shape, lat_total, lon_total):
        self.swath_rows, self.width = swath_shape
        self.rows, self.cols = tile_shape
        self.lat_total, self.lon_total = lat_total, lon_total
        self.col_frame = self.cols + 2 * HALO
        self.outer_rows = self.rows + 2 * RAW
        self.inner_rows = self.rows + 2 * INNER
        self.node_rows = [(self.rows + 2 * HALO) // s for s in SPACINGS[:COARSE]] + [self.outer_rows]
        self.node_cols = [-(-self.col_frame // (s * LANES)) * LANES for s in SPACINGS]
        self.row_starts = np.cumsum([0] + self.node_rows[:COARSE]).tolist()
        self.col_starts = np.cumsum([0] + self.node_cols[:COARSE]).tolist()
        col_cells = frame_index(self.col_frame, self.cols, HALO)
        outer = frame_index(self.outer_rows, self.rows, RAW)
        inner = frame_index(self.inner_rows, self.rows, INNER)
        col_tables, outer_rows, inner_rows = [], [], []
        self.part_nodes, place_all = [], []
        for k in range(COARSE):
            s = SPACINGS[k]
            tile = self.rows // s
            col_nodes = frame_index(self.node_cols[k], self.cols // s, HALO // s)
            row_nodes = frame_index(self.node_rows[k], tile, HALO // s)
            col_tables.append(basis(col_cells, col_nodes, s))
            outer_rows.append(basis(outer, row_nodes, s))
            inner_rows.append(basis(inner, row_nodes, s))
            for away in range((RAW - 2 * s) // s, INNER // s + 2):
                self.part_nodes.append((s, away))
                at = self.row_starts[k]
                place_all.append((at + tile + away, at + self.node_rows[k] - 1 - away))
        nodes = self.row_starts[-1]
        joins = np.zeros((2 * PART_ROWS, nodes), np.float32)
        for n, (after_at, before_at) in enumerate(place_all):
            joins[n, after_at] = 1.0
            joins[PART_ROWS + n, before_at] = 1.0
        outer_all = np.concatenate([np.concatenate(outer_rows, axis=1), joins], axis=0)
        inner_all = np.concatenate(inner_rows, axis=1)
        row_tables = [outer_all.T, inner_all.T, inner_all]
        self.row_places, at = [], 0
        for table in row_tables:
            self.row_places.append((at, table.shape[0], table.shape[1]))
            at += table.shape[0]
        lanes = -(-max(t.shape[1] for t in row_tables) // LANES) * LANES
        col_all = np.concatenate(col_tables, axis=1)
        self.turned_start = self.col_starts[-1] + lanes
        whole = np.zeros((max(at, *col_all.shape), self.turned_start + self.col_frame), np.float32)
        whole[: self.col_frame, : self.col_starts[-1]] = col_all
        whole[: self.col_starts[-1], self.turned_start :] = col_all.T
        for (start, height, width), table in zip(self.row_places, row_tables):
            whole[start : start + height, self.col_starts[-1] : self.col_starts[-1] + width] = table
        self.tables = halves(whole)


def call(kernel, outs, limit, scratch=(), spaces=None):
    def run(*operands):
        in_spaces = spaces or [pltpu.VMEM] * len(operands)
        return pl.pallas_call(
            kernel,
            out_shape=[jax.ShapeDtypeStruct(shape, jnp.float32) for shape in outs],
            in_specs=[pl.BlockSpec(memory_space=space) for space in in_spaces],
            out_specs=[pl.BlockSpec(memory_space=pltpu.VMEM)] * len(outs),
            scratch_shapes=list(scratch),
            compiler_params=pltpu.CompilerParams(vmem_limit_bytes=int(limit * MIB)),
        )(*operands)

    return run


def window(plan, obs_ref, to):
    sr, width, cols = plan.swath_rows, plan.width, plan.cols
    base = pl.multiple_of(to * cols, LANES)
    lane = lax.broadcasted_iota(jnp.int32, (sr, LANES), 1)
    before = obs_ref[:, pl.ds(pl.multiple_of(jnp.maximum(base - LANES, 0), LANES), LANES)]
    after = obs_ref[:, pl.ds(pl.multiple_of(jnp.minimum(base + cols, width - LANES), LANES), LANES)]
    before = jnp.where(to > 0, before, 0.0)
    after = jnp.where(to < plan.lon_total - 1, after, 0.0)
    return obs_ref[:, pl.ds(base, cols)], jnp.where(lane < HALO, after, before)


def pack(plan, observed, gauged):
    sr, width, cols, rows, n = plan.swath_rows, plan.width, plan.cols, plan.rows, plan.lon_total
    tiles = plan.col_frame // LANES

    def kernel(obs_hbm, gauge_hbm, *rest):
        wt_ref, out_refs, (obs_ref, gauge_ref, sems) = rest[0], rest[1 : n + 1], rest[n + 1 :]
        copies = [
            pltpu.make_async_copy(obs_hbm, obs_ref, sems.at[0]),
            pltpu.make_async_copy(gauge_hbm, gauge_ref, sems.at[1]),
        ]
        for copy in copies:
            copy.start()
        at = lax.axis_index("lon")
        half_lane = lax.broadcasted_iota(jnp.int32, (rows // 2, LANES), 1)
        copies[0].wait()
        for k, ref in enumerate(out_refs):
            main, sides = window(plan, obs_ref, lax.rem(at + k, n))
            if k in (1, n - 1):
                for t in range(tiles - 1):
                    ref[t * sr : (t + 1) * sr, :] = main[:, t * LANES : (t + 1) * LANES]
                ref[(tiles - 1) * sr : tiles * sr, :] = sides
            else:
                ref[:, 0:cols] = main
                ref[:, cols:] = sides
        copies[1].wait()
        wt_ref[...] = data_weight * gauge_ref[...].astype(jnp.float32)
        for k in (1, n - 1):
            edge = wt_ref[:, cols - LANES :] if k == 1 else wt_ref[:, 0:LANES]
            kept = (half_lane >= HALO) if k == 1 else (half_lane < HALO)
            turned = pltpu.roll(edge[rows // 2 :], HALO, 1)
            out_refs[k][tiles * sr :, :] = jnp.where(kept, edge[0 : rows // 2], turned)

    side = (tiles * sr + rows // 2, LANES)
    outs = [(rows, cols)] + [side if k in (1, n - 1) else (sr, plan.col_frame) for k in range(n)]
    scratch = [
        pltpu.VMEM((sr, width), jnp.float32),
        pltpu.VMEM((rows, cols), jnp.int32),
        pltpu.SemaphoreType.DMA((2,)),
    ]
    return call(kernel, outs, 53.25, scratch, [pltpu.HBM] * 2)(observed, gauged)


def misfit(plan, own, right, left, far, weight):
    sr, cols, rows, n = plan.swath_rows, plan.cols, plan.rows, plan.lon_total
    tiles = plan.col_frame // LANES

    def kernel(own_ref, right_ref, left_ref, wt_ref, *rest):
        far_refs, (mis_ref, side_ref, near_ref, next_ref) = rest[: n - 3], rest[n - 3 :]
        at = lax.axis_index("lon")
        lane = lax.broadcasted_iota(jnp.int32, (rows, LANES), 1)

        def side(ref, present):
            packed = ref[tiles * sr :, :]
            both = jnp.concatenate([packed, pltpu.roll(packed, HALO, 1)], axis=0)
            return jnp.where(present, both, 0.0)

        side_ref[...] = jnp.where(lane < HALO, side(left_ref, at < n - 1), side(right_ref, at > 0))

        for k, ref in enumerate((own_ref, right_ref, *far_refs, left_ref)):
            here = pl.ds(pl.multiple_of(lax.rem(at + (n - k), n) * sr, sr), sr)
            if k in (1, n - 1):
                for t in range(tiles - 1):
                    lanes = slice(t * LANES, (t + 1) * LANES)
                    mis_ref[here, lanes] = wt_ref[here, lanes] * ref[t * sr : (t + 1) * sr, :]
                mis_ref[here, cols:] = side_ref[here, :] * ref[(tiles - 1) * sr : tiles * sr, :]
            else:
                mis_ref[here, 0:cols] = wt_ref[here, :] * ref[:, 0:cols]
                mis_ref[here, cols:] = side_ref[here, :] * ref[:, cols:]

        up = lax.axis_index("lat") % 2
        depth = HALO - RAW
        shape = (PART_ROWS, depth)
        line = lax.broadcasted_iota(jnp.int32, shape, 0)
        cell = lax.broadcasted_iota(jnp.int32, shape, 1)
        for ref, low in ((near_ref, 1 - up), (next_ref, up)):
            far = mis_ref[pl.ds(pl.multiple_of(RAW + low * (rows - HALO - RAW), 8), depth), :]
            table = jnp.zeros(shape, jnp.float32)
            distance = jnp.where(low == 1, HALO - 1 - cell, RAW + cell)
            for m, (s, away) in enumerate(plan.part_nodes):
                numerator = jnp.abs(2 * distance - 2 * s * away - (s - 1)).astype(jnp.float32)
                table = jnp.where(line == m, wendland(numerator / (5.0 * s), jnp) / math.sqrt(s), table)
            ref[0:RAW, :] = mis_ref[pl.ds(pl.multiple_of(low * (rows - RAW), 8), RAW), :]
            ref[RAW : RAW + PART_ROWS, :] = jnp.dot(
                table, far, precision=lax.Precision.HIGHEST, preferred_element_type=jnp.float32
            )
            edge = pl.ds(pl.multiple_of(low * (rows - INNER), 8), INNER)
            ref[RAW + PART_ROWS :, 0:cols] = wt_ref[edge, :]
            ref[RAW + PART_ROWS :, cols:] = side_ref[edge, :]

    outs = [(rows, plan.col_frame), (rows, LANES)] + [(RAW + PART_ROWS + INNER, plan.col_frame)] * 2
    return call(kernel, outs, 4)(own, right, left, weight, *far)


def fetch(plan, after):
    def kernel(table_ref, after_ref, out_ref, sem):
        copy = pltpu.make_async_copy(table_ref, out_ref, sem)
        copy.start()
        copy.wait()

    table = jnp.asarray(plan.tables)
    return pl.pallas_call(
        kernel,
        out_shape=jax.ShapeDtypeStruct(table.shape, table.dtype),
        in_specs=[pl.BlockSpec(memory_space=pltpu.HBM), pl.BlockSpec(memory_space=pltpu.VMEM)],
        out_specs=pl.BlockSpec(memory_space=pltpu.VMEM),
        scratch_shapes=[pltpu.SemaphoreType.DMA],
        compiler_params=pltpu.CompilerParams(vmem_limit_bytes=MIB),
        cost_estimate=pl.CostEstimate(flops=0, bytes_accessed=2 * table.nbytes, transcendentals=0),
    )(table, after)


def operate(plan, mis, wt, side, near, following, tables):
    rows, cols, sr, lon_total = plan.rows, plan.cols, plan.swath_rows, plan.lon_total
    starts = plan.row_starts
    inner_rows = plan.inner_rows
    n_dev = plan.lat_total * lon_total

    def kernel(mis_ref, wt_ref, side_ref, near_ref, next_ref, table_ref, *out_refs):
        base_refs, image_refs = out_refs[:LEVELS], out_refs[LEVELS : 2 * LEVELS]
        surface_refs, part_ref = out_refs[2 * LEVELS : -1], out_refs[-1]
        lat = lax.axis_index("lat")
        lon = lax.axis_index("lon")
        even = lat % 2 == 0
        col_tables, turned_tables, row_tables = [], [], []
        for k in range(COARSE):
            places = slice(plan.col_starts[k], plan.col_starts[k + 1])
            turned_tables.append(tuple(table_ref[half, places, plan.turned_start :] for half in (0, 1)))
            lanes = slice(plan.col_starts[k], plan.col_starts[k + 1])
            col_tables.append(tuple(table_ref[half, 0 : plan.col_frame, lanes] for half in (0, 1)))
        for start, height, width in plan.row_places:
            lanes = slice(plan.col_starts[-1], plan.col_starts[-1] + width)
            row_tables.append(tuple(table_ref[half, start : start + height, lanes] for half in (0, 1)))
        outer_t, inner_t, inner_s = row_tables

        near_all, next_all = near_ref[...], next_ref[...]
        below = jnp.where(even, near_all, next_all)
        above = jnp.where(even, next_all, near_all)
        cells = jnp.concatenate([mis_ref[...], below[0:RAW], above[0:RAW]], axis=0)
        sums = slice(RAW, RAW + PART_ROWS)
        outer = jnp.concatenate([cells, below[sums], above[sums]], axis=0)
        own_weight = jnp.concatenate([wt_ref[...], side_ref[...]], axis=1)
        weight = jnp.concatenate([own_weight, below[RAW + PART_ROWS :], above[RAW + PART_ROWS :]], axis=0)

        masks = []
        for k in range(LEVELS):
            s = SPACINGS[k]
            masks.append(
                side_mask(plan.node_rows[k], rows // s, (HALO if k < COARSE else RAW) // s, lat, plan.lat_total - 1, 0)
                * side_mask(plan.node_cols[k], cols // s, HALO // s, lon, lon_total - 1, 1)
            )
        inner_mask = side_mask(inner_rows, rows, INNER, lat, plan.lat_total - 1, 0) * side_mask(
            plan.col_frame, cols, HALO, lon, lon_total - 1, 1
        )

        def collect(values, row_table):
            gathered = dot3(row_table, split(values))
            return [
                dot3(split(gathered[starts[k] : starts[k + 1]]), col_tables[k]) for k in range(COARSE)
            ]

        def spread(coeffs):
            return split(
                jnp.concatenate([dot3(split(coeffs[k]), turned_tables[k]) for k in range(COARSE)], axis=0)
            )

        def cut(x):
            return jnp.concatenate([x[0 : rows + INNER], x[x.shape[0] - INNER :]], axis=0)

        base = collect(outer, outer_t)
        base = [base[k] * masks[k] for k in range(COARSE)]
        finest = smooth(cells) * masks[COARSE]
        surface = dot3(inner_s, spread(base)) + cut(smooth(finest))
        base.append(cut(finest))
        masks[COARSE] = inner_mask

        image = collect(weight * surface, inner_t)
        image.append(smooth(weight * surface))
        rough_base, rough_image = [], []
        for k in range(LEVELS):
            once = autoreg(base[k]) * masks[k]
            rough_base.append(once)
            image[k] = (image[k] + level_scales[k] * autoreg(once)) * masks[k]
            rough_image.append(autoreg(image[k]))
        tile_table = tuple(part[0:rows] for part in inner_s)
        second = dot3(tile_table, spread(image)) + smooth(image[COARSE])[0:rows]

        own = [(slice(0, rows // s), slice(0, cols // s)) for s in SPACINGS]
        b = [base[k][own[k]] for k in range(LEVELS)]
        ab = [image[k][own[k]] for k in range(LEVELS)]
        rb = [rough_base[k][own[k]] for k in range(LEVELS)]
        rab = [rough_image[k][own[k]] for k in range(LEVELS)]
        sb, sab = surface[0:rows, 0:cols], second[:, 0:cols]
        w = weight[0:rows, 0:cols]

        for k in range(LEVELS):
            base_refs[k][...] = b[k]
            image_refs[k][...] = ab[k]
        surface_refs[0][0:rows, :] = sb
        surface_refs[0][rows:, :] = sab
        for k in range(1, lon_total):
            take = pl.ds(pl.multiple_of((lon ^ k) * sr, sr), sr)
            surface_refs[k][0:sr, :] = surface_refs[0][take, :]
            take = pl.ds(pl.multiple_of(rows + (lon ^ k) * sr, sr), sr)
            surface_refs[k][sr:, :] = surface_refs[0][take, :]

        def inner(first, other):
            total = fold(first[0] * other[0])
            for k in range(1, LEVELS):
                total = total + fold(first[k] * other[k])
            return total

        def curvature(first, other, field, other_field):
            total = fold(w * field * other_field)
            for k in range(LEVELS):
                total = total + level_scales[k] * fold(first[k] * other[k])
            return total

        a0 = inner(b, b)
        a1 = curvature(rb, rb, sb, sb)
        top = jnp.sum(a0, keepdims=True)
        bottom = jnp.sum(a1, keepdims=True)
        tau = jnp.where(bottom > 0.0, top / jnp.where(bottom > 0.0, bottom, 1.0), 0.0)
        r = [b[k] - tau * ab[k] for k in range(LEVELS)]
        rr = [rb[k] - tau * rab[k] for k in range(LEVELS)]
        sr_field = sb - tau * sab
        blocks = [
            a0,
            a1,
            inner(r, r),
            inner(r, ab),
            inner(ab, ab),
            curvature(rr, rr, sr_field, sr_field),
            curvature(rr, rab, sr_field, sab),
            curvature(rab, rab, sab, sab),
            curvature(rr, rb, sr_field, sb),
            curvature(rab, rb, sab, sb),
        ]
        lines = [jnp.sum(block, axis=0, keepdims=True) for block in blocks]
        lane = lax.broadcasted_iota(jnp.int32, (1, LANES), 1)
        lines.append(jnp.where(lane == 0, tau, 0.0))
        lines.append(jnp.zeros((16 - len(lines), LANES), jnp.float32))
        sums = jnp.sum(jnp.concatenate(lines, axis=0), axis=1, keepdims=True)
        place = lax.broadcasted_iota(jnp.int32, (16, LANES), 0)
        lanes = lax.broadcasted_iota(jnp.int32, (16, LANES), 1)
        line = jnp.sum(jnp.where(place == lanes, sums, 0.0), axis=0, keepdims=True)
        part_ref[...] = jnp.broadcast_to(line, (n_dev, LANES))

    level_shapes = [(rows // s, cols // s) for s in SPACINGS]
    outs = level_shapes * 2 + [(2 * rows, cols)] + [(2 * sr, cols)] * (lon_total - 1) + [(n_dev, LANES)]
    results = call(kernel, outs, 24)(mis, wt, side, near, following, tables)
    return results[:LEVELS], results[LEVELS : 2 * LEVELS], results[2 * LEVELS : -1], results[-1]


def finish(plan, parts, base, image, own_surface, far_surfaces):
    rows, cols, sr, lon_total = plan.rows, plan.cols, plan.swath_rows, plan.lon_total

    def kernel(part_ref, *rest):
        base_refs, image_refs = rest[:LEVELS], rest[LEVELS : 2 * LEVELS]
        own_ref, far_refs = rest[2 * LEVELS], rest[2 * LEVELS + 1 : 2 * LEVELS + lon_total]
        out_refs, swath_ref = rest[-LEVELS - 1 : -1], rest[-1]
        lon = lax.axis_index("lon")
        part = part_ref[...]
        lane = lax.broadcasted_iota(jnp.int32, part.shape, 1)

        def column(n):
            return jnp.sum(jnp.where(lane == n, part, 0.0), axis=1, keepdims=True)

        def total(values):
            return jnp.sum(values, axis=0, keepdims=True)

        a0, a1, p1, p2, p3, c1, c2, c3, c4, c5, tau = [column(n) for n in range(11)]
        sum0, sum1 = total(a0), total(a1)
        step = sum0 / sum1
        gap = tau - step
        norm = total(p1 + 2.0 * gap * p2 + gap * gap * p3)
        curv_res = total(c1 + 2.0 * gap * c2 + gap * gap * c3)
        curv_mix = total(c4 + gap * c5)
        ratio = norm / sum0
        curv = curv_res + 2.0 * ratio * curv_mix + ratio * ratio * sum1
        next_step = norm / curv
        alpha = step + next_step * (1.0 + ratio)
        beta = -next_step * step
        for k in range(LEVELS):
            out_refs[k][...] = alpha * base_refs[k][...] + beta * image_refs[k][...]
        take = pl.ds(pl.multiple_of(lon * sr, sr), sr)
        later = pl.ds(pl.multiple_of(rows + lon * sr, sr), sr)
        fields = [(own_ref[take, :], own_ref[later, :])]
        fields += [(ref[0:sr, :], ref[sr:, :]) for ref in far_refs]
        for k in range(lon_total):
            here = pl.ds(pl.multiple_of((lon ^ k) * cols, LANES), cols)
            swath_ref[:, here] = alpha * fields[k][0] + beta * fields[k][1]

    outs = [(rows // s, cols // s) for s in SPACINGS] + [(sr, plan.width)]
    return call(kernel, outs, 8)(parts, *base, *image, own_surface, *far_surfaces)


def turn(x, axis, total, k):
    return lax.ppermute(x, axis, [(i, (i + k) % total) for i in range(total)])


def flip(x, axis, total, k):
    return lax.ppermute(x, axis, [(i, i ^ k) for i in range(total)])


def odd_swap(x, axis, total):
    pairs = [(i, i + 1) for i in range(1, total - 1, 2)]
    return lax.ppermute(x, axis, pairs + [(j, i) for i, j in pairs])


def body(observed, gauged):
    lat_total, lon_total = lax.axis_size("lat"), lax.axis_size("lon")
    plan = Plan(observed.shape, gauged.shape, lat_total, lon_total)
    weight, own, *windows = pack(plan, observed, gauged)
    right, *far, left = [turn(x, "lon", lon_total, k) for k, x in enumerate(windows, 1)]
    mis, side, near, following = misfit(plan, own, right, left, far, weight)
    tables = fetch(plan, side)
    near = flip(near, "lat", lat_total, 1)
    following = odd_swap(following, "lat", lat_total)
    base, image, surfaces, parts = operate(plan, mis, weight, side, near, following, tables)
    far_surfaces = [flip(x, "lon", lon_total, k) for k, x in enumerate(surfaces[1:], 1)]
    parts = lax.all_to_all(parts, ("lat", "lon"), split_axis=0, concat_axis=0, tiled=True)
    return tuple(finish(plan, parts, base, image, surfaces[0], far_surfaces))


def solution(mesh):
    return jax.shard_map(
        body,
        mesh=mesh,
        in_specs=(P(("lat", "lon"), None), P("lat", "lon")),
        out_specs=(
            P("lat", "lon"),
            P("lat", "lon"),
            P("lat", "lon"),
            P("lat", "lon"),
            P(("lat", "lon"), None),
        ),
        check_vma=False,
    )
```

```python
import math

import jax
import jax.numpy as jnp
import numpy as np
from jax import lax
from jax.experimental import pallas as pl
from jax.experimental.pallas import tpu as pltpu
from jax.sharding import PartitionSpec as P

LEVELS = 4
SPACINGS = tuple(2 ** (LEVELS - 1 - k) for k in range(LEVELS))
COARSE = LEVELS - 1
HALO = 64
INNER = 32
RAW = 40
PART_ROWS = 8
NEAR = 8
LANES = 128

data_weight = 2.0
kappa_term = 5.0
level_scales = (0.02, 0.03, 0.05, 0.08)

MIB = 1024 * 1024


def wendland(distance, of=np):
    remain = of.maximum(1.0 - distance, 0.0)
    cube = remain * remain * remain
    return cube * cube * (35.0 * distance * distance + 18.0 * distance + 3.0) / 3.0


def frame_index(total, tile, halo):
    place = np.arange(total)
    index = np.where(place < tile + halo, place, place - total)
    return index, (place < tile + halo) | (place >= total - halo)


def basis(cells, nodes, spacing):
    (cell, cell_ok), (node, node_ok) = cells, nodes
    numerator = np.abs(2 * cell[:, None] - 2 * spacing * node[None, :] - (spacing - 1))
    table = wendland(numerator / (5.0 * spacing)) / math.sqrt(spacing)
    return np.where(cell_ok[:, None] & node_ok[None, :], table, 0.0).astype(np.float32)


def halves(table):
    high = table.astype(jnp.bfloat16)
    low = (table - high.astype(np.float32)).astype(jnp.bfloat16)
    return np.stack([high, low])


def split(x):
    high = x.astype(jnp.bfloat16)
    return high, (x - high.astype(jnp.float32)).astype(jnp.bfloat16)


def dot(a, b, contract):
    return lax.dot_general(a, b, ((contract[0:1], contract[1:2]), ((), ())), preferred_element_type=jnp.float32)


def dot3(a, b, contract=(1, 0)):
    (ah, al), (bh, bl) = a, b
    n = ah.shape[0]
    both = dot(jnp.concatenate([ah, al], axis=0), bh, contract)
    return both[0:n] + (both[n:] + dot(ah, bl, contract))


TAPS = (float(wendland(np.float64(0.4))), float(wendland(np.float64(0.8))))


def shift(x, step, axis):
    return pltpu.roll(x, step % x.shape[axis], axis)


def smooth(x):
    for axis in (0, 1):
        near = shift(x, 1, axis) + shift(x, -1, axis)
        far = shift(x, 2, axis) + shift(x, -2, axis)
        x = x + (TAPS[0] * near + TAPS[1] * far)
    return x


def autoreg(x):
    beside = shift(x, 1, 0) + shift(x, -1, 0) + shift(x, 1, 1) + shift(x, -1, 1)
    return kappa_term * x - beside


def side_mask(total, tile, halo, at, last, dim):
    shape = (total, 1) if dim == 0 else (1, total)
    place = lax.broadcasted_iota(jnp.int32, shape, dim)
    after = (place < tile + halo) & (at < last)
    before = (place >= total - halo) & (at > 0)
    return ((place < tile) | after | before).astype(jnp.float32)


class Plan:
    def __init__(self, swath_shape, tile_shape, lat_total, lon_total):
        self.swath_rows, self.width = swath_shape
        self.rows, self.cols = tile_shape
        self.lat_total, self.lon_total = lat_total, lon_total
        self.col_frame = self.cols + 2 * HALO
        self.outer_rows = self.rows + 2 * RAW
        self.inner_rows = self.rows + 2 * INNER
        wide = [-(-(self.rows // s + 2 * (INNER // s + 2)) // 16) * 16 for s in SPACINGS[:COARSE]]
        self.node_rows = wide + [self.outer_rows]
        self.near_rows = [min(w, self.rows // s + 2 * NEAR) for w, s in zip(wide, SPACINGS)] + [self.inner_rows]
        self.near_starts = np.cumsum([0] + self.near_rows[:COARSE]).tolist()
        self.node_cols = [-(-self.col_frame // (s * LANES)) * LANES for s in SPACINGS]
        self.row_starts = np.cumsum([0] + self.node_rows[:COARSE]).tolist()
        self.col_starts = np.cumsum([0] + self.node_cols[:COARSE]).tolist()
        col_cells = frame_index(self.col_frame, self.cols, HALO)
        outer = frame_index(self.outer_rows, self.rows, RAW)
        inner = frame_index(self.inner_rows, self.rows, INNER)
        col_tables, outer_rows, inner_rows, wide_rows = [], [], [], []
        self.part_nodes, place_all = [], []
        for k in range(COARSE):
            s = SPACINGS[k]
            tile = self.rows // s
            col_nodes = frame_index(self.node_cols[k], self.cols // s, HALO // s)
            row_nodes = frame_index(self.node_rows[k], tile, (self.node_rows[k] - tile) // 2)
            near_nodes = frame_index(self.near_rows[k], tile, (self.near_rows[k] - tile) // 2)
            col_tables.append(basis(col_cells, col_nodes, s))
            outer_rows.append(basis(outer, row_nodes, s))
            wide_rows.append(basis(inner, row_nodes, s))
            inner_rows.append(basis(inner, near_nodes, s))
            for away in range((RAW - 2 * s) // s, INNER // s + 2):
                self.part_nodes.append((s, away))
                at = self.row_starts[k]
                place_all.append((at + tile + away, at + self.node_rows[k] - 1 - away))
        nodes = self.row_starts[-1]
        joins = np.zeros((2 * PART_ROWS, nodes), np.float32)
        for n, (after_at, before_at) in enumerate(place_all):
            joins[n, after_at] = 1.0
            joins[PART_ROWS + n, before_at] = 1.0
        outer_all = np.concatenate([np.concatenate(outer_rows, axis=1), joins], axis=0)
        inner_all = np.concatenate(inner_rows, axis=1)
        wide_all = np.concatenate(wide_rows, axis=1)
        row_tables = [outer_all.T, inner_all.T, wide_all, inner_all[: self.rows]]
        self.row_places, at = [], 0
        for table in row_tables:
            self.row_places.append((at, table.shape[0], table.shape[1]))
            at += table.shape[0]
        lanes = -(-max(t.shape[1] for t in row_tables) // LANES) * LANES
        col_all = np.concatenate(col_tables, axis=1)
        self.turned_start = self.col_starts[-1] + lanes
        whole = np.zeros((max(at, *col_all.shape), self.turned_start + self.col_frame), np.float32)
        whole[: self.col_frame, : self.col_starts[-1]] = col_all
        whole[: self.col_starts[-1], self.turned_start :] = col_all.T
        for (start, height, width), table in zip(self.row_places, row_tables):
            whole[start : start + height, self.col_starts[-1] : self.col_starts[-1] + width] = table
        self.tables = halves(whole)
        tiles = self.col_frame // LANES
        self.sums = len(self.part_nodes)
        self.letter_rows = -(-(self.letter()[-1] + tiles * self.sums) // 8) * 8

    def letter(self):
        tiles = self.col_frame // LANES
        weights = tiles * RAW
        corner = weights + (tiles - 1) * INNER
        return 0, weights, corner, corner + INNER // 2


def call(kernel, outs, limit, scratch=(), spaces=None):
    def run(*operands):
        in_spaces = spaces or [pltpu.VMEM] * len(operands)
        return pl.pallas_call(
            kernel,
            out_shape=[jax.ShapeDtypeStruct(shape, jnp.float32) for shape in outs],
            in_specs=[pl.BlockSpec(memory_space=space) for space in in_spaces],
            out_specs=[pl.BlockSpec(memory_space=pltpu.VMEM)] * len(outs),
            scratch_shapes=list(scratch),
            compiler_params=pltpu.CompilerParams(vmem_limit_bytes=int(limit * MIB)),
        )(*operands)

    return run


def window(plan, obs_ref, to):
    sr, width, cols = plan.swath_rows, plan.width, plan.cols
    base = pl.multiple_of(to * cols, LANES)
    lane = lax.broadcasted_iota(jnp.int32, (sr, LANES), 1)
    before = obs_ref[:, pl.ds(pl.multiple_of(jnp.maximum(base - LANES, 0), LANES), LANES)]
    after = obs_ref[:, pl.ds(pl.multiple_of(jnp.minimum(base + cols, width - LANES), LANES), LANES)]
    before = jnp.where(to > 0, before, 0.0)
    after = jnp.where(to < plan.lon_total - 1, after, 0.0)
    return obs_ref[:, pl.ds(base, cols)], jnp.where(lane < HALO, after, before)


def pack(plan, observed, gauged):
    sr, width, cols, rows, n = plan.swath_rows, plan.width, plan.cols, plan.rows, plan.lon_total
    tiles = plan.col_frame // LANES

    def kernel(obs_hbm, gauge_hbm, *rest):
        wt_ref, out_refs, (obs_ref, gauge_ref, sems) = rest[0], rest[1 : n + 1], rest[n + 1 :]
        copies = [
            pltpu.make_async_copy(obs_hbm, obs_ref, sems.at[0]),
            pltpu.make_async_copy(gauge_hbm, gauge_ref, sems.at[1]),
        ]
        for copy in copies:
            copy.start()
        at = lax.axis_index("lon")
        half_lane = lax.broadcasted_iota(jnp.int32, (rows // 2, LANES), 1)
        copies[0].wait()
        for k, ref in enumerate(out_refs):
            main, sides = window(plan, obs_ref, lax.rem(at + k, n))
            if k in (1, n - 1):
                for t in range(tiles - 1):
                    ref[t * sr : (t + 1) * sr, :] = main[:, t * LANES : (t + 1) * LANES]
                ref[(tiles - 1) * sr : tiles * sr, :] = sides
            else:
                ref[:, 0:cols] = main
                ref[:, cols:] = sides
        copies[1].wait()
        wt_ref[...] = data_weight * gauge_ref[...].astype(jnp.float32)
        for k in (1, n - 1):
            edge = wt_ref[:, cols - LANES :] if k == 1 else wt_ref[:, 0:LANES]
            kept = (half_lane >= HALO) if k == 1 else (half_lane < HALO)
            turned = pltpu.roll(edge[rows // 2 :], HALO, 1)
            out_refs[k][tiles * sr :, :] = jnp.where(kept, edge[0 : rows // 2], turned)

    side = (tiles * sr + rows // 2, LANES)
    outs = [(rows, cols)] + [side if k in (1, n - 1) else (sr, plan.col_frame) for k in range(n)]
    scratch = [
        pltpu.VMEM((sr, width), jnp.float32),
        pltpu.VMEM((rows, cols), jnp.int32),
        pltpu.SemaphoreType.DMA((2,)),
    ]
    return call(kernel, outs, 53.25, scratch, [pltpu.HBM] * 2)(observed, gauged)


def misfit(plan, own, right, left, far, weight):
    sr, cols, rows, n = plan.swath_rows, plan.cols, plan.rows, plan.lon_total
    tiles = plan.col_frame // LANES

    def kernel(own_ref, right_ref, left_ref, wt_ref, *rest):
        far_refs, (mis_ref, side_ref, near_ref, next_ref) = rest[: n - 3], rest[n - 3 :]
        at = lax.axis_index("lon")
        lane = lax.broadcasted_iota(jnp.int32, (rows, LANES), 1)

        def side(ref, present):
            packed = ref[tiles * sr :, :]
            both = jnp.concatenate([packed, pltpu.roll(packed, HALO, 1)], axis=0)
            return jnp.where(present, both, 0.0)

        side_ref[...] = jnp.where(lane < HALO, side(left_ref, at < n - 1), side(right_ref, at > 0))

        for k, ref in enumerate((own_ref, right_ref, *far_refs, left_ref)):
            here = pl.ds(pl.multiple_of(lax.rem(at + (n - k), n) * sr, sr), sr)
            if k in (1, n - 1):
                for t in range(tiles - 1):
                    lanes = slice(t * LANES, (t + 1) * LANES)
                    mis_ref[here, lanes] = wt_ref[here, lanes] * ref[t * sr : (t + 1) * sr, :]
                mis_ref[here, cols:] = side_ref[here, :] * ref[(tiles - 1) * sr : tiles * sr, :]
            else:
                mis_ref[here, 0:cols] = wt_ref[here, :] * ref[:, 0:cols]
                mis_ref[here, cols:] = side_ref[here, :] * ref[:, cols:]

        up = lax.axis_index("lat") % 2
        depth = HALO - RAW
        shape = (PART_ROWS, depth)
        line = lax.broadcasted_iota(jnp.int32, shape, 0)
        cell = lax.broadcasted_iota(jnp.int32, shape, 1)
        for ref, low in ((near_ref, 1 - up), (next_ref, up)):
            far = mis_ref[pl.ds(pl.multiple_of(RAW + low * (rows - HALO - RAW), 8), depth), :]
            table = jnp.zeros(shape, jnp.float32)
            distance = jnp.where(low == 1, HALO - 1 - cell, RAW + cell)
            for m, (s, away) in enumerate(plan.part_nodes):
                numerator = jnp.abs(2 * distance - 2 * s * away - (s - 1)).astype(jnp.float32)
                table = jnp.where(line == m, wendland(numerator / (5.0 * s), jnp) / math.sqrt(s), table)
            edge = pl.ds(pl.multiple_of(low * (rows - INNER), 8), INNER)
            sums = jnp.dot(table, far, precision=lax.Precision.HIGHEST, preferred_element_type=jnp.float32)
            near = mis_ref[pl.ds(pl.multiple_of(low * (rows - RAW), 8), RAW), :]
            raw, weights, corner, parts = plan.letter()
            for t in range(tiles):
                lanes = slice(t * LANES, (t + 1) * LANES)
                ref[raw + t * RAW : raw + (t + 1) * RAW, :] = near[:, lanes]
                if t < tiles - 1:
                    ref[weights + t * INNER : weights + (t + 1) * INNER, :] = wt_ref[edge, lanes]
                ref[parts + t * plan.sums : parts + (t + 1) * plan.sums, :] = sums[0 : plan.sums, lanes]
            beside = side_ref[edge, :]
            turned = pltpu.roll(beside[INNER // 2 :], HALO, 1)
            some = lax.broadcasted_iota(jnp.int32, (INNER // 2, LANES), 1)
            outer = (some < INNER) | (some >= LANES - INNER)
            ref[corner : corner + INNER // 2, :] = jnp.where(outer, beside[0 : INNER // 2], turned)
            ref[parts + tiles * plan.sums :, :] = jnp.zeros((plan.letter_rows - parts - tiles * plan.sums, LANES), jnp.float32)

    outs = [(rows, plan.col_frame), (rows, LANES)] + [(plan.letter_rows, LANES)] * 2
    return call(kernel, outs, 4)(own, right, left, weight, *far)


def open_letter(plan, letter):
    tiles = plan.col_frame // LANES
    raw, weights, corner, parts = plan.letter()
    near = [letter[raw + t * RAW : raw + (t + 1) * RAW] for t in range(tiles)]
    sums = [letter[parts + t * plan.sums : parts + (t + 1) * plan.sums] for t in range(tiles)]
    sums = jnp.concatenate(sums, axis=1)
    sums = jnp.concatenate([sums, jnp.zeros((PART_ROWS - plan.sums, plan.col_frame), jnp.float32)], axis=0)
    rows = [letter[weights + t * INNER : weights + (t + 1) * INNER] for t in range(tiles - 1)]
    both = letter[corner : corner + INNER // 2]
    some = lax.broadcasted_iota(jnp.int32, (INNER // 2, LANES), 1)
    outer = (some < INNER) | (some >= LANES - INNER)
    beside = [jnp.where(outer, x, 0.0) for x in (both, pltpu.roll(both, HALO, 1))]
    rows.append(jnp.concatenate(beside, axis=0))
    return jnp.concatenate(near, axis=1), sums, jnp.concatenate(rows, axis=1)


def fetch(plan, after):
    def kernel(table_ref, after_ref, out_ref, sem):
        copy = pltpu.make_async_copy(table_ref, out_ref, sem)
        copy.start()
        copy.wait()

    table = jnp.asarray(plan.tables)
    return pl.pallas_call(
        kernel,
        out_shape=jax.ShapeDtypeStruct(table.shape, table.dtype),
        in_specs=[pl.BlockSpec(memory_space=pltpu.HBM), pl.BlockSpec(memory_space=pltpu.VMEM)],
        out_specs=pl.BlockSpec(memory_space=pltpu.VMEM),
        scratch_shapes=[pltpu.SemaphoreType.DMA],
        compiler_params=pltpu.CompilerParams(vmem_limit_bytes=MIB),
        cost_estimate=pl.CostEstimate(flops=0, bytes_accessed=2 * table.nbytes, transcendentals=0),
    )(table, after)


def operate(plan, mis, wt, side, near, following, tables):
    rows, cols, sr, lon_total = plan.rows, plan.cols, plan.swath_rows, plan.lon_total
    n_dev = plan.lat_total * lon_total

    def kernel(mis_ref, wt_ref, side_ref, near_ref, next_ref, table_ref, *out_refs):
        base_refs, image_refs = out_refs[:LEVELS], out_refs[LEVELS : 2 * LEVELS]
        surface_refs, part_ref = out_refs[2 * LEVELS : -1], out_refs[-1]
        lat = lax.axis_index("lat")
        lon = lax.axis_index("lon")
        even = lat % 2 == 0
        col_tables, turned_tables, row_tables = [], [], []
        for k in range(COARSE):
            places = slice(plan.col_starts[k], plan.col_starts[k + 1])
            turned_tables.append(tuple(table_ref[half, places, plan.turned_start :] for half in (0, 1)))
            lanes = slice(plan.col_starts[k], plan.col_starts[k + 1])
            col_tables.append(tuple(table_ref[half, 0 : plan.col_frame, lanes] for half in (0, 1)))
        for start, height, width in plan.row_places:
            lanes = slice(plan.col_starts[-1], plan.col_starts[-1] + width)
            row_tables.append(tuple(table_ref[half, start : start + height, lanes] for half in (0, 1)))
        outer_t, inner_t, wide_s, tile_s = row_tables

        near_all, next_all = near_ref[...], next_ref[...]
        below = jnp.where(even, near_all, next_all)
        above = jnp.where(even, next_all, near_all)
        below, below_sums, below_wt = open_letter(plan, below)
        above, above_sums, above_wt = open_letter(plan, above)
        cells = jnp.concatenate([mis_ref[...], below, above], axis=0)
        outer = jnp.concatenate([cells, below_sums, above_sums], axis=0)
        own_weight = jnp.concatenate([wt_ref[...], side_ref[...]], axis=1)
        weight = jnp.concatenate([own_weight, below_wt, above_wt], axis=0)

        masks = []
        for k in range(LEVELS):
            s = SPACINGS[k]
            masks.append(
                side_mask(plan.node_rows[k], rows // s, (plan.node_rows[k] - rows // s) // 2, lat, plan.lat_total - 1, 0)
                * side_mask(plan.node_cols[k], cols // s, HALO // s, lon, lon_total - 1, 1)
            )
        def collect(values, row_table, starts):
            gathered = dot3(row_table, split(values))
            return [
                dot3(split(gathered[starts[k] : starts[k + 1]]), col_tables[k]) for k in range(COARSE)
            ]

        def spread(coeffs, width):
            turned = [tuple(part[:, 0:width] for part in table) for table in turned_tables]
            return split(jnp.concatenate([dot3(split(coeffs[k]), turned[k]) for k in range(COARSE)], axis=0))

        def cut(x, k):
            total = plan.near_rows[k]
            if x.shape[0] == total:
                return x
            side = (total - rows // SPACINGS[k]) // 2
            return jnp.concatenate([x[0 : total - side], x[x.shape[0] - side :]], axis=0)

        base = collect(outer, outer_t, plan.row_starts)
        base = [base[k] * masks[k] for k in range(COARSE)]
        finest = smooth(cells) * masks[COARSE]
        surface = dot3(wide_s, spread(base, plan.col_frame)) + cut(smooth(finest), COARSE)
        base = [cut(x, k) for k, x in enumerate(base + [finest])]
        masks = []
        for k in range(LEVELS):
            tile = rows // SPACINGS[k]
            side = (plan.near_rows[k] - tile) // 2
            masks.append(
                side_mask(plan.near_rows[k], tile, side, lat, plan.lat_total - 1, 0)
                * side_mask(plan.node_cols[k], cols // SPACINGS[k], HALO // SPACINGS[k], lon, lon_total - 1, 1)
            )

        image = collect(weight * surface, inner_t, plan.near_starts)
        image.append(smooth(weight * surface))
        rough_base, rough_image = [], []
        for k in range(LEVELS):
            once = autoreg(base[k]) * masks[k]
            rough_base.append(once)
            image[k] = (image[k] + level_scales[k] * autoreg(once)) * masks[k]
            rough_image.append(autoreg(image[k]))
        second = dot3(tile_s, spread(image, cols)) + smooth(image[COARSE])[0:rows, 0:cols]

        own = [(slice(0, rows // s), slice(0, cols // s)) for s in SPACINGS]
        b = [base[k][own[k]] for k in range(LEVELS)]
        ab = [image[k][own[k]] for k in range(LEVELS)]
        rb = [rough_base[k][own[k]] for k in range(LEVELS)]
        rab = [rough_image[k][own[k]] for k in range(LEVELS)]
        sb, sab = surface[0:rows, 0:cols], second[:, 0:cols]
        w = weight[0:rows, 0:cols]

        for k in range(LEVELS):
            base_refs[k][...] = b[k]
            image_refs[k][...] = ab[k]
        surface_refs[0][0:rows, :] = sb
        surface_refs[0][rows:, :] = sab
        for k in range(1, lon_total):
            take = pl.ds(pl.multiple_of((lon ^ k) * sr, sr), sr)
            surface_refs[k][0:sr, :] = surface_refs[0][take, :]
            take = pl.ds(pl.multiple_of(rows + (lon ^ k) * sr, sr), sr)
            surface_refs[k][sr:, :] = surface_refs[0][take, :]

        def pieces(*arrays):
            height, width = arrays[0].shape
            for at in range(0, height, 8):
                for lane in range(0, width, LANES):
                    yield [x[at : at + 8, lane : min(lane + LANES, width)] for x in arrays]

        def gather(terms):
            totals = None
            for values in terms:
                totals = values if totals is None else [t + v for t, v in zip(totals, values)]
            short = LANES - totals[0].shape[1]
            if short:
                totals = [jnp.concatenate([t, jnp.zeros((8, short), jnp.float32)], axis=1) for t in totals]
            return totals

        def add_levels(per_level, scaled_from):
            out = list(per_level[0])
            for n in range(len(out)):
                scales = level_scales if n >= scaled_from else (1.0,) * LEVELS
                out[n] = sum(scales[k] * per_level[k][n] for k in range(LEVELS))
            return out

        first_sums = add_levels(
            [gather([x * x, y * y] for x, y in pieces(b[k], rb[k])) for k in range(LEVELS)], 1
        )
        a0 = first_sums[0]
        a1 = first_sums[1] + gather([v * f * f] for v, f in pieces(w, sb))[0]
        top = jnp.sum(a0, keepdims=True)
        bottom = jnp.sum(a1, keepdims=True)
        tau = jnp.where(bottom > 0.0, top / jnp.where(bottom > 0.0, bottom, 1.0), 0.0)

        def residual_terms(x, ax, y, ay):
            r, rr = x - tau * ax, y - tau * ay
            return [r * r, r * ax, ax * ax, rr * rr, rr * ay, ay * ay, rr * y, ay * y]

        def field_terms(v, f, af):
            r = f - tau * af
            vr, va = v * r, v * af
            return [vr * r, vr * af, va * af, vr * f, va * f]

        later_sums = add_levels(
            [gather(residual_terms(*p) for p in pieces(b[k], ab[k], rb[k], rab[k])) for k in range(LEVELS)], 3
        )
        fields = gather(field_terms(*p) for p in pieces(w, sb, sab))
        blocks = [a0, a1, *later_sums[:3], *(x + y for x, y in zip(later_sums[3:], fields))]
        lines = [jnp.sum(block, axis=0, keepdims=True) for block in blocks]
        lane = lax.broadcasted_iota(jnp.int32, (1, LANES), 1)
        lines.append(jnp.where(lane == 0, tau, 0.0))
        lines.append(jnp.zeros((16 - len(lines), LANES), jnp.float32))
        sums = jnp.sum(jnp.concatenate(lines, axis=0), axis=1, keepdims=True)
        place = lax.broadcasted_iota(jnp.int32, (16, LANES), 0)
        lanes = lax.broadcasted_iota(jnp.int32, (16, LANES), 1)
        line = jnp.sum(jnp.where(place == lanes, sums, 0.0), axis=0, keepdims=True)
        part_ref[...] = jnp.broadcast_to(line, (n_dev, LANES))

    level_shapes = [(rows // s, cols // s) for s in SPACINGS]
    outs = level_shapes * 2 + [(2 * rows, cols)] + [(2 * sr, cols)] * (lon_total - 1) + [(n_dev, LANES)]
    results = call(kernel, outs, 24)(mis, wt, side, near, following, tables)
    return results[:LEVELS], results[LEVELS : 2 * LEVELS], results[2 * LEVELS : -1], results[-1]


def finish(plan, parts, base, image, own_surface, far_surfaces):
    rows, cols, sr, lon_total = plan.rows, plan.cols, plan.swath_rows, plan.lon_total

    def kernel(part_ref, *rest):
        base_refs, image_refs = rest[:LEVELS], rest[LEVELS : 2 * LEVELS]
        own_ref, far_refs = rest[2 * LEVELS], rest[2 * LEVELS + 1 : 2 * LEVELS + lon_total]
        out_refs, swath_ref = rest[-LEVELS - 1 : -1], rest[-1]
        lon = lax.axis_index("lon")
        part = part_ref[...]
        lane = lax.broadcasted_iota(jnp.int32, part.shape, 1)

        def column(n):
            return jnp.sum(jnp.where(lane == n, part, 0.0), axis=1, keepdims=True)

        def total(values):
            return jnp.sum(values, axis=0, keepdims=True)

        a0, a1, p1, p2, p3, c1, c2, c3, c4, c5, tau = [column(n) for n in range(11)]
        sum0, sum1 = total(a0), total(a1)
        step = sum0 / sum1
        gap = tau - step
        norm = total(p1 + 2.0 * gap * p2 + gap * gap * p3)
        curv_res = total(c1 + 2.0 * gap * c2 + gap * gap * c3)
        curv_mix = total(c4 + gap * c5)
        ratio = norm / sum0
        curv = curv_res + 2.0 * ratio * curv_mix + ratio * ratio * sum1
        next_step = norm / curv
        alpha = step + next_step * (1.0 + ratio)
        beta = -next_step * step
        for k in range(LEVELS):
            out_refs[k][...] = alpha * base_refs[k][...] + beta * image_refs[k][...]
        take = pl.ds(pl.multiple_of(lon * sr, sr), sr)
        later = pl.ds(pl.multiple_of(rows + lon * sr, sr), sr)
        fields = [(own_ref[take, :], own_ref[later, :])]
        fields += [(ref[0:sr, :], ref[sr:, :]) for ref in far_refs]
        for k in range(lon_total):
            here = pl.ds(pl.multiple_of((lon ^ k) * cols, LANES), cols)
            swath_ref[:, here] = alpha * fields[k][0] + beta * fields[k][1]

    outs = [(rows // s, cols // s) for s in SPACINGS] + [(sr, plan.width)]
    return call(kernel, outs, 8)(parts, *base, *image, own_surface, *far_surfaces)


def turn(x, axis, total, k):
    return lax.ppermute(x, axis, [(i, (i + k) % total) for i in range(total)])


def flip(x, axis, total, k):
    return lax.ppermute(x, axis, [(i, i ^ k) for i in range(total)])


def odd_swap(x, axis, total):
    pairs = [(i, i + 1) for i in range(1, total - 1, 2)]
    return lax.ppermute(x, axis, pairs + [(j, i) for i, j in pairs])


def body(observed, gauged):
    lat_total, lon_total = lax.axis_size("lat"), lax.axis_size("lon")
    plan = Plan(observed.shape, gauged.shape, lat_total, lon_total)
    weight, own, *windows = pack(plan, observed, gauged)
    right, *far, left = [turn(x, "lon", lon_total, k) for k, x in enumerate(windows, 1)]
    mis, side, near, following = misfit(plan, own, right, left, far, weight)
    tables = fetch(plan, side)
    near = flip(near, "lat", lat_total, 1)
    following = odd_swap(following, "lat", lat_total)
    base, image, surfaces, parts = operate(plan, mis, weight, side, near, following, tables)
    far_surfaces = [flip(x, "lon", lon_total, k) for k, x in enumerate(surfaces[1:], 1)]
    parts = lax.all_to_all(parts, ("lat", "lon"), split_axis=0, concat_axis=0, tiled=True)
    return tuple(finish(plan, parts, base, image, surfaces[0], far_surfaces))


def solution(mesh):
    return jax.shard_map(
        body,
        mesh=mesh,
        in_specs=(P(("lat", "lon"), None), P("lat", "lon")),
        out_specs=(
            P("lat", "lon"),
            P("lat", "lon"),
            P("lat", "lon"),
            P("lat", "lon"),
            P(("lat", "lon"), None),
        ),
        check_vma=False,
    )
```

```python
import math

import jax
import jax.numpy as jnp
import numpy as np
from jax import lax
from jax.experimental import pallas as pl
from jax.experimental.pallas import tpu as pltpu
from jax.sharding import PartitionSpec as P

LEVELS = 4
SPACINGS = tuple(2 ** (LEVELS - 1 - k) for k in range(LEVELS))
COARSE = LEVELS - 1
HALO = 64
INNER = 32
RAW = 40
PART_ROWS = 8
EDGE = 32
NEAR = 8
LANES = 128

data_weight = 2.0
kappa_term = 5.0
level_scales = (0.02, 0.03, 0.05, 0.08)

MIB = 1024 * 1024


def wendland(distance, of=np):
    remain = of.maximum(1.0 - distance, 0.0)
    cube = remain * remain * remain
    return cube * cube * (35.0 * distance * distance + 18.0 * distance + 3.0) / 3.0


def frame_index(total, tile, halo):
    place = np.arange(total)
    index = np.where(place < tile + halo, place, place - total)
    return index, (place < tile + halo) | (place >= total - halo)


def basis(cells, nodes, spacing):
    (cell, cell_ok), (node, node_ok) = cells, nodes
    numerator = np.abs(2 * cell[:, None] - 2 * spacing * node[None, :] - (spacing - 1))
    table = wendland(numerator / (5.0 * spacing)) / math.sqrt(spacing)
    return np.where(cell_ok[:, None] & node_ok[None, :], table, 0.0).astype(np.float32)


def halves(table):
    high = table.astype(jnp.bfloat16)
    low = (table - high.astype(np.float32)).astype(jnp.bfloat16)
    return np.stack([high, low])


def split(x):
    high = x.astype(jnp.bfloat16)
    return high, (x - high.astype(jnp.float32)).astype(jnp.bfloat16)


def dot(a, b, contract):
    return lax.dot_general(a, b, ((contract[0:1], contract[1:2]), ((), ())), preferred_element_type=jnp.float32)


def dot3(a, b, contract=(1, 0)):
    (ah, al), (bh, bl) = a, b
    n = ah.shape[0]
    both = dot(jnp.concatenate([ah, al], axis=0), bh, contract)
    return both[0:n] + (both[n:] + dot(ah, bl, contract))


TAPS = (float(wendland(np.float64(0.4))), float(wendland(np.float64(0.8))))


def shift(x, step, axis):
    return pltpu.roll(x, step % x.shape[axis], axis)


def smooth(x):
    for axis in (0, 1):
        near = shift(x, 1, axis) + shift(x, -1, axis)
        far = shift(x, 2, axis) + shift(x, -2, axis)
        x = x + (TAPS[0] * near + TAPS[1] * far)
    return x


def autoreg(x):
    beside = shift(x, 1, 0) + shift(x, -1, 0) + shift(x, 1, 1) + shift(x, -1, 1)
    return kappa_term * x - beside


def side_mask(total, tile, halo, at, last, dim):
    shape = (total, 1) if dim == 0 else (1, total)
    place = lax.broadcasted_iota(jnp.int32, shape, dim)
    after = (place < tile + halo) & (at < last)
    before = (place >= total - halo) & (at > 0)
    return ((place < tile) | after | before).astype(jnp.float32)


class Plan:
    def __init__(self, swath_shape, tile_shape, lat_total, lon_total):
        self.swath_rows, self.width = swath_shape
        self.rows, self.cols = tile_shape
        self.lat_total, self.lon_total = lat_total, lon_total
        self.col_frame = self.cols + 2 * HALO
        self.outer_rows = self.rows + 2 * RAW
        self.inner_rows = self.rows + 2 * INNER
        wide = [-(-(self.rows // s + 2 * (INNER // s + 2)) // 16) * 16 for s in SPACINGS[:COARSE]]
        self.node_rows = wide + [self.outer_rows]
        self.near_rows = [min(w, self.rows // s + 2 * NEAR) for w, s in zip(wide, SPACINGS)]
        self.near_rows.append(self.rows + 2 * NEAR)
        self.near_starts = np.cumsum([0] + self.near_rows[:COARSE]).tolist()
        self.node_cols = [-(-self.col_frame // (s * LANES)) * LANES for s in SPACINGS]
        self.row_starts = np.cumsum([0] + self.node_rows[:COARSE]).tolist()
        self.col_starts = np.cumsum([0] + self.node_cols[:COARSE]).tolist()
        col_cells = frame_index(self.col_frame, self.cols, HALO)
        outer = frame_index(self.outer_rows, self.rows, RAW)
        inner = frame_index(self.inner_rows, self.rows, INNER)
        col_tables, outer_rows, inner_rows, wide_rows = [], [], [], []
        self.part_nodes, place_all = [], []
        for k in range(COARSE):
            s = SPACINGS[k]
            tile = self.rows // s
            col_nodes = frame_index(self.node_cols[k], self.cols // s, HALO // s)
            row_nodes = frame_index(self.node_rows[k], tile, (self.node_rows[k] - tile) // 2)
            near_nodes = frame_index(self.near_rows[k], tile, (self.near_rows[k] - tile) // 2)
            col_tables.append(basis(col_cells, col_nodes, s))
            outer_rows.append(basis(outer, row_nodes, s))
            wide_rows.append(basis(inner, row_nodes, s))
            inner_rows.append(basis(inner, near_nodes, s))
            for away in range((RAW - 2 * s) // s, INNER // s + 2):
                self.part_nodes.append((s, away))
                at = self.row_starts[k]
                place_all.append((at + tile + away, at + self.node_rows[k] - 1 - away))
        nodes = self.row_starts[-1]
        joins = np.zeros((2 * PART_ROWS, nodes), np.float32)
        for n, (after_at, before_at) in enumerate(place_all):
            joins[n, after_at] = 1.0
            joins[PART_ROWS + n, before_at] = 1.0
        outer_all = np.concatenate([np.concatenate(outer_rows, axis=1), joins], axis=0)
        inner_all = np.concatenate(inner_rows, axis=1)
        wide_all = np.concatenate(wide_rows, axis=1)
        self.edge_nodes, sel = [], []
        for k in range(COARSE):
            first, total = self.rows // SPACINGS[k] - NEAR, self.node_rows[k]
            self.edge_nodes.append(total - first + NEAR)
            sel += [self.row_starts[k] + at for at in (*range(first, total), *range(NEAR))]
        self.edge_starts = np.cumsum([0] + self.edge_nodes).tolist()
        edge_rows = [*range(self.rows - EDGE, self.inner_rows), *range(EDGE)]
        row_tables = [
            outer_all[: self.rows].T,
            outer_all[self.rows :].T[sel],
            inner_all.T,
            wide_all,
            wide_all[edge_rows][:, sel],
            inner_all[: self.rows],
        ]
        lanes = -(-max(t.shape[1] for t in row_tables) // LANES) * LANES
        self.row_places, ends = [], [0, 0]
        for table in row_tables:
            side = int(ends[1] < ends[0])
            self.row_places.append((ends[side], table.shape[0], self.col_starts[-1] + side * lanes, table.shape[1]))
            ends[side] += table.shape[0]
        at = max(ends)
        col_all = np.concatenate(col_tables, axis=1)
        self.turned_start = self.col_starts[-1] + 2 * lanes
        whole = np.zeros((max(at, *col_all.shape), self.turned_start + self.col_frame), np.float32)
        whole[: self.col_frame, : self.col_starts[-1]] = col_all
        whole[: self.col_starts[-1], self.turned_start :] = col_all.T
        for (start, height, lane, width), table in zip(self.row_places, row_tables):
            whole[start : start + height, lane : lane + width] = table
        self.tables = halves(whole)
        tiles = self.col_frame // LANES
        self.sums = len(self.part_nodes)
        self.letter_rows = -(-(self.letter()[-1] + tiles * self.sums) // 8) * 8

    def pick(self, table_ref):
        col_tables, turned_tables, row_tables = [], [], []
        for k in range(COARSE):
            places = slice(self.col_starts[k], self.col_starts[k + 1])
            turned_tables.append(tuple(table_ref[half, places, self.turned_start :] for half in (0, 1)))
            col_tables.append(tuple(table_ref[half, 0 : self.col_frame, places] for half in (0, 1)))
        for start, height, lane, width in self.row_places:
            rows, lanes = slice(start, start + height), slice(lane, lane + width)
            row_tables.append(tuple(table_ref[half, rows, lanes] for half in (0, 1)))
        return col_tables, turned_tables, row_tables

    def masks(self, heights):
        lat, lon = lax.axis_index("lat"), lax.axis_index("lon")
        out = []
        for k, s in enumerate(SPACINGS):
            tile = self.rows // s
            rows = side_mask(heights[k], tile, (heights[k] - tile) // 2, lat, self.lat_total - 1, 0)
            cols = side_mask(self.node_cols[k], self.cols // s, HALO // s, lon, self.lon_total - 1, 1)
            out.append(rows * cols)
        return out

    def letter(self):
        tiles = self.col_frame // LANES
        weights = tiles * RAW
        corner = weights + (tiles - 1) * INNER
        return 0, weights, corner, corner + INNER // 2


def call(kernel, outs, limit, scratch=(), spaces=None):
    def run(*operands):
        in_spaces = spaces or [pltpu.VMEM] * len(operands)
        return pl.pallas_call(
            kernel,
            out_shape=[jax.ShapeDtypeStruct(shape, jnp.float32) for shape in outs],
            in_specs=[pl.BlockSpec(memory_space=space) for space in in_spaces],
            out_specs=[pl.BlockSpec(memory_space=pltpu.VMEM)] * len(outs),
            scratch_shapes=list(scratch),
            compiler_params=pltpu.CompilerParams(vmem_limit_bytes=int(limit * MIB)),
        )(*operands)

    return run


def window(plan, obs_ref, to):
    sr, width, cols = plan.swath_rows, plan.width, plan.cols
    base = pl.multiple_of(to * cols, LANES)
    lane = lax.broadcasted_iota(jnp.int32, (sr, LANES), 1)
    before = obs_ref[:, pl.ds(pl.multiple_of(jnp.maximum(base - LANES, 0), LANES), LANES)]
    after = obs_ref[:, pl.ds(pl.multiple_of(jnp.minimum(base + cols, width - LANES), LANES), LANES)]
    before = jnp.where(to > 0, before, 0.0)
    after = jnp.where(to < plan.lon_total - 1, after, 0.0)
    return obs_ref[:, pl.ds(base, cols)], jnp.where(lane < HALO, after, before)


def pack(plan, observed, gauged):
    sr, width, cols, rows, n = plan.swath_rows, plan.width, plan.cols, plan.rows, plan.lon_total
    tiles = plan.col_frame // LANES

    def kernel(obs_hbm, gauge_hbm, *rest):
        wt_ref, out_refs, (obs_ref, gauge_ref, sems) = rest[0], rest[1 : n + 1], rest[n + 1 :]
        copies = [
            pltpu.make_async_copy(obs_hbm, obs_ref, sems.at[0]),
            pltpu.make_async_copy(gauge_hbm, gauge_ref, sems.at[1]),
        ]
        for copy in copies:
            copy.start()
        at = lax.axis_index("lon")
        half_lane = lax.broadcasted_iota(jnp.int32, (rows // 2, LANES), 1)
        copies[0].wait()
        for k, ref in enumerate(out_refs):
            main, sides = window(plan, obs_ref, lax.rem(at + k, n))
            if k in (1, n - 1):
                for t in range(tiles - 1):
                    ref[t * sr : (t + 1) * sr, :] = main[:, t * LANES : (t + 1) * LANES]
                ref[(tiles - 1) * sr : tiles * sr, :] = sides
            else:
                ref[:, 0:cols] = main
                ref[:, cols:] = sides
        copies[1].wait()
        wt_ref[...] = data_weight * gauge_ref[...].astype(jnp.float32)
        for k in (1, n - 1):
            edge = wt_ref[:, cols - LANES :] if k == 1 else wt_ref[:, 0:LANES]
            kept = (half_lane >= HALO) if k == 1 else (half_lane < HALO)
            turned = pltpu.roll(edge[rows // 2 :], HALO, 1)
            out_refs[k][tiles * sr :, :] = jnp.where(kept, edge[0 : rows // 2], turned)

    side = (tiles * sr + rows // 2, LANES)
    outs = [(rows, cols)] + [side if k in (1, n - 1) else (sr, plan.col_frame) for k in range(n)]
    scratch = [
        pltpu.VMEM((sr, width), jnp.float32),
        pltpu.VMEM((rows, cols), jnp.int32),
        pltpu.SemaphoreType.DMA((2,)),
    ]
    return call(kernel, outs, 53.25, scratch, [pltpu.HBM] * 2)(observed, gauged)


def misfit(plan, own, right, left, far, weight, tables):
    sr, cols, rows, n = plan.swath_rows, plan.cols, plan.rows, plan.lon_total
    tiles = plan.col_frame // LANES

    def kernel(own_ref, right_ref, left_ref, wt_ref, table_ref, *rest):
        far_refs, (mis_ref, side_ref, near_ref, next_ref) = rest[: n - 3], rest[n - 3 :]
        at = lax.axis_index("lon")
        lane = lax.broadcasted_iota(jnp.int32, (rows, LANES), 1)

        def side(ref, present):
            packed = ref[tiles * sr :, :]
            both = jnp.concatenate([packed, pltpu.roll(packed, HALO, 1)], axis=0)
            return jnp.where(present, both, 0.0)

        side_ref[...] = jnp.where(lane < HALO, side(left_ref, at < n - 1), side(right_ref, at > 0))

        for k, ref in enumerate((own_ref, right_ref, *far_refs, left_ref)):
            here = pl.ds(pl.multiple_of(lax.rem(at + (n - k), n) * sr, sr), sr)
            if k in (1, n - 1):
                for t in range(tiles - 1):
                    lanes = slice(t * LANES, (t + 1) * LANES)
                    mis_ref[here, lanes] = wt_ref[here, lanes] * ref[t * sr : (t + 1) * sr, :]
                mis_ref[here, cols:] = side_ref[here, :] * ref[(tiles - 1) * sr : tiles * sr, :]
            else:
                mis_ref[here, 0:cols] = wt_ref[here, :] * ref[:, 0:cols]
                mis_ref[here, cols:] = side_ref[here, :] * ref[:, cols:]

        up = lax.axis_index("lat") % 2
        depth = HALO - RAW
        shape = (PART_ROWS, depth)
        line = lax.broadcasted_iota(jnp.int32, shape, 0)
        cell = lax.broadcasted_iota(jnp.int32, shape, 1)
        for ref, low in ((near_ref, 1 - up), (next_ref, up)):
            far = mis_ref[pl.ds(pl.multiple_of(RAW + low * (rows - HALO - RAW), 8), depth), :]
            table = jnp.zeros(shape, jnp.float32)
            distance = jnp.where(low == 1, HALO - 1 - cell, RAW + cell)
            for m, (s, away) in enumerate(plan.part_nodes):
                numerator = jnp.abs(2 * distance - 2 * s * away - (s - 1)).astype(jnp.float32)
                table = jnp.where(line == m, wendland(numerator / (5.0 * s), jnp) / math.sqrt(s), table)
            edge = pl.ds(pl.multiple_of(low * (rows - INNER), 8), INNER)
            sums = jnp.dot(table, far, precision=lax.Precision.HIGHEST, preferred_element_type=jnp.float32)
            near = mis_ref[pl.ds(pl.multiple_of(low * (rows - RAW), 8), RAW), :]
            raw, weights, corner, parts = plan.letter()
            for t in range(tiles):
                lanes = slice(t * LANES, (t + 1) * LANES)
                ref[raw + t * RAW : raw + (t + 1) * RAW, :] = near[:, lanes]
                if t < tiles - 1:
                    ref[weights + t * INNER : weights + (t + 1) * INNER, :] = wt_ref[edge, lanes]
                ref[parts + t * plan.sums : parts + (t + 1) * plan.sums, :] = sums[0 : plan.sums, lanes]
            beside = side_ref[edge, :]
            turned = pltpu.roll(beside[INNER // 2 :], HALO, 1)
            some = lax.broadcasted_iota(jnp.int32, (INNER // 2, LANES), 1)
            outer = (some < INNER) | (some >= LANES - INNER)
            ref[corner : corner + INNER // 2, :] = jnp.where(outer, beside[0 : INNER // 2], turned)
            ref[parts + tiles * plan.sums :, :] = jnp.zeros((plan.letter_rows - parts - tiles * plan.sums, LANES), jnp.float32)

    outs = [(rows, plan.col_frame), (rows, LANES)] + [(plan.letter_rows, LANES)] * 2
    return call(kernel, outs, 4)(own, right, left, weight, tables, *far)


def open_letter(plan, letter):
    tiles = plan.col_frame // LANES
    raw, weights, corner, parts = plan.letter()
    near = [letter[raw + t * RAW : raw + (t + 1) * RAW] for t in range(tiles)]
    sums = [letter[parts + t * plan.sums : parts + (t + 1) * plan.sums] for t in range(tiles)]
    sums = jnp.concatenate(sums, axis=1)
    sums = jnp.concatenate([sums, jnp.zeros((PART_ROWS - plan.sums, plan.col_frame), jnp.float32)], axis=0)
    rows = [letter[weights + t * INNER : weights + (t + 1) * INNER] for t in range(tiles - 1)]
    both = letter[corner : corner + INNER // 2]
    some = lax.broadcasted_iota(jnp.int32, (INNER // 2, LANES), 1)
    outer = (some < INNER) | (some >= LANES - INNER)
    beside = [jnp.where(outer, x, 0.0) for x in (both, pltpu.roll(both, HALO, 1))]
    rows.append(jnp.concatenate(beside, axis=0))
    return jnp.concatenate(near, axis=1), sums, jnp.concatenate(rows, axis=1)


def fetch(plan, after):
    def kernel(table_ref, after_ref, out_ref, sem):
        copy = pltpu.make_async_copy(table_ref, out_ref, sem)
        copy.start()
        copy.wait()

    table = jnp.asarray(plan.tables)
    return pl.pallas_call(
        kernel,
        out_shape=jax.ShapeDtypeStruct(table.shape, table.dtype),
        in_specs=[pl.BlockSpec(memory_space=pltpu.HBM), pl.BlockSpec(memory_space=pltpu.VMEM)],
        out_specs=pl.BlockSpec(memory_space=pltpu.VMEM),
        scratch_shapes=[pltpu.SemaphoreType.DMA],
        compiler_params=pltpu.CompilerParams(vmem_limit_bytes=MIB),
        cost_estimate=pl.CostEstimate(flops=0, bytes_accessed=2 * table.nbytes, transcendentals=0),
    )(table, after)


def inside(plan, mis, tables):
    rows, inner_rows = plan.rows, plan.inner_rows
    shapes = [(plan.node_rows[k], plan.node_cols[k]) for k in range(COARSE)] + [(rows + 2 * NEAR, plan.col_frame)]

    def kernel(mis_ref, table_ref, *out_refs):
        base_refs, surface_ref = out_refs[:LEVELS], out_refs[LEVELS]
        col_tables, turned_tables, (own_t, _, _, wide_s, _, _) = plan.pick(table_ref)
        masks = plan.masks([height for height, _ in shapes])
        mis = mis_ref[...]
        gathered = dot3(own_t, split(mis))
        starts = plan.row_starts
        base = [dot3(split(gathered[starts[k] : starts[k + 1]]), col_tables[k]) * masks[k] for k in range(COARSE)]
        blank = jnp.zeros((2 * NEAR, plan.col_frame), jnp.float32)
        base.append(smooth(jnp.concatenate([mis, blank], axis=0)) * masks[COARSE])
        for k in range(LEVELS):
            base_refs[k][...] = base[k]
        fine = smooth(base[COARSE])
        blank = jnp.zeros((inner_rows - rows - 2 * NEAR, plan.col_frame), jnp.float32)
        fine = jnp.concatenate([fine[0 : rows + NEAR], blank, fine[rows + NEAR :]], axis=0)
        spread = jnp.concatenate([dot3(split(base[k]), turned_tables[k]) for k in range(COARSE)], axis=0)
        surface_ref[...] = fine + dot3(wide_s, split(spread))

    *base, surface = call(kernel, shapes + [(inner_rows, plan.col_frame)], 24)(mis, tables)
    return base, surface


def operate(plan, mid, mid_surface, wt, side, near, following, tables):
    rows, cols, sr, lon_total = plan.rows, plan.cols, plan.swath_rows, plan.lon_total
    n_dev = plan.lat_total * lon_total

    def kernel(mid_surface_ref, wt_ref, side_ref, near_ref, next_ref, table_ref, *out_refs):
        mid_refs, out_refs = out_refs[:LEVELS], out_refs[LEVELS:]
        base_refs, image_refs = out_refs[:LEVELS], out_refs[LEVELS : 2 * LEVELS]
        surface_refs, part_ref = out_refs[2 * LEVELS : -1], out_refs[-1]
        lat = lax.axis_index("lat")
        lon = lax.axis_index("lon")
        even = lat % 2 == 0
        col_tables, turned_tables, row_tables = plan.pick(table_ref)
        _, edge_t, inner_t, _, edge_s, tile_s = row_tables
        near_all, next_all = near_ref[...], next_ref[...]
        below = jnp.where(even, near_all, next_all)
        above = jnp.where(even, next_all, near_all)
        below, below_sums, below_wt = open_letter(plan, below)
        above, above_sums, above_wt = open_letter(plan, above)
        own_weight = jnp.concatenate([wt_ref[...], side_ref[...]], axis=1)
        weight = jnp.concatenate([own_weight, below_wt, above_wt], axis=0)

        masks = plan.masks(plan.node_rows)

        def collect(gathered, starts):
            return [dot3(split(gathered[starts[k] : starts[k + 1]]), col_tables[k]) for k in range(COARSE)]

        def spread(coeffs, width):
            turned = [tuple(part[:, 0:width] for part in table) for table in turned_tables]
            return split(jnp.concatenate([dot3(split(coeffs[k]), turned[k]) for k in range(COARSE)], axis=0))

        def cut(x, k, total):
            if x.shape[0] == total:
                return x
            side = (total - rows // SPACINGS[k]) // 2
            return jnp.concatenate([x[0 : total - side], x[x.shape[0] - side :]], axis=0)

        def blank(height, like):
            return jnp.zeros((height, like.shape[1]), jnp.float32)

        around = jnp.concatenate([below, above, below_sums, above_sums], axis=0)
        edge = collect(dot3(edge_t, split(around)), plan.edge_starts)
        base = []
        for k in range(COARSE):
            first = plan.edge_nodes[k] - NEAR
            tile = rows // SPACINGS[k]
            mask = jnp.concatenate([masks[k][tile - NEAR :], masks[k][0:NEAR]], axis=0)
            edge[k] = edge[k] * mask
            added = [edge[k][first:], edge[k][0:first]]
            if tile > 2 * NEAR:
                added.insert(1, blank(tile - 2 * NEAR, edge[k]))
            base.append(cut(mid_refs[k][...] + jnp.concatenate(added, axis=0), k, plan.near_rows[k]))
        strip = jnp.concatenate([blank(NEAR, below), below, above, blank(NEAR, above)], axis=0)
        fine_mask = masks[COARSE]
        strip_mask = jnp.concatenate([fine_mask[rows - NEAR :], fine_mask[0:NEAR]], axis=0)
        strip = smooth(strip) * strip_mask
        last = strip.shape[0] - NEAR
        added = [strip[last:], blank(rows - 2 * NEAR, strip), strip[0 : 2 * NEAR], strip[last - NEAR : last]]
        base.append(mid_refs[COARSE][...] + jnp.concatenate(added, axis=0))
        fine = smooth(strip)
        added = [fine[last:], blank(rows - 2 * NEAR, fine), fine[0 : NEAR + INNER], fine[last - INNER : last]]
        surface = mid_surface_ref[...] + jnp.concatenate(added, axis=0)
        coarse = dot3(edge_s, spread(edge, plan.col_frame))
        body_rows = coarse.shape[0] - EDGE
        added = [coarse[body_rows:], blank(rows - 2 * EDGE, coarse), coarse[0:body_rows]]
        surface = surface + jnp.concatenate(added, axis=0)
        masks = plan.masks(plan.near_rows)

        misfit_again = weight * surface
        image = collect(dot3(inner_t, split(misfit_again)), plan.near_starts)
        image.append(smooth(cut(misfit_again, COARSE, plan.near_rows[COARSE])))
        rough_base, rough_image = [], []
        for k in range(LEVELS):
            once = autoreg(base[k]) * masks[k]
            rough_base.append(once)
            image[k] = (image[k] + level_scales[k] * autoreg(once)) * masks[k]
            rough_image.append(autoreg(image[k]))
        second = dot3(tile_s, spread(image, cols)) + smooth(image[COARSE])[0:rows, 0:cols]

        own = [(slice(0, rows // s), slice(0, cols // s)) for s in SPACINGS]
        b = [base[k][own[k]] for k in range(LEVELS)]
        ab = [image[k][own[k]] for k in range(LEVELS)]
        rb = [rough_base[k][own[k]] for k in range(LEVELS)]
        rab = [rough_image[k][own[k]] for k in range(LEVELS)]
        sb, sab = surface[0:rows, 0:cols], second[:, 0:cols]
        w = weight[0:rows, 0:cols]

        for k in range(LEVELS):
            base_refs[k][...] = b[k]
            image_refs[k][...] = ab[k]
        surface_refs[0][0:rows, :] = sb
        surface_refs[0][rows:, :] = sab
        for k in range(1, lon_total):
            take = pl.ds(pl.multiple_of((lon ^ k) * sr, sr), sr)
            surface_refs[k][0:sr, :] = surface_refs[0][take, :]
            take = pl.ds(pl.multiple_of(rows + (lon ^ k) * sr, sr), sr)
            surface_refs[k][sr:, :] = surface_refs[0][take, :]

        def pieces(*arrays):
            height, width = arrays[0].shape
            for at in range(0, height, 8):
                for lane in range(0, width, LANES):
                    yield [x[at : at + 8, lane : min(lane + LANES, width)] for x in arrays]

        def gather(terms):
            totals = None
            for values in terms:
                totals = values if totals is None else [t + v for t, v in zip(totals, values)]
            short = LANES - totals[0].shape[1]
            if short:
                totals = [jnp.concatenate([t, jnp.zeros((8, short), jnp.float32)], axis=1) for t in totals]
            return totals

        def add_levels(per_level, scaled_from):
            out = list(per_level[0])
            for n in range(len(out)):
                scales = level_scales if n >= scaled_from else (1.0,) * LEVELS
                out[n] = sum(scales[k] * per_level[k][n] for k in range(LEVELS))
            return out

        first_sums = add_levels(
            [gather([x * x, y * y] for x, y in pieces(b[k], rb[k])) for k in range(LEVELS)], 1
        )
        a0 = first_sums[0]
        a1 = first_sums[1] + gather([v * f * f] for v, f in pieces(w, sb))[0]
        top = jnp.sum(a0, keepdims=True)
        bottom = jnp.sum(a1, keepdims=True)
        tau = jnp.where(bottom > 0.0, top / jnp.where(bottom > 0.0, bottom, 1.0), 0.0)

        def residual_terms(x, ax, y, ay):
            r, rr = x - tau * ax, y - tau * ay
            return [r * r, r * ax, ax * ax, rr * rr, rr * ay, ay * ay, rr * y, ay * y]

        def field_terms(v, f, af):
            r = f - tau * af
            vr, va = v * r, v * af
            return [vr * r, vr * af, va * af, vr * f, va * f]

        later_sums = add_levels(
            [gather(residual_terms(*p) for p in pieces(b[k], ab[k], rb[k], rab[k])) for k in range(LEVELS)], 3
        )
        fields = gather(field_terms(*p) for p in pieces(w, sb, sab))
        blocks = [a0, a1, *later_sums[:3], *(x + y for x, y in zip(later_sums[3:], fields))]
        lines = [jnp.sum(block, axis=0, keepdims=True) for block in blocks]
        lane = lax.broadcasted_iota(jnp.int32, (1, LANES), 1)
        lines.append(jnp.where(lane == 0, tau, 0.0))
        lines.append(jnp.zeros((16 - len(lines), LANES), jnp.float32))
        sums = jnp.sum(jnp.concatenate(lines, axis=0), axis=1, keepdims=True)
        place = lax.broadcasted_iota(jnp.int32, (16, LANES), 0)
        lanes = lax.broadcasted_iota(jnp.int32, (16, LANES), 1)
        line = jnp.sum(jnp.where(place == lanes, sums, 0.0), axis=0, keepdims=True)
        part_ref[...] = jnp.broadcast_to(line, (n_dev, LANES))

    level_shapes = [(rows // s, cols // s) for s in SPACINGS]
    outs = level_shapes * 2 + [(2 * rows, cols)] + [(2 * sr, cols)] * (lon_total - 1) + [(n_dev, LANES)]
    results = call(kernel, outs, 24)(mid_surface, wt, side, near, following, tables, *mid)
    return results[:LEVELS], results[LEVELS : 2 * LEVELS], results[2 * LEVELS : -1], results[-1]


def finish(plan, parts, base, image, own_surface, far_surfaces):
    rows, cols, sr, lon_total = plan.rows, plan.cols, plan.swath_rows, plan.lon_total

    def kernel(part_ref, *rest):
        base_refs, image_refs = rest[:LEVELS], rest[LEVELS : 2 * LEVELS]
        own_ref, far_refs = rest[2 * LEVELS], rest[2 * LEVELS + 1 : 2 * LEVELS + lon_total]
        out_refs, swath_ref = rest[-LEVELS - 1 : -1], rest[-1]
        lon = lax.axis_index("lon")
        part = part_ref[...]
        lane = lax.broadcasted_iota(jnp.int32, part.shape, 1)

        def column(n):
            return jnp.sum(jnp.where(lane == n, part, 0.0), axis=1, keepdims=True)

        def total(values):
            return jnp.sum(values, axis=0, keepdims=True)

        a0, a1, p1, p2, p3, c1, c2, c3, c4, c5, tau = [column(n) for n in range(11)]
        sum0, sum1 = total(a0), total(a1)
        step = sum0 / sum1
        gap = tau - step
        norm = total(p1 + 2.0 * gap * p2 + gap * gap * p3)
        curv_res = total(c1 + 2.0 * gap * c2 + gap * gap * c3)
        curv_mix = total(c4 + gap * c5)
        ratio = norm / sum0
        curv = curv_res + 2.0 * ratio * curv_mix + ratio * ratio * sum1
        next_step = norm / curv
        alpha = step + next_step * (1.0 + ratio)
        beta = -next_step * step
        for k in range(LEVELS):
            out_refs[k][...] = alpha * base_refs[k][...] + beta * image_refs[k][...]
        take = pl.ds(pl.multiple_of(lon * sr, sr), sr)
        later = pl.ds(pl.multiple_of(rows + lon * sr, sr), sr)
        fields = [(own_ref[take, :], own_ref[later, :])]
        fields += [(ref[0:sr, :], ref[sr:, :]) for ref in far_refs]
        for k in range(lon_total):
            here = pl.ds(pl.multiple_of((lon ^ k) * cols, LANES), cols)
            swath_ref[:, here] = alpha * fields[k][0] + beta * fields[k][1]

    outs = [(rows // s, cols // s) for s in SPACINGS] + [(sr, plan.width)]
    return call(kernel, outs, 8)(parts, *base, *image, own_surface, *far_surfaces)


def turn(x, axis, total, k):
    return lax.ppermute(x, axis, [(i, (i + k) % total) for i in range(total)])


def flip(x, axis, total, k):
    return lax.ppermute(x, axis, [(i, i ^ k) for i in range(total)])


def odd_swap(x, axis, total):
    pairs = [(i, i + 1) for i in range(1, total - 1, 2)]
    return lax.ppermute(x, axis, pairs + [(j, i) for i, j in pairs])


def body(observed, gauged):
    lat_total, lon_total = lax.axis_size("lat"), lax.axis_size("lon")
    plan = Plan(observed.shape, gauged.shape, lat_total, lon_total)
    weight, own, *windows = pack(plan, observed, gauged)
    tables = fetch(plan, own)
    right, *far, left = [turn(x, "lon", lon_total, k) for k, x in enumerate(windows, 1)]
    mis, side, near, following = misfit(plan, own, right, left, far, weight, tables)
    mid, mid_surface = inside(plan, mis, tables)
    near = flip(near, "lat", lat_total, 1)
    following = odd_swap(following, "lat", lat_total)
    base, image, surfaces, parts = operate(plan, mid, mid_surface, weight, side, near, following, tables)
    far_surfaces = [flip(x, "lon", lon_total, k) for k, x in enumerate(surfaces[1:], 1)]
    parts = lax.all_to_all(parts, ("lat", "lon"), split_axis=0, concat_axis=0, tiled=True)
    return tuple(finish(plan, parts, base, image, surfaces[0], far_surfaces))


def solution(mesh):
    return jax.shard_map(
        body,
        mesh=mesh,
        in_specs=(P(("lat", "lon"), None), P("lat", "lon")),
        out_specs=(
            P("lat", "lon"),
            P("lat", "lon"),
            P("lat", "lon"),
            P("lat", "lon"),
            P(("lat", "lon"), None),
        ),
        check_vma=False,
    )
```

```python
import math

import jax
import jax.numpy as jnp
import numpy as np
from jax import lax
from jax.experimental import pallas as pl
from jax.experimental.pallas import tpu as pltpu
from jax.sharding import PartitionSpec as P

LEVELS = 4
SPACINGS = tuple(2 ** (LEVELS - 1 - k) for k in range(LEVELS))
COARSE = LEVELS - 1
HALO = 64
INNER = 32
RAW = 40
PART_ROWS = 8
EDGE = 32
NEAR = 8
LANES = 128

data_weight = 2.0
kappa_term = 5.0
level_scales = (0.02, 0.03, 0.05, 0.08)

MIB = 1024 * 1024


def wendland(distance, of=np):
    remain = of.maximum(1.0 - distance, 0.0)
    cube = remain * remain * remain
    return cube * cube * (35.0 * distance * distance + 18.0 * distance + 3.0) / 3.0


def frame_index(total, tile, halo):
    place = np.arange(total)
    index = np.where(place < tile + halo, place, place - total)
    return index, (place < tile + halo) | (place >= total - halo)


def basis(cells, nodes, spacing):
    (cell, cell_ok), (node, node_ok) = cells, nodes
    numerator = np.abs(2 * cell[:, None] - 2 * spacing * node[None, :] - (spacing - 1))
    table = wendland(numerator / (5.0 * spacing)) / math.sqrt(spacing)
    return np.where(cell_ok[:, None] & node_ok[None, :], table, 0.0).astype(np.float32)


def halves(table):
    high = table.astype(jnp.bfloat16)
    low = (table - high.astype(np.float32)).astype(jnp.bfloat16)
    return np.stack([high, low])


def split(x):
    high = x.astype(jnp.bfloat16)
    return high, (x - high.astype(jnp.float32)).astype(jnp.bfloat16)


def dot(a, b, contract):
    return lax.dot_general(a, b, ((contract[0:1], contract[1:2]), ((), ())), preferred_element_type=jnp.float32)


def dot3(a, b, contract=(1, 0)):
    (ah, al), (bh, bl) = a, b
    n = ah.shape[0]
    both = dot(jnp.concatenate([ah, al], axis=0), bh, contract)
    return both[0:n] + (both[n:] + dot(ah, bl, contract))


TAPS = (float(wendland(np.float64(0.4))), float(wendland(np.float64(0.8))))


def shift(x, step, axis):
    return pltpu.roll(x, step % x.shape[axis], axis)


def smooth(x):
    for axis in (0, 1):
        near = shift(x, 1, axis) + shift(x, -1, axis)
        far = shift(x, 2, axis) + shift(x, -2, axis)
        x = x + (TAPS[0] * near + TAPS[1] * far)
    return x


def autoreg(x):
    beside = shift(x, 1, 0) + shift(x, -1, 0) + shift(x, 1, 1) + shift(x, -1, 1)
    return kappa_term * x - beside


def side_mask(total, tile, halo, at, last, dim):
    shape = (total, 1) if dim == 0 else (1, total)
    place = lax.broadcasted_iota(jnp.int32, shape, dim)
    after = (place < tile + halo) & (at < last)
    before = (place >= total - halo) & (at > 0)
    return ((place < tile) | after | before).astype(jnp.float32)


class Plan:
    def __init__(self, swath_shape, tile_shape, lat_total, lon_total):
        self.swath_rows, self.width = swath_shape
        self.rows, self.cols = tile_shape
        self.lat_total, self.lon_total = lat_total, lon_total
        self.col_frame = self.cols + 2 * HALO
        self.outer_rows = self.rows + 2 * RAW
        self.inner_rows = self.rows + 2 * INNER
        wide = [-(-(self.rows // s + 2 * (INNER // s + 2)) // 16) * 16 for s in SPACINGS[:COARSE]]
        self.node_rows = wide + [self.outer_rows]
        self.near_rows = [min(w, self.rows // s + 2 * NEAR) for w, s in zip(wide, SPACINGS)]
        self.near_rows.append(self.rows + 2 * NEAR)
        self.near_starts = np.cumsum([0] + self.near_rows[:COARSE]).tolist()
        self.node_cols = [-(-self.col_frame // (s * LANES)) * LANES for s in SPACINGS]
        self.row_starts = np.cumsum([0] + self.node_rows[:COARSE]).tolist()
        self.col_starts = np.cumsum([0] + self.node_cols[:COARSE]).tolist()
        col_cells = frame_index(self.col_frame, self.cols, HALO)
        outer = frame_index(self.outer_rows, self.rows, RAW)
        inner = frame_index(self.inner_rows, self.rows, INNER)
        col_tables, outer_rows, inner_rows, wide_rows = [], [], [], []
        self.part_nodes, place_all = [], []
        for k in range(COARSE):
            s = SPACINGS[k]
            tile = self.rows // s
            col_nodes = frame_index(self.node_cols[k], self.cols // s, HALO // s)
            row_nodes = frame_index(self.node_rows[k], tile, (self.node_rows[k] - tile) // 2)
            near_nodes = frame_index(self.near_rows[k], tile, (self.near_rows[k] - tile) // 2)
            col_tables.append(basis(col_cells, col_nodes, s))
            outer_rows.append(basis(outer, row_nodes, s))
            wide_rows.append(basis(inner, row_nodes, s))
            inner_rows.append(basis(inner, near_nodes, s))
            for away in range((RAW - 2 * s) // s, INNER // s + 2):
                self.part_nodes.append((s, away))
                at = self.row_starts[k]
                place_all.append((at + tile + away, at + self.node_rows[k] - 1 - away))
        nodes = self.row_starts[-1]
        joins = np.zeros((2 * PART_ROWS, nodes), np.float32)
        for n, (after_at, before_at) in enumerate(place_all):
            joins[n, after_at] = 1.0
            joins[PART_ROWS + n, before_at] = 1.0
        outer_all = np.concatenate([np.concatenate(outer_rows, axis=1), joins], axis=0)
        inner_all = np.concatenate(inner_rows, axis=1)
        wide_all = np.concatenate(wide_rows, axis=1)
        self.edge_nodes, sel = [], []
        for k in range(COARSE):
            first, total = self.rows // SPACINGS[k] - NEAR, self.node_rows[k]
            self.edge_nodes.append(total - first + NEAR)
            sel += [self.row_starts[k] + at for at in (*range(first, total), *range(NEAR))]
        self.edge_starts = np.cumsum([0] + self.edge_nodes).tolist()
        edge_rows = [*range(self.rows - EDGE, self.inner_rows), *range(EDGE)]
        row_tables = [
            outer_all[: self.rows].T,
            outer_all[self.rows :].T[sel],
            inner_all.T,
            wide_all,
            wide_all[edge_rows][:, sel],
            inner_all[: self.rows],
        ]
        lanes = -(-max(t.shape[1] for t in row_tables) // LANES) * LANES
        self.row_places, ends = [], [0, 0]
        for table in row_tables:
            side = int(ends[1] < ends[0])
            self.row_places.append((ends[side], table.shape[0], self.col_starts[-1] + side * lanes, table.shape[1]))
            ends[side] += table.shape[0]
        at = max(ends)
        col_all = np.concatenate(col_tables, axis=1)
        self.turned_start = self.col_starts[-1] + 2 * lanes
        whole = np.zeros((max(at, *col_all.shape), self.turned_start + self.col_frame), np.float32)
        whole[: self.col_frame, : self.col_starts[-1]] = col_all
        whole[: self.col_starts[-1], self.turned_start :] = col_all.T
        for (start, height, lane, width), table in zip(self.row_places, row_tables):
            whole[start : start + height, lane : lane + width] = table
        self.tables = halves(whole)
        tiles = self.col_frame // LANES
        self.sums = len(self.part_nodes)
        self.letter_rows = -(-(self.letter()[-1] + tiles * self.sums) // 8) * 8

    def pick(self, table_ref):
        col_tables, turned_tables, row_tables = [], [], []
        for k in range(COARSE):
            places = slice(self.col_starts[k], self.col_starts[k + 1])
            turned_tables.append(tuple(table_ref[half, places, self.turned_start :] for half in (0, 1)))
            col_tables.append(tuple(table_ref[half, 0 : self.col_frame, places] for half in (0, 1)))
        for start, height, lane, width in self.row_places:
            rows, lanes = slice(start, start + height), slice(lane, lane + width)
            row_tables.append(tuple(table_ref[half, rows, lanes] for half in (0, 1)))
        return col_tables, turned_tables, row_tables

    def masks(self, heights):
        lat, lon = lax.axis_index("lat"), lax.axis_index("lon")
        out = []
        for k, s in enumerate(SPACINGS):
            tile = self.rows // s
            rows = side_mask(heights[k], tile, (heights[k] - tile) // 2, lat, self.lat_total - 1, 0)
            cols = side_mask(self.node_cols[k], self.cols // s, HALO // s, lon, self.lon_total - 1, 1)
            out.append(rows * cols)
        return out

    def letter(self):
        tiles = self.col_frame // LANES
        weights = tiles * RAW
        corner = weights + (tiles - 1) * INNER
        return 0, weights, corner, corner + INNER // 2


def call(kernel, outs, limit, scratch=(), spaces=None):
    def run(*operands):
        in_spaces = spaces or [pltpu.VMEM] * len(operands)
        return pl.pallas_call(
            kernel,
            out_shape=[jax.ShapeDtypeStruct(shape, jnp.float32) for shape in outs],
            in_specs=[pl.BlockSpec(memory_space=space) for space in in_spaces],
            out_specs=[pl.BlockSpec(memory_space=pltpu.VMEM)] * len(outs),
            scratch_shapes=list(scratch),
            compiler_params=pltpu.CompilerParams(vmem_limit_bytes=int(limit * MIB)),
        )(*operands)

    return run


def window(plan, obs_ref, to):
    sr, width, cols = plan.swath_rows, plan.width, plan.cols
    base = pl.multiple_of(to * cols, LANES)
    lane = lax.broadcasted_iota(jnp.int32, (sr, LANES), 1)
    before = obs_ref[:, pl.ds(pl.multiple_of(jnp.maximum(base - LANES, 0), LANES), LANES)]
    after = obs_ref[:, pl.ds(pl.multiple_of(jnp.minimum(base + cols, width - LANES), LANES), LANES)]
    before = jnp.where(to > 0, before, 0.0)
    after = jnp.where(to < plan.lon_total - 1, after, 0.0)
    return obs_ref[:, pl.ds(base, cols)], jnp.where(lane < HALO, after, before)


def pack(plan, observed, gauged):
    sr, width, cols, rows, n = plan.swath_rows, plan.width, plan.cols, plan.rows, plan.lon_total
    tiles = plan.col_frame // LANES

    def kernel(obs_hbm, gauge_hbm, *rest):
        wt_ref, out_refs, (obs_ref, gauge_ref, sems) = rest[0], rest[1 : n + 1], rest[n + 1 :]
        copies = [
            pltpu.make_async_copy(obs_hbm, obs_ref, sems.at[0]),
            pltpu.make_async_copy(gauge_hbm, gauge_ref, sems.at[1]),
        ]
        for copy in copies:
            copy.start()
        at = lax.axis_index("lon")
        half_lane = lax.broadcasted_iota(jnp.int32, (rows // 2, LANES), 1)
        copies[0].wait()
        for k, ref in enumerate(out_refs):
            main, sides = window(plan, obs_ref, lax.rem(at + k, n))
            if k in (1, n - 1):
                for t in range(tiles - 1):
                    ref[t * sr : (t + 1) * sr, :] = main[:, t * LANES : (t + 1) * LANES]
                ref[(tiles - 1) * sr : tiles * sr, :] = sides
            else:
                ref[:, 0:cols] = main
                ref[:, cols:] = sides
        copies[1].wait()
        wt_ref[...] = data_weight * gauge_ref[...].astype(jnp.float32)
        for k in (1, n - 1):
            edge = wt_ref[:, cols - LANES :] if k == 1 else wt_ref[:, 0:LANES]
            kept = (half_lane >= HALO) if k == 1 else (half_lane < HALO)
            turned = pltpu.roll(edge[rows // 2 :], HALO, 1)
            out_refs[k][tiles * sr :, :] = jnp.where(kept, edge[0 : rows // 2], turned)

    side = (tiles * sr + rows // 2, LANES)
    outs = [(rows, cols)] + [side if k in (1, n - 1) else (sr, plan.col_frame) for k in range(n)]
    scratch = [
        pltpu.VMEM((sr, width), jnp.float32),
        pltpu.VMEM((rows, cols), jnp.int32),
        pltpu.SemaphoreType.DMA((2,)),
    ]
    return call(kernel, outs, 53.25, scratch, [pltpu.HBM] * 2)(observed, gauged)


def misfit(plan, own, right, left, far, weight, tables):
    sr, cols, rows, n = plan.swath_rows, plan.cols, plan.rows, plan.lon_total
    tiles = plan.col_frame // LANES

    def kernel(own_ref, right_ref, left_ref, wt_ref, table_ref, *rest):
        far_refs, (mis_ref, side_ref, near_ref, next_ref) = rest[: n - 3], rest[n - 3 :]
        at = lax.axis_index("lon")
        lane = lax.broadcasted_iota(jnp.int32, (rows, LANES), 1)

        def side(ref, present):
            packed = ref[tiles * sr :, :]
            both = jnp.concatenate([packed, pltpu.roll(packed, HALO, 1)], axis=0)
            return jnp.where(present, both, 0.0)

        side_ref[...] = jnp.where(lane < HALO, side(left_ref, at < n - 1), side(right_ref, at > 0))

        for k, ref in enumerate((own_ref, right_ref, *far_refs, left_ref)):
            here = pl.ds(pl.multiple_of(lax.rem(at + (n - k), n) * sr, sr), sr)
            if k in (1, n - 1):
                for t in range(tiles - 1):
                    lanes = slice(t * LANES, (t + 1) * LANES)
                    mis_ref[here, lanes] = wt_ref[here, lanes] * ref[t * sr : (t + 1) * sr, :]
                mis_ref[here, cols:] = side_ref[here, :] * ref[(tiles - 1) * sr : tiles * sr, :]
            else:
                mis_ref[here, 0:cols] = wt_ref[here, :] * ref[:, 0:cols]
                mis_ref[here, cols:] = side_ref[here, :] * ref[:, cols:]

        up = lax.axis_index("lat") % 2
        depth = HALO - RAW
        shape = (PART_ROWS, depth)
        line = lax.broadcasted_iota(jnp.int32, shape, 0)
        cell = lax.broadcasted_iota(jnp.int32, shape, 1)
        for ref, low in ((near_ref, 1 - up), (next_ref, up)):
            far = mis_ref[pl.ds(pl.multiple_of(RAW + low * (rows - HALO - RAW), 8), depth), :]
            table = jnp.zeros(shape, jnp.float32)
            distance = jnp.where(low == 1, HALO - 1 - cell, RAW + cell)
            for m, (s, away) in enumerate(plan.part_nodes):
                numerator = jnp.abs(2 * distance - 2 * s * away - (s - 1)).astype(jnp.float32)
                table = jnp.where(line == m, wendland(numerator / (5.0 * s), jnp) / math.sqrt(s), table)
            edge = pl.ds(pl.multiple_of(low * (rows - INNER), 8), INNER)
            sums = jnp.dot(table, far, precision=lax.Precision.HIGHEST, preferred_element_type=jnp.float32)
            near = mis_ref[pl.ds(pl.multiple_of(low * (rows - RAW), 8), RAW), :]
            raw, weights, corner, parts = plan.letter()
            for t in range(tiles):
                lanes = slice(t * LANES, (t + 1) * LANES)
                ref[raw + t * RAW : raw + (t + 1) * RAW, :] = near[:, lanes]
                if t < tiles - 1:
                    ref[weights + t * INNER : weights + (t + 1) * INNER, :] = wt_ref[edge, lanes]
                ref[parts + t * plan.sums : parts + (t + 1) * plan.sums, :] = sums[0 : plan.sums, lanes]
            beside = side_ref[edge, :]
            turned = pltpu.roll(beside[INNER // 2 :], HALO, 1)
            some = lax.broadcasted_iota(jnp.int32, (INNER // 2, LANES), 1)
            outer = (some < INNER) | (some >= LANES - INNER)
            ref[corner : corner + INNER // 2, :] = jnp.where(outer, beside[0 : INNER // 2], turned)
            ref[parts + tiles * plan.sums :, :] = jnp.zeros((plan.letter_rows - parts - tiles * plan.sums, LANES), jnp.float32)

    outs = [(rows, plan.col_frame), (rows, LANES)] + [(plan.letter_rows, LANES)] * 2
    return call(kernel, outs, 4)(own, right, left, weight, tables, *far)


def open_letter(plan, letter):
    tiles = plan.col_frame // LANES
    raw, weights, corner, parts = plan.letter()
    near = [letter[raw + t * RAW : raw + (t + 1) * RAW] for t in range(tiles)]
    sums = [letter[parts + t * plan.sums : parts + (t + 1) * plan.sums] for t in range(tiles)]
    sums = jnp.concatenate(sums, axis=1)
    sums = jnp.concatenate([sums, jnp.zeros((PART_ROWS - plan.sums, plan.col_frame), jnp.float32)], axis=0)
    rows = [letter[weights + t * INNER : weights + (t + 1) * INNER] for t in range(tiles - 1)]
    both = letter[corner : corner + INNER // 2]
    some = lax.broadcasted_iota(jnp.int32, (INNER // 2, LANES), 1)
    outer = (some < INNER) | (some >= LANES - INNER)
    beside = [jnp.where(outer, x, 0.0) for x in (both, pltpu.roll(both, HALO, 1))]
    rows.append(jnp.concatenate(beside, axis=0))
    return jnp.concatenate(near, axis=1), sums, jnp.concatenate(rows, axis=1)


def fetch(plan, after):
    def kernel(table_ref, after_ref, out_ref, sem):
        copy = pltpu.make_async_copy(table_ref, out_ref, sem)
        copy.start()
        copy.wait()

    table = jnp.asarray(plan.tables)
    return pl.pallas_call(
        kernel,
        out_shape=jax.ShapeDtypeStruct(table.shape, table.dtype),
        in_specs=[pl.BlockSpec(memory_space=pltpu.HBM), pl.BlockSpec(memory_space=pltpu.VMEM)],
        out_specs=pl.BlockSpec(memory_space=pltpu.VMEM),
        scratch_shapes=[pltpu.SemaphoreType.DMA],
        compiler_params=pltpu.CompilerParams(vmem_limit_bytes=MIB),
        cost_estimate=pl.CostEstimate(flops=0, bytes_accessed=2 * table.nbytes, transcendentals=0),
    )(table, after)


def inside(plan, mis, tables):
    rows, inner_rows = plan.rows, plan.inner_rows
    shapes = [(plan.node_rows[k], plan.node_cols[k]) for k in range(COARSE)] + [(rows + 2 * NEAR, plan.col_frame)]

    def kernel(mis_ref, table_ref, *out_refs):
        base_refs, (surface_ref, once_ref, twice_ref) = out_refs[:LEVELS], out_refs[LEVELS:]
        col_tables, turned_tables, (own_t, _, _, wide_s, _, _) = plan.pick(table_ref)
        masks = plan.masks([height for height, _ in shapes])
        mis = mis_ref[...]
        gathered = dot3(own_t, split(mis))
        starts = plan.row_starts
        base = [dot3(split(gathered[starts[k] : starts[k + 1]]), col_tables[k]) * masks[k] for k in range(COARSE)]
        blank = jnp.zeros((2 * NEAR, plan.col_frame), jnp.float32)
        base.append(smooth(jnp.concatenate([mis, blank], axis=0)) * masks[COARSE])
        for k in range(LEVELS):
            base_refs[k][...] = base[k]
        once = autoreg(base[COARSE]) * masks[COARSE]
        once_ref[...] = once
        twice_ref[...] = level_scales[COARSE] * autoreg(once)
        fine = smooth(base[COARSE])
        blank = jnp.zeros((inner_rows - rows - 2 * NEAR, plan.col_frame), jnp.float32)
        fine = jnp.concatenate([fine[0 : rows + NEAR], blank, fine[rows + NEAR :]], axis=0)
        spread = jnp.concatenate([dot3(split(base[k]), turned_tables[k]) for k in range(COARSE)], axis=0)
        surface_ref[...] = fine + dot3(wide_s, split(spread))

    outs = shapes + [(inner_rows, plan.col_frame)] + shapes[COARSE:] * 2
    *base, surface, once, twice = call(kernel, outs, 24)(mis, tables)
    return base, surface, once, twice


def operate(plan, mid, mid_surface, mid_once, mid_twice, wt, side, near, following, tables):
    rows, cols, sr, lon_total = plan.rows, plan.cols, plan.swath_rows, plan.lon_total
    n_dev = plan.lat_total * lon_total

    def kernel(mid_surface_ref, wt_ref, side_ref, near_ref, next_ref, table_ref, *out_refs):
        mid_refs, (once_ref, twice_ref), out_refs = out_refs[:LEVELS], out_refs[LEVELS : LEVELS + 2], out_refs[LEVELS + 2 :]
        base_refs, image_refs = out_refs[:LEVELS], out_refs[LEVELS : 2 * LEVELS]
        surface_refs, part_ref = out_refs[2 * LEVELS : -1], out_refs[-1]
        lat = lax.axis_index("lat")
        lon = lax.axis_index("lon")
        even = lat % 2 == 0
        col_tables, turned_tables, row_tables = plan.pick(table_ref)
        _, edge_t, inner_t, _, edge_s, tile_s = row_tables
        near_all, next_all = near_ref[...], next_ref[...]
        below = jnp.where(even, near_all, next_all)
        above = jnp.where(even, next_all, near_all)
        below, below_sums, below_wt = open_letter(plan, below)
        above, above_sums, above_wt = open_letter(plan, above)
        own_weight = jnp.concatenate([wt_ref[...], side_ref[...]], axis=1)
        weight = jnp.concatenate([own_weight, below_wt, above_wt], axis=0)

        masks = plan.masks(plan.node_rows)

        def collect(gathered, starts):
            return [dot3(split(gathered[starts[k] : starts[k + 1]]), col_tables[k]) for k in range(COARSE)]

        def spread(coeffs, width):
            turned = [tuple(part[:, 0:width] for part in table) for table in turned_tables]
            return split(jnp.concatenate([dot3(split(coeffs[k]), turned[k]) for k in range(COARSE)], axis=0))

        def cut(x, k, total):
            if x.shape[0] == total:
                return x
            side = (total - rows // SPACINGS[k]) // 2
            return jnp.concatenate([x[0 : total - side], x[x.shape[0] - side :]], axis=0)

        def blank(height, like):
            return jnp.zeros((height, like.shape[1]), jnp.float32)

        around = jnp.concatenate([below, above, below_sums, above_sums], axis=0)
        edge = collect(dot3(edge_t, split(around)), plan.edge_starts)
        base = []
        for k in range(COARSE):
            first = plan.edge_nodes[k] - NEAR
            tile = rows // SPACINGS[k]
            mask = jnp.concatenate([masks[k][tile - NEAR :], masks[k][0:NEAR]], axis=0)
            edge[k] = edge[k] * mask
            added = [edge[k][first:], edge[k][0:first]]
            if tile > 2 * NEAR:
                added.insert(1, blank(tile - 2 * NEAR, edge[k]))
            base.append(cut(mid_refs[k][...] + jnp.concatenate(added, axis=0), k, plan.near_rows[k]))
        strip = jnp.concatenate([blank(NEAR, below), below, above, blank(NEAR, above)], axis=0)
        fine_mask = masks[COARSE]
        strip_mask = jnp.concatenate([fine_mask[rows - NEAR :], fine_mask[0:NEAR]], axis=0)
        strip = smooth(strip) * strip_mask
        last = strip.shape[0] - NEAR
        added = [strip[last:], blank(rows - 2 * NEAR, strip), strip[0 : 2 * NEAR], strip[last - NEAR : last]]
        base.append(mid_refs[COARSE][...] + jnp.concatenate(added, axis=0))
        short, short_mask = [jnp.concatenate([x[0 : 3 * NEAR], x[last - 2 * NEAR :]], axis=0) for x in (strip, strip_mask)]
        once = autoreg(short) * short_mask

        def place(x):
            parts = [x[5 * NEAR :], blank(rows - 2 * NEAR, x), x[0 : 2 * NEAR], x[4 * NEAR : 5 * NEAR]]
            return jnp.concatenate(parts, axis=0)

        fine_once = once_ref[...] + place(once)
        fine_twice = twice_ref[...] + place(level_scales[COARSE] * autoreg(once))
        fine = smooth(strip)
        added = [fine[last:], blank(rows - 2 * NEAR, fine), fine[0 : NEAR + INNER], fine[last - INNER : last]]
        surface = mid_surface_ref[...] + jnp.concatenate(added, axis=0)
        coarse = dot3(edge_s, spread(edge, plan.col_frame))
        body_rows = coarse.shape[0] - EDGE
        added = [coarse[body_rows:], blank(rows - 2 * EDGE, coarse), coarse[0:body_rows]]
        surface = surface + jnp.concatenate(added, axis=0)
        masks = plan.masks(plan.near_rows)

        misfit_again = weight * surface
        image = collect(dot3(inner_t, split(misfit_again)), plan.near_starts)
        image.append(smooth(cut(misfit_again, COARSE, plan.near_rows[COARSE])))
        rough_base, rough_image = [], []
        for k in range(LEVELS):
            if k == COARSE:
                once, twice = fine_once, fine_twice
            else:
                once = autoreg(base[k]) * masks[k]
                twice = level_scales[k] * autoreg(once)
            rough_base.append(once)
            image[k] = (image[k] + twice) * masks[k]
            rough_image.append(autoreg(image[k]))
        second = dot3(tile_s, spread(image, cols)) + smooth(image[COARSE])[0:rows, 0:cols]

        own = [(slice(0, rows // s), slice(0, cols // s)) for s in SPACINGS]
        b = [base[k][own[k]] for k in range(LEVELS)]
        ab = [image[k][own[k]] for k in range(LEVELS)]
        rb = [rough_base[k][own[k]] for k in range(LEVELS)]
        rab = [rough_image[k][own[k]] for k in range(LEVELS)]
        sb, sab = surface[0:rows, 0:cols], second[:, 0:cols]
        w = weight[0:rows, 0:cols]

        for k in range(LEVELS):
            base_refs[k][...] = b[k]
            image_refs[k][...] = ab[k]
        surface_refs[0][0:rows, :] = sb
        surface_refs[0][rows:, :] = sab
        for k in range(1, lon_total):
            take = pl.ds(pl.multiple_of((lon ^ k) * sr, sr), sr)
            surface_refs[k][0:sr, :] = surface_refs[0][take, :]
            take = pl.ds(pl.multiple_of(rows + (lon ^ k) * sr, sr), sr)
            surface_refs[k][sr:, :] = surface_refs[0][take, :]

        def pieces(*arrays):
            height, width = arrays[0].shape
            for at in range(0, height, 8):
                for lane in range(0, width, LANES):
                    yield [x[at : at + 8, lane : min(lane + LANES, width)] for x in arrays]

        def gather(terms):
            totals = None
            for values in terms:
                totals = values if totals is None else [t + v for t, v in zip(totals, values)]
            short = LANES - totals[0].shape[1]
            if short:
                totals = [jnp.concatenate([t, jnp.zeros((8, short), jnp.float32)], axis=1) for t in totals]
            return totals

        def add_levels(per_level, scaled_from):
            out = list(per_level[0])
            for n in range(len(out)):
                scales = level_scales if n >= scaled_from else (1.0,) * LEVELS
                out[n] = sum(scales[k] * per_level[k][n] for k in range(LEVELS))
            return out

        first_sums = add_levels(
            [gather([x * x, y * y] for x, y in pieces(b[k], rb[k])) for k in range(LEVELS)], 1
        )
        a0 = first_sums[0]
        a1 = first_sums[1] + gather([v * f * f] for v, f in pieces(w, sb))[0]
        top = jnp.sum(a0, keepdims=True)
        bottom = jnp.sum(a1, keepdims=True)
        tau = jnp.where(bottom > 0.0, top / jnp.where(bottom > 0.0, bottom, 1.0), 0.0)

        def residual_terms(x, ax, y, ay):
            r, rr = x - tau * ax, y - tau * ay
            return [r * r, r * ax, ax * ax, rr * rr, rr * ay, ay * ay, rr * y, ay * y]

        def field_terms(v, f, af):
            r = f - tau * af
            vr, va = v * r, v * af
            return [vr * r, vr * af, va * af, vr * f, va * f]

        later_sums = add_levels(
            [gather(residual_terms(*p) for p in pieces(b[k], ab[k], rb[k], rab[k])) for k in range(LEVELS)], 3
        )
        fields = gather(field_terms(*p) for p in pieces(w, sb, sab))
        blocks = [a0, a1, *later_sums[:3], *(x + y for x, y in zip(later_sums[3:], fields))]
        lines = [jnp.sum(block, axis=0, keepdims=True) for block in blocks]
        lane = lax.broadcasted_iota(jnp.int32, (1, LANES), 1)
        lines.append(jnp.where(lane == 0, tau, 0.0))
        lines.append(jnp.zeros((16 - len(lines), LANES), jnp.float32))
        sums = jnp.sum(jnp.concatenate(lines, axis=0), axis=1, keepdims=True)
        place = lax.broadcasted_iota(jnp.int32, (16, LANES), 0)
        lanes = lax.broadcasted_iota(jnp.int32, (16, LANES), 1)
        line = jnp.sum(jnp.where(place == lanes, sums, 0.0), axis=0, keepdims=True)
        part_ref[...] = jnp.broadcast_to(line, (n_dev, LANES))

    level_shapes = [(rows // s, cols // s) for s in SPACINGS]
    outs = level_shapes * 2 + [(2 * rows, cols)] + [(2 * sr, cols)] * (lon_total - 1) + [(n_dev, LANES)]
    results = call(kernel, outs, 24)(mid_surface, wt, side, near, following, tables, *mid, mid_once, mid_twice)
    return results[:LEVELS], results[LEVELS : 2 * LEVELS], results[2 * LEVELS : -1], results[-1]


def finish(plan, parts, base, image, own_surface, far_surfaces):
    rows, cols, sr, lon_total = plan.rows, plan.cols, plan.swath_rows, plan.lon_total

    def kernel(part_ref, *rest):
        base_refs, image_refs = rest[:LEVELS], rest[LEVELS : 2 * LEVELS]
        own_ref, far_refs = rest[2 * LEVELS], rest[2 * LEVELS + 1 : 2 * LEVELS + lon_total]
        out_refs, swath_ref = rest[-LEVELS - 1 : -1], rest[-1]
        lon = lax.axis_index("lon")
        part = part_ref[...]
        lane = lax.broadcasted_iota(jnp.int32, part.shape, 1)

        def column(n):
            return jnp.sum(jnp.where(lane == n, part, 0.0), axis=1, keepdims=True)

        def total(values):
            return jnp.sum(values, axis=0, keepdims=True)

        a0, a1, p1, p2, p3, c1, c2, c3, c4, c5, tau = [column(n) for n in range(11)]
        sum0, sum1 = total(a0), total(a1)
        step = sum0 / sum1
        gap = tau - step
        norm = total(p1 + 2.0 * gap * p2 + gap * gap * p3)
        curv_res = total(c1 + 2.0 * gap * c2 + gap * gap * c3)
        curv_mix = total(c4 + gap * c5)
        ratio = norm / sum0
        curv = curv_res + 2.0 * ratio * curv_mix + ratio * ratio * sum1
        next_step = norm / curv
        alpha = step + next_step * (1.0 + ratio)
        beta = -next_step * step
        for k in range(LEVELS):
            out_refs[k][...] = alpha * base_refs[k][...] + beta * image_refs[k][...]
        take = pl.ds(pl.multiple_of(lon * sr, sr), sr)
        later = pl.ds(pl.multiple_of(rows + lon * sr, sr), sr)
        fields = [(own_ref[take, :], own_ref[later, :])]
        fields += [(ref[0:sr, :], ref[sr:, :]) for ref in far_refs]
        for k in range(lon_total):
            here = pl.ds(pl.multiple_of((lon ^ k) * cols, LANES), cols)
            swath_ref[:, here] = alpha * fields[k][0] + beta * fields[k][1]

    outs = [(rows // s, cols // s) for s in SPACINGS] + [(sr, plan.width)]
    return call(kernel, outs, 8)(parts, *base, *image, own_surface, *far_surfaces)


def turn(x, axis, total, k):
    return lax.ppermute(x, axis, [(i, (i + k) % total) for i in range(total)])


def flip(x, axis, total, k):
    return lax.ppermute(x, axis, [(i, i ^ k) for i in range(total)])


def odd_swap(x, axis, total):
    pairs = [(i, i + 1) for i in range(1, total - 1, 2)]
    return lax.ppermute(x, axis, pairs + [(j, i) for i, j in pairs])


def body(observed, gauged):
    lat_total, lon_total = lax.axis_size("lat"), lax.axis_size("lon")
    plan = Plan(observed.shape, gauged.shape, lat_total, lon_total)
    weight, own, *windows = pack(plan, observed, gauged)
    tables = fetch(plan, own)
    right, *far, left = [turn(x, "lon", lon_total, k) for k, x in enumerate(windows, 1)]
    mis, side, near, following = misfit(plan, own, right, left, far, weight, tables)
    mid, mid_surface, mid_once, mid_twice = inside(plan, mis, tables)
    near = flip(near, "lat", lat_total, 1)
    following = odd_swap(following, "lat", lat_total)
    base, image, surfaces, parts = operate(plan, mid, mid_surface, mid_once, mid_twice, weight, side, near, following, tables)
    far_surfaces = [flip(x, "lon", lon_total, k) for k, x in enumerate(surfaces[1:], 1)]
    parts = lax.all_to_all(parts, ("lat", "lon"), split_axis=0, concat_axis=0, tiled=True)
    return tuple(finish(plan, parts, base, image, surfaces[0], far_surfaces))


def solution(mesh):
    return jax.shard_map(
        body,
        mesh=mesh,
        in_specs=(P(("lat", "lon"), None), P("lat", "lon")),
        out_specs=(
            P("lat", "lon"),
            P("lat", "lon"),
            P("lat", "lon"),
            P("lat", "lon"),
            P(("lat", "lon"), None),
        ),
        check_vma=False,
    )
```

```python
import math

import jax
import jax.numpy as jnp
import numpy as np
from jax import lax
from jax.experimental import pallas as pl
from jax.experimental.pallas import tpu as pltpu
from jax.sharding import PartitionSpec as P

LEVELS = 4
SPACINGS = tuple(2 ** (LEVELS - 1 - k) for k in range(LEVELS))
COARSE = LEVELS - 1
HALO = 64
INNER = 32
RAW = 40
PART_ROWS = 8
EDGE = 32
NEAR = 8
LANES = 128

data_weight = 2.0
kappa_term = 5.0
level_scales = (0.02, 0.03, 0.05, 0.08)

MIB = 1024 * 1024


def wendland(distance, of=np):
    remain = of.maximum(1.0 - distance, 0.0)
    cube = remain * remain * remain
    return cube * cube * (35.0 * distance * distance + 18.0 * distance + 3.0) / 3.0


def frame_index(total, tile, halo):
    place = np.arange(total)
    index = np.where(place < tile + halo, place, place - total)
    return index, (place < tile + halo) | (place >= total - halo)


def basis(cells, nodes, spacing):
    (cell, cell_ok), (node, node_ok) = cells, nodes
    numerator = np.abs(2 * cell[:, None] - 2 * spacing * node[None, :] - (spacing - 1))
    table = wendland(numerator / (5.0 * spacing)) / math.sqrt(spacing)
    return np.where(cell_ok[:, None] & node_ok[None, :], table, 0.0).astype(np.float32)


def halves(table):
    high = table.astype(jnp.bfloat16)
    low = (table - high.astype(np.float32)).astype(jnp.bfloat16)
    return np.stack([high, low])


def split(x):
    high = x.astype(jnp.bfloat16)
    return high, (x - high.astype(jnp.float32)).astype(jnp.bfloat16)


def dot(a, b, contract):
    return lax.dot_general(a, b, ((contract[0:1], contract[1:2]), ((), ())), preferred_element_type=jnp.float32)


def dot3(a, b, contract=(1, 0)):
    (ah, al), (bh, bl) = a, b
    n = ah.shape[0]
    both = dot(jnp.concatenate([ah, al], axis=0), bh, contract)
    return both[0:n] + (both[n:] + dot(ah, bl, contract))


TAPS = (float(wendland(np.float64(0.4))), float(wendland(np.float64(0.8))))


def shift(x, step, axis):
    return pltpu.roll(x, step % x.shape[axis], axis)


def smooth(x):
    for axis in (0, 1):
        near = shift(x, 1, axis) + shift(x, -1, axis)
        far = shift(x, 2, axis) + shift(x, -2, axis)
        x = x + (TAPS[0] * near + TAPS[1] * far)
    return x


def autoreg(x):
    beside = shift(x, 1, 0) + shift(x, -1, 0) + shift(x, 1, 1) + shift(x, -1, 1)
    return kappa_term * x - beside


def side_mask(total, tile, halo, at, last, dim):
    shape = (total, 1) if dim == 0 else (1, total)
    place = lax.broadcasted_iota(jnp.int32, shape, dim)
    after = (place < tile + halo) & (at < last)
    before = (place >= total - halo) & (at > 0)
    return ((place < tile) | after | before).astype(jnp.float32)


class Plan:
    def __init__(self, swath_shape, tile_shape, lat_total, lon_total):
        self.swath_rows, self.width = swath_shape
        self.rows, self.cols = tile_shape
        self.lat_total, self.lon_total = lat_total, lon_total
        self.col_frame = self.cols + 2 * HALO
        self.outer_rows = self.rows + 2 * RAW
        self.inner_rows = self.rows + 2 * INNER
        wide = [-(-(self.rows // s + 2 * (INNER // s + 2)) // 16) * 16 for s in SPACINGS[:COARSE]]
        self.node_rows = wide + [self.outer_rows]
        self.near_rows = [min(w, self.rows // s + 2 * NEAR) for w, s in zip(wide, SPACINGS)]
        self.near_rows.append(self.rows + 2 * NEAR)
        self.near_starts = np.cumsum([0] + self.near_rows[:COARSE]).tolist()
        self.node_cols = [-(-self.col_frame // (s * LANES)) * LANES for s in SPACINGS]
        self.row_starts = np.cumsum([0] + self.node_rows[:COARSE]).tolist()
        self.col_starts = np.cumsum([0] + self.node_cols[:COARSE]).tolist()
        col_cells = frame_index(self.col_frame, self.cols, HALO)
        outer = frame_index(self.outer_rows, self.rows, RAW)
        inner = frame_index(self.inner_rows, self.rows, INNER)
        col_tables, outer_rows, inner_rows, wide_rows = [], [], [], []
        self.part_nodes, place_all = [], []
        for k in range(COARSE):
            s = SPACINGS[k]
            tile = self.rows // s
            col_nodes = frame_index(self.node_cols[k], self.cols // s, HALO // s)
            row_nodes = frame_index(self.node_rows[k], tile, (self.node_rows[k] - tile) // 2)
            near_nodes = frame_index(self.near_rows[k], tile, (self.near_rows[k] - tile) // 2)
            col_tables.append(basis(col_cells, col_nodes, s))
            outer_rows.append(basis(outer, row_nodes, s))
            wide_rows.append(basis(inner, row_nodes, s))
            inner_rows.append(basis(inner, near_nodes, s))
            for away in range((RAW - 2 * s) // s, INNER // s + 2):
                self.part_nodes.append((s, away))
                at = self.row_starts[k]
                place_all.append((at + tile + away, at + self.node_rows[k] - 1 - away))
        nodes = self.row_starts[-1]
        joins = np.zeros((2 * PART_ROWS, nodes), np.float32)
        for n, (after_at, before_at) in enumerate(place_all):
            joins[n, after_at] = 1.0
            joins[PART_ROWS + n, before_at] = 1.0
        outer_all = np.concatenate([np.concatenate(outer_rows, axis=1), joins], axis=0)
        inner_all = np.concatenate(inner_rows, axis=1)
        wide_all = np.concatenate(wide_rows, axis=1)
        self.edge_nodes, sel = [], []
        for k in range(COARSE):
            first, total = self.rows // SPACINGS[k] - NEAR, self.node_rows[k]
            self.edge_nodes.append(total - first + NEAR)
            sel += [self.row_starts[k] + at for at in (*range(first, total), *range(NEAR))]
        self.edge_starts = np.cumsum([0] + self.edge_nodes).tolist()
        edge_rows = [*range(self.rows - EDGE, self.inner_rows), *range(EDGE)]
        row_tables = [
            outer_all[: self.rows].T,
            outer_all[self.rows :].T[sel],
            inner_all.T,
            wide_all,
            wide_all[edge_rows][:, sel],
            inner_all[: self.rows],
        ]
        lanes = -(-max(t.shape[1] for t in row_tables) // LANES) * LANES
        self.row_places, ends = [], [0, 0]
        for table in row_tables:
            side = int(ends[1] < ends[0])
            self.row_places.append((ends[side], table.shape[0], self.col_starts[-1] + side * lanes, table.shape[1]))
            ends[side] += table.shape[0]
        at = max(ends)
        col_all = np.concatenate(col_tables, axis=1)
        self.turned_start = self.col_starts[-1] + 2 * lanes
        whole = np.zeros((max(at, *col_all.shape), self.turned_start + self.col_frame), np.float32)
        whole[: self.col_frame, : self.col_starts[-1]] = col_all
        whole[: self.col_starts[-1], self.turned_start :] = col_all.T
        for (start, height, lane, width), table in zip(self.row_places, row_tables):
            whole[start : start + height, lane : lane + width] = table
        self.tables = halves(whole)
        tiles = self.col_frame // LANES
        self.sums = len(self.part_nodes)
        self.letter_rows = -(-(self.letter()[-1] + tiles * self.sums) // 8) * 8

    def pick(self, table_ref):
        col_tables, turned_tables, row_tables = [], [], []
        for k in range(COARSE):
            places = slice(self.col_starts[k], self.col_starts[k + 1])
            turned_tables.append(tuple(table_ref[half, places, self.turned_start :] for half in (0, 1)))
            col_tables.append(tuple(table_ref[half, 0 : self.col_frame, places] for half in (0, 1)))
        for start, height, lane, width in self.row_places:
            rows, lanes = slice(start, start + height), slice(lane, lane + width)
            row_tables.append(tuple(table_ref[half, rows, lanes] for half in (0, 1)))
        return col_tables, turned_tables, row_tables

    def masks(self, heights):
        lat, lon = lax.axis_index("lat"), lax.axis_index("lon")
        out = []
        for k, s in enumerate(SPACINGS):
            tile = self.rows // s
            rows = side_mask(heights[k], tile, (heights[k] - tile) // 2, lat, self.lat_total - 1, 0)
            cols = side_mask(self.node_cols[k], self.cols // s, HALO // s, lon, self.lon_total - 1, 1)
            out.append(rows * cols)
        return out

    def letter(self):
        tiles = self.col_frame // LANES
        weights = tiles * RAW
        corner = weights + (tiles - 1) * INNER
        return 0, weights, corner, corner + INNER // 2


def call(kernel, outs, limit, scratch=(), spaces=None):
    def run(*operands):
        in_spaces = spaces or [pltpu.VMEM] * len(operands)
        return pl.pallas_call(
            kernel,
            out_shape=[jax.ShapeDtypeStruct(shape, jnp.float32) for shape in outs],
            in_specs=[pl.BlockSpec(memory_space=space) for space in in_spaces],
            out_specs=[pl.BlockSpec(memory_space=pltpu.VMEM)] * len(outs),
            scratch_shapes=list(scratch),
            compiler_params=pltpu.CompilerParams(vmem_limit_bytes=int(limit * MIB)),
        )(*operands)

    return run


def window(plan, obs_ref, to):
    sr, width, cols = plan.swath_rows, plan.width, plan.cols
    base = pl.multiple_of(to * cols, LANES)
    lane = lax.broadcasted_iota(jnp.int32, (sr, LANES), 1)
    before = obs_ref[:, pl.ds(pl.multiple_of(jnp.maximum(base - LANES, 0), LANES), LANES)]
    after = obs_ref[:, pl.ds(pl.multiple_of(jnp.minimum(base + cols, width - LANES), LANES), LANES)]
    before = jnp.where(to > 0, before, 0.0)
    after = jnp.where(to < plan.lon_total - 1, after, 0.0)
    return obs_ref[:, pl.ds(base, cols)], jnp.where(lane < HALO, after, before)


def pack(plan, observed, gauged):
    sr, width, cols, rows, n = plan.swath_rows, plan.width, plan.cols, plan.rows, plan.lon_total
    tiles = plan.col_frame // LANES

    def kernel(obs_hbm, gauge_hbm, *rest):
        wt_ref, out_refs, (obs_ref, gauge_ref, sems) = rest[0], rest[1 : n + 1], rest[n + 1 :]
        copies = [
            pltpu.make_async_copy(obs_hbm, obs_ref, sems.at[0]),
            pltpu.make_async_copy(gauge_hbm, gauge_ref, sems.at[1]),
        ]
        for copy in copies:
            copy.start()
        at = lax.axis_index("lon")
        half_lane = lax.broadcasted_iota(jnp.int32, (rows // 2, LANES), 1)
        copies[0].wait()
        for k, ref in enumerate(out_refs):
            main, sides = window(plan, obs_ref, lax.rem(at + k, n))
            if k in (1, n - 1):
                for t in range(tiles - 1):
                    ref[t * sr : (t + 1) * sr, :] = main[:, t * LANES : (t + 1) * LANES]
                ref[(tiles - 1) * sr : tiles * sr, :] = sides
            else:
                ref[:, 0:cols] = main
                ref[:, cols:] = sides
        copies[1].wait()
        wt_ref[...] = data_weight * gauge_ref[...].astype(jnp.float32)
        for k in (1, n - 1):
            edge = wt_ref[:, cols - LANES :] if k == 1 else wt_ref[:, 0:LANES]
            kept = (half_lane >= HALO) if k == 1 else (half_lane < HALO)
            turned = pltpu.roll(edge[rows // 2 :], HALO, 1)
            out_refs[k][tiles * sr :, :] = jnp.where(kept, edge[0 : rows // 2], turned)

    side = (tiles * sr + rows // 2, LANES)
    outs = [(rows, cols)] + [side if k in (1, n - 1) else (sr, plan.col_frame) for k in range(n)]
    scratch = [
        pltpu.VMEM((sr, width), jnp.float32),
        pltpu.VMEM((rows, cols), jnp.int32),
        pltpu.SemaphoreType.DMA((2,)),
    ]
    return call(kernel, outs, 53.25, scratch, [pltpu.HBM] * 2)(observed, gauged)


def misfit(plan, own, right, left, far, weight, tables):
    sr, cols, rows, n = plan.swath_rows, plan.cols, plan.rows, plan.lon_total
    tiles = plan.col_frame // LANES

    def kernel(own_ref, right_ref, left_ref, wt_ref, table_ref, *rest):
        far_refs, (mis_ref, side_ref, near_ref, next_ref) = rest[: n - 3], rest[n - 3 :]
        at = lax.axis_index("lon")
        lane = lax.broadcasted_iota(jnp.int32, (rows, LANES), 1)

        def side(ref, present):
            packed = ref[tiles * sr :, :]
            both = jnp.concatenate([packed, pltpu.roll(packed, HALO, 1)], axis=0)
            return jnp.where(present, both, 0.0)

        side_ref[...] = jnp.where(lane < HALO, side(left_ref, at < n - 1), side(right_ref, at > 0))

        for k, ref in enumerate((own_ref, right_ref, *far_refs, left_ref)):
            here = pl.ds(pl.multiple_of(lax.rem(at + (n - k), n) * sr, sr), sr)
            if k in (1, n - 1):
                for t in range(tiles - 1):
                    lanes = slice(t * LANES, (t + 1) * LANES)
                    mis_ref[here, lanes] = wt_ref[here, lanes] * ref[t * sr : (t + 1) * sr, :]
                mis_ref[here, cols:] = side_ref[here, :] * ref[(tiles - 1) * sr : tiles * sr, :]
            else:
                mis_ref[here, 0:cols] = wt_ref[here, :] * ref[:, 0:cols]
                mis_ref[here, cols:] = side_ref[here, :] * ref[:, cols:]

        up = lax.axis_index("lat") % 2
        depth = HALO - RAW
        shape = (PART_ROWS, depth)
        line = lax.broadcasted_iota(jnp.int32, shape, 0)
        cell = lax.broadcasted_iota(jnp.int32, shape, 1)
        for ref, low in ((near_ref, 1 - up), (next_ref, up)):
            far = mis_ref[pl.ds(pl.multiple_of(RAW + low * (rows - HALO - RAW), 8), depth), :]
            table = jnp.zeros(shape, jnp.float32)
            distance = jnp.where(low == 1, HALO - 1 - cell, RAW + cell)
            for m, (s, away) in enumerate(plan.part_nodes):
                numerator = jnp.abs(2 * distance - 2 * s * away - (s - 1)).astype(jnp.float32)
                table = jnp.where(line == m, wendland(numerator / (5.0 * s), jnp) / math.sqrt(s), table)
            edge = pl.ds(pl.multiple_of(low * (rows - INNER), 8), INNER)
            sums = jnp.dot(table, far, precision=lax.Precision.HIGHEST, preferred_element_type=jnp.float32)
            near = mis_ref[pl.ds(pl.multiple_of(low * (rows - RAW), 8), RAW), :]
            raw, weights, corner, parts = plan.letter()
            for t in range(tiles):
                lanes = slice(t * LANES, (t + 1) * LANES)
                ref[raw + t * RAW : raw + (t + 1) * RAW, :] = near[:, lanes]
                if t < tiles - 1:
                    ref[weights + t * INNER : weights + (t + 1) * INNER, :] = wt_ref[edge, lanes]
                ref[parts + t * plan.sums : parts + (t + 1) * plan.sums, :] = sums[0 : plan.sums, lanes]
            beside = side_ref[edge, :]
            turned = pltpu.roll(beside[INNER // 2 :], HALO, 1)
            some = lax.broadcasted_iota(jnp.int32, (INNER // 2, LANES), 1)
            outer = (some < INNER) | (some >= LANES - INNER)
            ref[corner : corner + INNER // 2, :] = jnp.where(outer, beside[0 : INNER // 2], turned)
            ref[parts + tiles * plan.sums :, :] = jnp.zeros((plan.letter_rows - parts - tiles * plan.sums, LANES), jnp.float32)

    outs = [(rows, plan.col_frame), (rows, LANES)] + [(plan.letter_rows, LANES)] * 2
    return call(kernel, outs, 4)(own, right, left, weight, tables, *far)


def open_letter(plan, letter):
    tiles = plan.col_frame // LANES
    raw, weights, corner, parts = plan.letter()
    near = [letter[raw + t * RAW : raw + (t + 1) * RAW] for t in range(tiles)]
    sums = [letter[parts + t * plan.sums : parts + (t + 1) * plan.sums] for t in range(tiles)]
    sums = jnp.concatenate(sums, axis=1)
    sums = jnp.concatenate([sums, jnp.zeros((PART_ROWS - plan.sums, plan.col_frame), jnp.float32)], axis=0)
    rows = [letter[weights + t * INNER : weights + (t + 1) * INNER] for t in range(tiles - 1)]
    both = letter[corner : corner + INNER // 2]
    some = lax.broadcasted_iota(jnp.int32, (INNER // 2, LANES), 1)
    outer = (some < INNER) | (some >= LANES - INNER)
    beside = [jnp.where(outer, x, 0.0) for x in (both, pltpu.roll(both, HALO, 1))]
    rows.append(jnp.concatenate(beside, axis=0))
    return jnp.concatenate(near, axis=1), sums, jnp.concatenate(rows, axis=1)


def fetch(plan, after):
    def kernel(table_ref, after_ref, out_ref, sem):
        copy = pltpu.make_async_copy(table_ref, out_ref, sem)
        copy.start()
        copy.wait()

    table = jnp.asarray(plan.tables)
    return pl.pallas_call(
        kernel,
        out_shape=jax.ShapeDtypeStruct(table.shape, table.dtype),
        in_specs=[pl.BlockSpec(memory_space=pltpu.HBM), pl.BlockSpec(memory_space=pltpu.VMEM)],
        out_specs=pl.BlockSpec(memory_space=pltpu.VMEM),
        scratch_shapes=[pltpu.SemaphoreType.DMA],
        compiler_params=pltpu.CompilerParams(vmem_limit_bytes=MIB),
        cost_estimate=pl.CostEstimate(flops=0, bytes_accessed=2 * table.nbytes, transcendentals=0),
    )(table, after)


def inside(plan, mis, wt, side, tables):
    rows, inner_rows = plan.rows, plan.inner_rows
    shapes = [(plan.node_rows[k], plan.node_cols[k]) for k in range(COARSE)] + [(rows + 2 * NEAR, plan.col_frame)]

    def kernel(mis_ref, wt_ref, side_ref, table_ref, *out_refs):
        base_refs, (surface_ref, once_ref, twice_ref, again_ref) = out_refs[:LEVELS], out_refs[LEVELS:]
        col_tables, turned_tables, (own_t, _, _, wide_s, _, _) = plan.pick(table_ref)
        masks = plan.masks([height for height, _ in shapes])
        mis = mis_ref[...]
        gathered = dot3(own_t, split(mis))
        starts = plan.row_starts
        base = [dot3(split(gathered[starts[k] : starts[k + 1]]), col_tables[k]) * masks[k] for k in range(COARSE)]
        blank = jnp.zeros((2 * NEAR, plan.col_frame), jnp.float32)
        base.append(smooth(jnp.concatenate([mis, blank], axis=0)) * masks[COARSE])
        for k in range(LEVELS):
            base_refs[k][...] = base[k]
        once = autoreg(base[COARSE]) * masks[COARSE]
        once_ref[...] = once
        twice_ref[...] = level_scales[COARSE] * autoreg(once)
        fine = smooth(base[COARSE])
        blank = jnp.zeros((inner_rows - rows - 2 * NEAR, plan.col_frame), jnp.float32)
        fine = jnp.concatenate([fine[0 : rows + NEAR], blank, fine[rows + NEAR :]], axis=0)
        spread = jnp.concatenate([dot3(split(base[k]), turned_tables[k]) for k in range(COARSE)], axis=0)
        surface = fine + dot3(wide_s, split(spread))
        surface_ref[...] = surface
        again = jnp.concatenate([wt_ref[...], side_ref[...]], axis=1) * surface[0:rows]
        blank = jnp.zeros((2 * NEAR, plan.col_frame), jnp.float32)
        again_ref[...] = smooth(jnp.concatenate([again, blank], axis=0))

    outs = shapes + [(inner_rows, plan.col_frame)] + shapes[COARSE:] * 3
    *base, surface, once, twice, again = call(kernel, outs, 24)(mis, wt, side, tables)
    return base, surface, once, twice, again


def operate(plan, mid, mid_surface, mid_once, mid_twice, mid_again, wt, side, near, following, tables):
    rows, cols, sr, lon_total = plan.rows, plan.cols, plan.swath_rows, plan.lon_total
    n_dev = plan.lat_total * lon_total

    def kernel(mid_surface_ref, wt_ref, side_ref, near_ref, next_ref, table_ref, *out_refs):
        mid_refs, (once_ref, twice_ref, again_ref) = out_refs[:LEVELS], out_refs[LEVELS : LEVELS + 3]
        out_refs = out_refs[LEVELS + 3 :]
        base_refs, image_refs = out_refs[:LEVELS], out_refs[LEVELS : 2 * LEVELS]
        surface_refs, part_ref = out_refs[2 * LEVELS : -1], out_refs[-1]
        lat = lax.axis_index("lat")
        lon = lax.axis_index("lon")
        even = lat % 2 == 0
        col_tables, turned_tables, row_tables = plan.pick(table_ref)
        _, edge_t, inner_t, _, edge_s, tile_s = row_tables
        near_all, next_all = near_ref[...], next_ref[...]
        below = jnp.where(even, near_all, next_all)
        above = jnp.where(even, next_all, near_all)
        below, below_sums, below_wt = open_letter(plan, below)
        above, above_sums, above_wt = open_letter(plan, above)
        own_weight = jnp.concatenate([wt_ref[...], side_ref[...]], axis=1)
        weight = jnp.concatenate([own_weight, below_wt, above_wt], axis=0)

        masks = plan.masks(plan.node_rows)

        def collect(gathered, starts):
            return [dot3(split(gathered[starts[k] : starts[k + 1]]), col_tables[k]) for k in range(COARSE)]

        def spread(coeffs, width):
            turned = [tuple(part[:, 0:width] for part in table) for table in turned_tables]
            return split(jnp.concatenate([dot3(split(coeffs[k]), turned[k]) for k in range(COARSE)], axis=0))

        def cut(x, k, total):
            if x.shape[0] == total:
                return x
            side = (total - rows // SPACINGS[k]) // 2
            return jnp.concatenate([x[0 : total - side], x[x.shape[0] - side :]], axis=0)

        def blank(height, like):
            return jnp.zeros((height, like.shape[1]), jnp.float32)

        around = jnp.concatenate([below, above, below_sums, above_sums], axis=0)
        edge = collect(dot3(edge_t, split(around)), plan.edge_starts)
        base = []
        for k in range(COARSE):
            first = plan.edge_nodes[k] - NEAR
            tile = rows // SPACINGS[k]
            mask = jnp.concatenate([masks[k][tile - NEAR :], masks[k][0:NEAR]], axis=0)
            edge[k] = edge[k] * mask
            added = [edge[k][first:], edge[k][0:first]]
            if tile > 2 * NEAR:
                added.insert(1, blank(tile - 2 * NEAR, edge[k]))
            base.append(cut(mid_refs[k][...] + jnp.concatenate(added, axis=0), k, plan.near_rows[k]))
        strip = jnp.concatenate([blank(NEAR, below), below, above, blank(NEAR, above)], axis=0)
        fine_mask = masks[COARSE]
        strip_mask = jnp.concatenate([fine_mask[rows - NEAR :], fine_mask[0:NEAR]], axis=0)
        strip = smooth(strip) * strip_mask
        last = strip.shape[0] - NEAR
        added = [strip[last:], blank(rows - 2 * NEAR, strip), strip[0 : 2 * NEAR], strip[last - NEAR : last]]
        base.append(mid_refs[COARSE][...] + jnp.concatenate(added, axis=0))
        short, short_mask = [jnp.concatenate([x[0 : 3 * NEAR], x[last - 2 * NEAR :]], axis=0) for x in (strip, strip_mask)]
        once = autoreg(short) * short_mask

        def place(x):
            parts = [x[5 * NEAR :], blank(rows - 2 * NEAR, x), x[0 : 2 * NEAR], x[4 * NEAR : 5 * NEAR]]
            return jnp.concatenate(parts, axis=0)

        fine_once = once_ref[...] + place(once)
        fine_twice = twice_ref[...] + place(level_scales[COARSE] * autoreg(once))
        fine = smooth(strip)
        added = [fine[last:], blank(rows - 2 * NEAR, fine), fine[0 : NEAR + INNER], fine[last - INNER : last]]
        extra = jnp.concatenate(added, axis=0)
        coarse = dot3(edge_s, spread(edge, plan.col_frame))
        body_rows = coarse.shape[0] - EDGE
        added = [coarse[body_rows:], blank(rows - 2 * EDGE, coarse), coarse[0:body_rows]]
        extra = extra + jnp.concatenate(added, axis=0)
        surface = mid_surface_ref[...] + extra
        masks = plan.masks(plan.near_rows)

        misfit_again = weight * surface
        image = collect(dot3(inner_t, split(misfit_again)), plan.near_starts)
        reach = EDGE + NEAR
        changed = [
            weight[rows - reach : rows] * extra[rows - reach : rows],
            misfit_again[rows : rows + NEAR],
            misfit_again[plan.inner_rows - NEAR :],
            weight[0:reach] * extra[0:reach],
        ]
        changed = smooth(jnp.concatenate(changed, axis=0))
        first = reach + 2 * NEAR
        changed = [changed[first:], blank(rows - 2 * reach, changed), changed[0:first]]
        image.append(again_ref[...] + jnp.concatenate(changed, axis=0))
        rough_base, rough_image = [], []
        for k in range(LEVELS):
            if k == COARSE:
                once, twice = fine_once, fine_twice
            else:
                once = autoreg(base[k]) * masks[k]
                twice = level_scales[k] * autoreg(once)
            rough_base.append(once)
            image[k] = (image[k] + twice) * masks[k]
            rough_image.append(autoreg(image[k]))
        second = dot3(tile_s, spread(image, cols)) + smooth(image[COARSE])[0:rows, 0:cols]

        own = [(slice(0, rows // s), slice(0, cols // s)) for s in SPACINGS]
        b = [base[k][own[k]] for k in range(LEVELS)]
        ab = [image[k][own[k]] for k in range(LEVELS)]
        rb = [rough_base[k][own[k]] for k in range(LEVELS)]
        rab = [rough_image[k][own[k]] for k in range(LEVELS)]
        sb, sab = surface[0:rows, 0:cols], second[:, 0:cols]
        w = weight[0:rows, 0:cols]

        for k in range(LEVELS):
            base_refs[k][...] = b[k]
            image_refs[k][...] = ab[k]
        surface_refs[0][0:rows, :] = sb
        surface_refs[0][rows:, :] = sab
        for k in range(1, lon_total):
            take = pl.ds(pl.multiple_of((lon ^ k) * sr, sr), sr)
            surface_refs[k][0:sr, :] = surface_refs[0][take, :]
            take = pl.ds(pl.multiple_of(rows + (lon ^ k) * sr, sr), sr)
            surface_refs[k][sr:, :] = surface_refs[0][take, :]

        def pieces(*arrays):
            height, width = arrays[0].shape
            for at in range(0, height, 8):
                for lane in range(0, width, LANES):
                    yield [x[at : at + 8, lane : min(lane + LANES, width)] for x in arrays]

        def gather(terms):
            totals = None
            for values in terms:
                totals = values if totals is None else [t + v for t, v in zip(totals, values)]
            short = LANES - totals[0].shape[1]
            if short:
                totals = [jnp.concatenate([t, jnp.zeros((8, short), jnp.float32)], axis=1) for t in totals]
            return totals

        def add_levels(per_level, scaled_from):
            out = list(per_level[0])
            for n in range(len(out)):
                scales = level_scales if n >= scaled_from else (1.0,) * LEVELS
                out[n] = sum(scales[k] * per_level[k][n] for k in range(LEVELS))
            return out

        first_sums = add_levels(
            [gather([x * x, y * y] for x, y in pieces(b[k], rb[k])) for k in range(LEVELS)], 1
        )
        a0 = first_sums[0]
        a1 = first_sums[1] + gather([v * f * f] for v, f in pieces(w, sb))[0]
        top = jnp.sum(a0, keepdims=True)
        bottom = jnp.sum(a1, keepdims=True)
        tau = jnp.where(bottom > 0.0, top / jnp.where(bottom > 0.0, bottom, 1.0), 0.0)

        def residual_terms(x, ax, y, ay):
            r, rr = x - tau * ax, y - tau * ay
            return [r * r, r * ax, ax * ax, rr * rr, rr * ay, ay * ay, rr * y, ay * y]

        def field_terms(v, f, af):
            r = f - tau * af
            vr, va = v * r, v * af
            return [vr * r, vr * af, va * af, vr * f, va * f]

        later_sums = add_levels(
            [gather(residual_terms(*p) for p in pieces(b[k], ab[k], rb[k], rab[k])) for k in range(LEVELS)], 3
        )
        fields = gather(field_terms(*p) for p in pieces(w, sb, sab))
        blocks = [a0, a1, *later_sums[:3], *(x + y for x, y in zip(later_sums[3:], fields))]
        lines = [jnp.sum(block, axis=0, keepdims=True) for block in blocks]
        lane = lax.broadcasted_iota(jnp.int32, (1, LANES), 1)
        lines.append(jnp.where(lane == 0, tau, 0.0))
        lines.append(jnp.zeros((16 - len(lines), LANES), jnp.float32))
        sums = jnp.sum(jnp.concatenate(lines, axis=0), axis=1, keepdims=True)
        place = lax.broadcasted_iota(jnp.int32, (16, LANES), 0)
        lanes = lax.broadcasted_iota(jnp.int32, (16, LANES), 1)
        line = jnp.sum(jnp.where(place == lanes, sums, 0.0), axis=0, keepdims=True)
        part_ref[...] = jnp.broadcast_to(line, (n_dev, LANES))

    level_shapes = [(rows // s, cols // s) for s in SPACINGS]
    outs = level_shapes * 2 + [(2 * rows, cols)] + [(2 * sr, cols)] * (lon_total - 1) + [(n_dev, LANES)]
    results = call(kernel, outs, 24)(mid_surface, wt, side, near, following, tables, *mid, mid_once, mid_twice, mid_again)
    return results[:LEVELS], results[LEVELS : 2 * LEVELS], results[2 * LEVELS : -1], results[-1]


def finish(plan, parts, base, image, own_surface, far_surfaces):
    rows, cols, sr, lon_total = plan.rows, plan.cols, plan.swath_rows, plan.lon_total

    def kernel(part_ref, *rest):
        base_refs, image_refs = rest[:LEVELS], rest[LEVELS : 2 * LEVELS]
        own_ref, far_refs = rest[2 * LEVELS], rest[2 * LEVELS + 1 : 2 * LEVELS + lon_total]
        out_refs, swath_ref = rest[-LEVELS - 1 : -1], rest[-1]
        lon = lax.axis_index("lon")
        part = part_ref[...]
        lane = lax.broadcasted_iota(jnp.int32, part.shape, 1)

        def column(n):
            return jnp.sum(jnp.where(lane == n, part, 0.0), axis=1, keepdims=True)

        def total(values):
            return jnp.sum(values, axis=0, keepdims=True)

        a0, a1, p1, p2, p3, c1, c2, c3, c4, c5, tau = [column(n) for n in range(11)]
        sum0, sum1 = total(a0), total(a1)
        step = sum0 / sum1
        gap = tau - step
        norm = total(p1 + 2.0 * gap * p2 + gap * gap * p3)
        curv_res = total(c1 + 2.0 * gap * c2 + gap * gap * c3)
        curv_mix = total(c4 + gap * c5)
        ratio = norm / sum0
        curv = curv_res + 2.0 * ratio * curv_mix + ratio * ratio * sum1
        next_step = norm / curv
        alpha = step + next_step * (1.0 + ratio)
        beta = -next_step * step
        for k in range(LEVELS):
            out_refs[k][...] = alpha * base_refs[k][...] + beta * image_refs[k][...]
        take = pl.ds(pl.multiple_of(lon * sr, sr), sr)
        later = pl.ds(pl.multiple_of(rows + lon * sr, sr), sr)
        fields = [(own_ref[take, :], own_ref[later, :])]
        fields += [(ref[0:sr, :], ref[sr:, :]) for ref in far_refs]
        for k in range(lon_total):
            here = pl.ds(pl.multiple_of((lon ^ k) * cols, LANES), cols)
            swath_ref[:, here] = alpha * fields[k][0] + beta * fields[k][1]

    outs = [(rows // s, cols // s) for s in SPACINGS] + [(sr, plan.width)]
    return call(kernel, outs, 8)(parts, *base, *image, own_surface, *far_surfaces)


def turn(x, axis, total, k):
    return lax.ppermute(x, axis, [(i, (i + k) % total) for i in range(total)])


def flip(x, axis, total, k):
    return lax.ppermute(x, axis, [(i, i ^ k) for i in range(total)])


def odd_swap(x, axis, total):
    pairs = [(i, i + 1) for i in range(1, total - 1, 2)]
    return lax.ppermute(x, axis, pairs + [(j, i) for i, j in pairs])


def body(observed, gauged):
    lat_total, lon_total = lax.axis_size("lat"), lax.axis_size("lon")
    plan = Plan(observed.shape, gauged.shape, lat_total, lon_total)
    weight, own, *windows = pack(plan, observed, gauged)
    tables = fetch(plan, own)
    right, *far, left = [turn(x, "lon", lon_total, k) for k, x in enumerate(windows, 1)]
    mis, side, near, following = misfit(plan, own, right, left, far, weight, tables)
    mid, mid_surface, mid_once, mid_twice, mid_again = inside(plan, mis, weight, side, tables)
    near = flip(near, "lat", lat_total, 1)
    following = odd_swap(following, "lat", lat_total)
    base, image, surfaces, parts = operate(
        plan, mid, mid_surface, mid_once, mid_twice, mid_again, weight, side, near, following, tables
    )
    far_surfaces = [flip(x, "lon", lon_total, k) for k, x in enumerate(surfaces[1:], 1)]
    parts = lax.all_to_all(parts, ("lat", "lon"), split_axis=0, concat_axis=0, tiled=True)
    return tuple(finish(plan, parts, base, image, surfaces[0], far_surfaces))


def solution(mesh):
    return jax.shard_map(
        body,
        mesh=mesh,
        in_specs=(P(("lat", "lon"), None), P("lat", "lon")),
        out_specs=(
            P("lat", "lon"),
            P("lat", "lon"),
            P("lat", "lon"),
            P("lat", "lon"),
            P(("lat", "lon"), None),
        ),
        check_vma=False,
    )
```

```python
import math

import jax
import jax.numpy as jnp
import numpy as np
from jax import lax
from jax.experimental import pallas as pl
from jax.experimental.pallas import tpu as pltpu
from jax.sharding import PartitionSpec as P

LEVELS = 4
SPACINGS = tuple(2 ** (LEVELS - 1 - k) for k in range(LEVELS))
COARSE = LEVELS - 1
HALO = 64
INNER = 32
RAW = 40
PART_ROWS = 8
EDGE = 32
NEAR = 8
LANES = 128

data_weight = 2.0
kappa_term = 5.0
level_scales = (0.02, 0.03, 0.05, 0.08)

MIB = 1024 * 1024


def wendland(distance, of=np):
    remain = of.maximum(1.0 - distance, 0.0)
    cube = remain * remain * remain
    return cube * cube * (35.0 * distance * distance + 18.0 * distance + 3.0) / 3.0


def frame_index(total, tile, halo):
    place = np.arange(total)
    index = np.where(place < tile + halo, place, place - total)
    return index, (place < tile + halo) | (place >= total - halo)


def basis(cells, nodes, spacing):
    (cell, cell_ok), (node, node_ok) = cells, nodes
    numerator = np.abs(2 * cell[:, None] - 2 * spacing * node[None, :] - (spacing - 1))
    table = wendland(numerator / (5.0 * spacing)) / math.sqrt(spacing)
    return np.where(cell_ok[:, None] & node_ok[None, :], table, 0.0).astype(np.float32)


def halves(table):
    high = table.astype(jnp.bfloat16)
    low = (table - high.astype(np.float32)).astype(jnp.bfloat16)
    return np.stack([high, low])


def split(x):
    high = x.astype(jnp.bfloat16)
    return high, (x - high.astype(jnp.float32)).astype(jnp.bfloat16)


def dot(a, b, contract):
    return lax.dot_general(a, b, ((contract[0:1], contract[1:2]), ((), ())), preferred_element_type=jnp.float32)


def dot3(a, b, contract=(1, 0)):
    (ah, al), (bh, bl) = a, b
    n = ah.shape[0]
    both = dot(jnp.concatenate([ah, al], axis=0), bh, contract)
    return both[0:n] + (both[n:] + dot(ah, bl, contract))


TAPS = (float(wendland(np.float64(0.4))), float(wendland(np.float64(0.8))))


def shift(x, step, axis):
    return pltpu.roll(x, step % x.shape[axis], axis)


def smooth(x):
    for axis in (0, 1):
        near = shift(x, 1, axis) + shift(x, -1, axis)
        far = shift(x, 2, axis) + shift(x, -2, axis)
        x = x + (TAPS[0] * near + TAPS[1] * far)
    return x


def autoreg(x):
    beside = shift(x, 1, 0) + shift(x, -1, 0) + shift(x, 1, 1) + shift(x, -1, 1)
    return kappa_term * x - beside


def side_mask(total, tile, halo, at, last, dim):
    shape = (total, 1) if dim == 0 else (1, total)
    place = lax.broadcasted_iota(jnp.int32, shape, dim)
    after = (place < tile + halo) & (at < last)
    before = (place >= total - halo) & (at > 0)
    return ((place < tile) | after | before).astype(jnp.float32)


class Plan:
    def __init__(self, swath_shape, tile_shape, lat_total, lon_total):
        self.swath_rows, self.width = swath_shape
        self.rows, self.cols = tile_shape
        self.lat_total, self.lon_total = lat_total, lon_total
        self.col_frame = self.cols + 2 * HALO
        self.outer_rows = self.rows + 2 * RAW
        self.inner_rows = self.rows + 2 * INNER
        wide = [-(-(self.rows // s + 2 * (INNER // s + 2)) // 16) * 16 for s in SPACINGS[:COARSE]]
        self.node_rows = wide + [self.outer_rows]
        self.near_rows = [min(w, self.rows // s + 2 * NEAR) for w, s in zip(wide, SPACINGS)]
        self.near_rows.append(self.rows + 2 * NEAR)
        self.near_starts = np.cumsum([0] + self.near_rows[:COARSE]).tolist()
        self.node_cols = [-(-self.col_frame // (s * LANES)) * LANES for s in SPACINGS]
        self.row_starts = np.cumsum([0] + self.node_rows[:COARSE]).tolist()
        self.col_starts = np.cumsum([0] + self.node_cols[:COARSE]).tolist()
        col_cells = frame_index(self.col_frame, self.cols, HALO)
        outer = frame_index(self.outer_rows, self.rows, RAW)
        inner = frame_index(self.inner_rows, self.rows, INNER)
        col_tables, outer_rows, inner_rows, wide_rows = [], [], [], []
        self.part_nodes, place_all = [], []
        for k in range(COARSE):
            s = SPACINGS[k]
            tile = self.rows // s
            col_nodes = frame_index(self.node_cols[k], self.cols // s, HALO // s)
            row_nodes = frame_index(self.node_rows[k], tile, (self.node_rows[k] - tile) // 2)
            near_nodes = frame_index(self.near_rows[k], tile, (self.near_rows[k] - tile) // 2)
            col_tables.append(basis(col_cells, col_nodes, s))
            outer_rows.append(basis(outer, row_nodes, s))
            wide_rows.append(basis(inner, row_nodes, s))
            inner_rows.append(basis(inner, near_nodes, s))
            for away in range((RAW - 2 * s) // s, INNER // s + 2):
                self.part_nodes.append((s, away))
                at = self.row_starts[k]
                place_all.append((at + tile + away, at + self.node_rows[k] - 1 - away))
        nodes = self.row_starts[-1]
        joins = np.zeros((2 * PART_ROWS, nodes), np.float32)
        for n, (after_at, before_at) in enumerate(place_all):
            joins[n, after_at] = 1.0
            joins[PART_ROWS + n, before_at] = 1.0
        outer_all = np.concatenate([np.concatenate(outer_rows, axis=1), joins], axis=0)
        inner_all = np.concatenate(inner_rows, axis=1)
        wide_all = np.concatenate(wide_rows, axis=1)
        self.edge_nodes, sel = [], []
        for k in range(COARSE):
            first, total = self.rows // SPACINGS[k] - NEAR, self.node_rows[k]
            self.edge_nodes.append(total - first + NEAR)
            sel += [self.row_starts[k] + at for at in (*range(first, total), *range(NEAR))]
        self.edge_starts = np.cumsum([0] + self.edge_nodes).tolist()
        edge_rows = [*range(self.rows - EDGE, self.inner_rows), *range(EDGE)]
        row_tables = [
            outer_all[: self.rows].T,
            outer_all[self.rows :].T[sel],
            inner_all.T,
            wide_all,
            wide_all[edge_rows][:, sel],
            inner_all[: self.rows],
        ]
        lanes = -(-max(t.shape[1] for t in row_tables) // LANES) * LANES
        self.row_places, ends = [], [0, 0]
        for table in row_tables:
            side = int(ends[1] < ends[0])
            self.row_places.append((ends[side], table.shape[0], self.col_starts[-1] + side * lanes, table.shape[1]))
            ends[side] += table.shape[0]
        at = max(ends)
        col_all = np.concatenate(col_tables, axis=1)
        self.turned_start = self.col_starts[-1] + 2 * lanes
        whole = np.zeros((max(at, *col_all.shape), self.turned_start + self.col_frame), np.float32)
        whole[: self.col_frame, : self.col_starts[-1]] = col_all
        whole[: self.col_starts[-1], self.turned_start :] = col_all.T
        for (start, height, lane, width), table in zip(self.row_places, row_tables):
            whole[start : start + height, lane : lane + width] = table
        self.tables = halves(whole)
        tiles = self.col_frame // LANES
        self.sums = len(self.part_nodes)
        self.letter_rows = -(-(self.letter()[-1] + tiles * self.sums) // 8) * 8

    def pick(self, table_ref):
        col_tables, turned_tables, row_tables = [], [], []
        for k in range(COARSE):
            places = slice(self.col_starts[k], self.col_starts[k + 1])
            turned_tables.append(tuple(table_ref[half, places, self.turned_start :] for half in (0, 1)))
            col_tables.append(tuple(table_ref[half, 0 : self.col_frame, places] for half in (0, 1)))
        for start, height, lane, width in self.row_places:
            rows, lanes = slice(start, start + height), slice(lane, lane + width)
            row_tables.append(tuple(table_ref[half, rows, lanes] for half in (0, 1)))
        return col_tables, turned_tables, row_tables

    def masks(self, heights):
        lat, lon = lax.axis_index("lat"), lax.axis_index("lon")
        out = []
        for k, s in enumerate(SPACINGS):
            tile = self.rows // s
            rows = side_mask(heights[k], tile, (heights[k] - tile) // 2, lat, self.lat_total - 1, 0)
            cols = side_mask(self.node_cols[k], self.cols // s, HALO // s, lon, self.lon_total - 1, 1)
            out.append(rows * cols)
        return out

    def letter(self):
        tiles = self.col_frame // LANES
        weights = tiles * RAW
        corner = weights + (tiles - 1) * INNER
        return 0, weights, corner, corner + INNER // 2


def call(kernel, outs, limit, scratch=(), spaces=None):
    def run(*operands):
        in_spaces = spaces or [pltpu.VMEM] * len(operands)
        return pl.pallas_call(
            kernel,
            out_shape=[jax.ShapeDtypeStruct(shape, jnp.float32) for shape in outs],
            in_specs=[pl.BlockSpec(memory_space=space) for space in in_spaces],
            out_specs=[pl.BlockSpec(memory_space=pltpu.VMEM)] * len(outs),
            scratch_shapes=list(scratch),
            compiler_params=pltpu.CompilerParams(vmem_limit_bytes=int(limit * MIB)),
        )(*operands)

    return run


def window(plan, obs_ref, to):
    sr, width, cols = plan.swath_rows, plan.width, plan.cols
    base = pl.multiple_of(to * cols, LANES)
    lane = lax.broadcasted_iota(jnp.int32, (sr, LANES), 1)
    before = obs_ref[:, pl.ds(pl.multiple_of(jnp.maximum(base - LANES, 0), LANES), LANES)]
    after = obs_ref[:, pl.ds(pl.multiple_of(jnp.minimum(base + cols, width - LANES), LANES), LANES)]
    before = jnp.where(to > 0, before, 0.0)
    after = jnp.where(to < plan.lon_total - 1, after, 0.0)
    return obs_ref[:, pl.ds(base, cols)], jnp.where(lane < HALO, after, before)


def pack(plan, observed, gauged):
    sr, width, cols, rows, n = plan.swath_rows, plan.width, plan.cols, plan.rows, plan.lon_total
    tiles = plan.col_frame // LANES

    def kernel(obs_hbm, gauge_hbm, *rest):
        wt_ref, out_refs, (obs_ref, gauge_ref, sems) = rest[0], rest[1 : n + 1], rest[n + 1 :]
        copies = [
            pltpu.make_async_copy(obs_hbm, obs_ref, sems.at[0]),
            pltpu.make_async_copy(gauge_hbm, gauge_ref, sems.at[1]),
        ]
        for copy in copies:
            copy.start()
        at = lax.axis_index("lon")
        half_lane = lax.broadcasted_iota(jnp.int32, (rows // 2, LANES), 1)
        copies[0].wait()
        for k, ref in enumerate(out_refs):
            main, sides = window(plan, obs_ref, lax.rem(at + k, n))
            if k in (1, n - 1):
                for t in range(tiles - 1):
                    ref[t * sr : (t + 1) * sr, :] = main[:, t * LANES : (t + 1) * LANES]
                ref[(tiles - 1) * sr : tiles * sr, :] = sides
            else:
                ref[:, 0:cols] = main
                ref[:, cols:] = sides
        copies[1].wait()
        wt_ref[...] = data_weight * gauge_ref[...].astype(jnp.float32)
        for k in (1, n - 1):
            edge = wt_ref[:, cols - LANES :] if k == 1 else wt_ref[:, 0:LANES]
            kept = (half_lane >= HALO) if k == 1 else (half_lane < HALO)
            turned = pltpu.roll(edge[rows // 2 :], HALO, 1)
            out_refs[k][tiles * sr :, :] = jnp.where(kept, edge[0 : rows // 2], turned)

    side = (tiles * sr + rows // 2, LANES)
    outs = [(rows, cols)] + [side if k in (1, n - 1) else (sr, plan.col_frame) for k in range(n)]
    scratch = [
        pltpu.VMEM((sr, width), jnp.float32),
        pltpu.VMEM((rows, cols), jnp.int32),
        pltpu.SemaphoreType.DMA((2,)),
    ]
    return call(kernel, outs, 53.25, scratch, [pltpu.HBM] * 2)(observed, gauged)


def misfit(plan, own, right, left, far, weight, tables):
    sr, cols, rows, n = plan.swath_rows, plan.cols, plan.rows, plan.lon_total
    tiles = plan.col_frame // LANES

    def kernel(own_ref, right_ref, left_ref, wt_ref, table_ref, *rest):
        far_refs, (mis_ref, side_ref, near_ref, next_ref) = rest[: n - 3], rest[n - 3 :]
        at = lax.axis_index("lon")
        lane = lax.broadcasted_iota(jnp.int32, (rows, LANES), 1)

        def side(ref, present):
            packed = ref[tiles * sr :, :]
            both = jnp.concatenate([packed, pltpu.roll(packed, HALO, 1)], axis=0)
            return jnp.where(present, both, 0.0)

        side_ref[...] = jnp.where(lane < HALO, side(left_ref, at < n - 1), side(right_ref, at > 0))

        for k, ref in enumerate((own_ref, right_ref, *far_refs, left_ref)):
            here = pl.ds(pl.multiple_of(lax.rem(at + (n - k), n) * sr, sr), sr)
            if k in (1, n - 1):
                for t in range(tiles - 1):
                    lanes = slice(t * LANES, (t + 1) * LANES)
                    mis_ref[here, lanes] = wt_ref[here, lanes] * ref[t * sr : (t + 1) * sr, :]
                mis_ref[here, cols:] = side_ref[here, :] * ref[(tiles - 1) * sr : tiles * sr, :]
            else:
                mis_ref[here, 0:cols] = wt_ref[here, :] * ref[:, 0:cols]
                mis_ref[here, cols:] = side_ref[here, :] * ref[:, cols:]

        up = lax.axis_index("lat") % 2
        depth = HALO - RAW
        shape = (PART_ROWS, depth)
        line = lax.broadcasted_iota(jnp.int32, shape, 0)
        cell = lax.broadcasted_iota(jnp.int32, shape, 1)
        for ref, low in ((near_ref, 1 - up), (next_ref, up)):
            far = mis_ref[pl.ds(pl.multiple_of(RAW + low * (rows - HALO - RAW), 8), depth), :]
            table = jnp.zeros(shape, jnp.float32)
            distance = jnp.where(low == 1, HALO - 1 - cell, RAW + cell)
            for m, (s, away) in enumerate(plan.part_nodes):
                numerator = jnp.abs(2 * distance - 2 * s * away - (s - 1)).astype(jnp.float32)
                table = jnp.where(line == m, wendland(numerator / (5.0 * s), jnp) / math.sqrt(s), table)
            edge = pl.ds(pl.multiple_of(low * (rows - INNER), 8), INNER)
            sums = jnp.dot(table, far, precision=lax.Precision.HIGHEST, preferred_element_type=jnp.float32)
            near = mis_ref[pl.ds(pl.multiple_of(low * (rows - RAW), 8), RAW), :]
            raw, weights, corner, parts = plan.letter()
            for t in range(tiles):
                lanes = slice(t * LANES, (t + 1) * LANES)
                ref[raw + t * RAW : raw + (t + 1) * RAW, :] = near[:, lanes]
                if t < tiles - 1:
                    ref[weights + t * INNER : weights + (t + 1) * INNER, :] = wt_ref[edge, lanes]
                ref[parts + t * plan.sums : parts + (t + 1) * plan.sums, :] = sums[0 : plan.sums, lanes]
            beside = side_ref[edge, :]
            turned = pltpu.roll(beside[INNER // 2 :], HALO, 1)
            some = lax.broadcasted_iota(jnp.int32, (INNER // 2, LANES), 1)
            outer = (some < INNER) | (some >= LANES - INNER)
            ref[corner : corner + INNER // 2, :] = jnp.where(outer, beside[0 : INNER // 2], turned)
            ref[parts + tiles * plan.sums :, :] = jnp.zeros((plan.letter_rows - parts - tiles * plan.sums, LANES), jnp.float32)

    outs = [(rows, plan.col_frame), (rows, LANES)] + [(plan.letter_rows, LANES)] * 2
    return call(kernel, outs, 4)(own, right, left, weight, tables, *far)


def open_letter(plan, letter):
    tiles = plan.col_frame // LANES
    raw, weights, corner, parts = plan.letter()
    near = [letter[raw + t * RAW : raw + (t + 1) * RAW] for t in range(tiles)]
    sums = [letter[parts + t * plan.sums : parts + (t + 1) * plan.sums] for t in range(tiles)]
    sums = jnp.concatenate(sums, axis=1)
    sums = jnp.concatenate([sums, jnp.zeros((PART_ROWS - plan.sums, plan.col_frame), jnp.float32)], axis=0)
    rows = [letter[weights + t * INNER : weights + (t + 1) * INNER] for t in range(tiles - 1)]
    both = letter[corner : corner + INNER // 2]
    some = lax.broadcasted_iota(jnp.int32, (INNER // 2, LANES), 1)
    outer = (some < INNER) | (some >= LANES - INNER)
    beside = [jnp.where(outer, x, 0.0) for x in (both, pltpu.roll(both, HALO, 1))]
    rows.append(jnp.concatenate(beside, axis=0))
    return jnp.concatenate(near, axis=1), sums, jnp.concatenate(rows, axis=1)


def fetch(plan, after):
    def kernel(table_ref, after_ref, out_ref, sem):
        copy = pltpu.make_async_copy(table_ref, out_ref, sem)
        copy.start()
        copy.wait()

    table = jnp.asarray(plan.tables)
    return pl.pallas_call(
        kernel,
        out_shape=jax.ShapeDtypeStruct(table.shape, table.dtype),
        in_specs=[pl.BlockSpec(memory_space=pltpu.HBM), pl.BlockSpec(memory_space=pltpu.VMEM)],
        out_specs=pl.BlockSpec(memory_space=pltpu.VMEM),
        scratch_shapes=[pltpu.SemaphoreType.DMA],
        compiler_params=pltpu.CompilerParams(vmem_limit_bytes=MIB),
        cost_estimate=pl.CostEstimate(flops=0, bytes_accessed=2 * table.nbytes, transcendentals=0),
    )(table, after)


def inside(plan, mis, wt, side, tables):
    rows, inner_rows = plan.rows, plan.inner_rows
    shapes = [(plan.node_rows[k], plan.node_cols[k]) for k in range(COARSE)] + [(rows + 2 * NEAR, plan.col_frame)]

    def kernel(mis_ref, wt_ref, side_ref, table_ref, *out_refs):
        base_refs, (surface_ref, once_ref, image_ref, rough_ref, second_ref) = out_refs[:LEVELS], out_refs[LEVELS:]
        col_tables, turned_tables, (own_t, _, _, wide_s, _, _) = plan.pick(table_ref)
        masks = plan.masks([height for height, _ in shapes])
        mis = mis_ref[...]
        gathered = dot3(own_t, split(mis))
        starts = plan.row_starts
        base = [dot3(split(gathered[starts[k] : starts[k + 1]]), col_tables[k]) * masks[k] for k in range(COARSE)]
        blank = jnp.zeros((2 * NEAR, plan.col_frame), jnp.float32)
        base.append(smooth(jnp.concatenate([mis, blank], axis=0)) * masks[COARSE])
        for k in range(LEVELS):
            base_refs[k][...] = base[k]
        once = autoreg(base[COARSE]) * masks[COARSE]
        once_ref[...] = once
        twice = level_scales[COARSE] * autoreg(once)
        fine = smooth(base[COARSE])
        blank = jnp.zeros((inner_rows - rows - 2 * NEAR, plan.col_frame), jnp.float32)
        fine = jnp.concatenate([fine[0 : rows + NEAR], blank, fine[rows + NEAR :]], axis=0)
        spread = jnp.concatenate([dot3(split(base[k]), turned_tables[k]) for k in range(COARSE)], axis=0)
        surface = fine + dot3(wide_s, split(spread))
        surface_ref[...] = surface
        again = jnp.concatenate([wt_ref[...], side_ref[...]], axis=1) * surface[0:rows]
        blank = jnp.zeros((2 * NEAR, plan.col_frame), jnp.float32)
        image = (smooth(jnp.concatenate([again, blank], axis=0)) + twice) * masks[COARSE]
        image_ref[...] = image
        rough_ref[...] = autoreg(image)
        second_ref[...] = smooth(image)[0:rows, 0 : plan.cols]

    outs = shapes + [(inner_rows, plan.col_frame)] + shapes[COARSE:] * 3 + [(rows, plan.cols)]
    results = call(kernel, outs, 24)(mis, wt, side, tables)
    return results[:LEVELS], results[LEVELS], results[LEVELS + 1 :]


def operate(plan, mid, mid_surface, mid_fine, wt, side, near, following, tables):
    rows, cols, sr, lon_total = plan.rows, plan.cols, plan.swath_rows, plan.lon_total
    n_dev = plan.lat_total * lon_total

    def kernel(mid_surface_ref, wt_ref, side_ref, near_ref, next_ref, table_ref, *out_refs):
        mid_refs, (once_ref, fine_ref, rough_ref, second_ref) = out_refs[:LEVELS], out_refs[LEVELS : LEVELS + 4]
        out_refs = out_refs[LEVELS + 4 :]
        base_refs, image_refs = out_refs[:LEVELS], out_refs[LEVELS : 2 * LEVELS]
        surface_refs, part_ref = out_refs[2 * LEVELS : -1], out_refs[-1]
        lat = lax.axis_index("lat")
        lon = lax.axis_index("lon")
        even = lat % 2 == 0
        col_tables, turned_tables, row_tables = plan.pick(table_ref)
        _, edge_t, inner_t, _, edge_s, tile_s = row_tables
        near_all, next_all = near_ref[...], next_ref[...]
        below = jnp.where(even, near_all, next_all)
        above = jnp.where(even, next_all, near_all)
        below, below_sums, below_wt = open_letter(plan, below)
        above, above_sums, above_wt = open_letter(plan, above)
        own_weight = jnp.concatenate([wt_ref[...], side_ref[...]], axis=1)
        weight = jnp.concatenate([own_weight, below_wt, above_wt], axis=0)

        masks = plan.masks(plan.node_rows)

        def collect(gathered, starts):
            return [dot3(split(gathered[starts[k] : starts[k + 1]]), col_tables[k]) for k in range(COARSE)]

        def spread(coeffs, width):
            turned = [tuple(part[:, 0:width] for part in table) for table in turned_tables]
            return split(jnp.concatenate([dot3(split(coeffs[k]), turned[k]) for k in range(COARSE)], axis=0))

        def cut(x, k, total):
            if x.shape[0] == total:
                return x
            side = (total - rows // SPACINGS[k]) // 2
            return jnp.concatenate([x[0 : total - side], x[x.shape[0] - side :]], axis=0)

        def blank(height, like):
            return jnp.zeros((height, like.shape[1]), jnp.float32)

        around = jnp.concatenate([below, above, below_sums, above_sums], axis=0)
        edge = collect(dot3(edge_t, split(around)), plan.edge_starts)
        base = []
        for k in range(COARSE):
            first = plan.edge_nodes[k] - NEAR
            tile = rows // SPACINGS[k]
            mask = jnp.concatenate([masks[k][tile - NEAR :], masks[k][0:NEAR]], axis=0)
            edge[k] = edge[k] * mask
            added = [edge[k][first:], edge[k][0:first]]
            if tile > 2 * NEAR:
                added.insert(1, blank(tile - 2 * NEAR, edge[k]))
            base.append(cut(mid_refs[k][...] + jnp.concatenate(added, axis=0), k, plan.near_rows[k]))
        strip = jnp.concatenate([blank(NEAR, below), below, above, blank(NEAR, above)], axis=0)
        fine_mask = masks[COARSE]
        strip_mask = jnp.concatenate([fine_mask[rows - NEAR :], fine_mask[0:NEAR]], axis=0)
        strip = smooth(strip) * strip_mask
        last = strip.shape[0] - NEAR
        added = [strip[last:], blank(rows - 2 * NEAR, strip), strip[0 : 2 * NEAR], strip[last - NEAR : last]]
        base.append(mid_refs[COARSE][...] + jnp.concatenate(added, axis=0))
        short, short_mask = [jnp.concatenate([x[0 : 3 * NEAR], x[last - 2 * NEAR :]], axis=0) for x in (strip, strip_mask)]
        once = autoreg(short) * short_mask

        def place(x):
            parts = [x[5 * NEAR :], blank(rows - 2 * NEAR, x), x[0 : 2 * NEAR], x[4 * NEAR : 5 * NEAR]]
            return jnp.concatenate(parts, axis=0)

        fine_once = once_ref[...] + place(once)
        twice_edge = level_scales[COARSE] * autoreg(once)
        fine = smooth(strip)
        added = [fine[last:], blank(rows - 2 * NEAR, fine), fine[0 : NEAR + INNER], fine[last - INNER : last]]
        extra = jnp.concatenate(added, axis=0)
        coarse = dot3(edge_s, spread(edge, plan.col_frame))
        body_rows = coarse.shape[0] - EDGE
        added = [coarse[body_rows:], blank(rows - 2 * EDGE, coarse), coarse[0:body_rows]]
        extra = extra + jnp.concatenate(added, axis=0)
        surface = mid_surface_ref[...] + extra
        masks = plan.masks(plan.near_rows)

        misfit_again = weight * surface
        image = collect(dot3(inner_t, split(misfit_again)), plan.near_starts)
        reach = EDGE + NEAR
        changed = [
            weight[rows - reach : rows] * extra[rows - reach : rows],
            misfit_again[rows : rows + NEAR],
            misfit_again[plan.inner_rows - NEAR :],
            weight[0:reach] * extra[0:reach],
        ]
        changed = smooth(jnp.concatenate(changed, axis=0))
        ends = [blank(EDGE, below), twice_edge[0 : 2 * NEAR], twice_edge[4 * NEAR :], blank(EDGE, below)]
        fine_mask = masks[COARSE]
        changed_mask = jnp.concatenate([fine_mask[rows - reach :], fine_mask[0:reach]], axis=0)
        changed = (changed + jnp.concatenate(ends, axis=0)) * changed_mask

        def spot(x):
            first = reach + 2 * NEAR
            return jnp.concatenate([x[first:], blank(rows - 2 * reach, x), x[0:first]], axis=0)

        rough_base, rough_image = [], []
        for k in range(COARSE):
            once = autoreg(base[k]) * masks[k]
            rough_base.append(once)
            image[k] = (image[k] + level_scales[k] * autoreg(once)) * masks[k]
            rough_image.append(autoreg(image[k]))
        rough_base.append(fine_once)
        image.append(fine_ref[...] + spot(changed))
        rough_image.append(rough_ref[...] + spot(autoreg(changed)))
        second_fine = second_ref[...] + spot(smooth(changed))[0:rows, 0:cols]
        second = dot3(tile_s, spread(image, cols)) + second_fine

        own = [(slice(0, rows // s), slice(0, cols // s)) for s in SPACINGS]
        b = [base[k][own[k]] for k in range(LEVELS)]
        ab = [image[k][own[k]] for k in range(LEVELS)]
        rb = [rough_base[k][own[k]] for k in range(LEVELS)]
        rab = [rough_image[k][own[k]] for k in range(LEVELS)]
        sb, sab = surface[0:rows, 0:cols], second[:, 0:cols]
        w = weight[0:rows, 0:cols]

        for k in range(LEVELS):
            base_refs[k][...] = b[k]
            image_refs[k][...] = ab[k]
        surface_refs[0][0:rows, :] = sb
        surface_refs[0][rows:, :] = sab
        for k in range(1, lon_total):
            take = pl.ds(pl.multiple_of((lon ^ k) * sr, sr), sr)
            surface_refs[k][0:sr, :] = surface_refs[0][take, :]
            take = pl.ds(pl.multiple_of(rows + (lon ^ k) * sr, sr), sr)
            surface_refs[k][sr:, :] = surface_refs[0][take, :]

        def pieces(*arrays):
            height, width = arrays[0].shape
            for at in range(0, height, 8):
                for lane in range(0, width, LANES):
                    yield [x[at : at + 8, lane : min(lane + LANES, width)] for x in arrays]

        def gather(terms):
            totals = None
            for values in terms:
                totals = values if totals is None else [t + v for t, v in zip(totals, values)]
            short = LANES - totals[0].shape[1]
            if short:
                totals = [jnp.concatenate([t, jnp.zeros((8, short), jnp.float32)], axis=1) for t in totals]
            return totals

        def add_levels(per_level, scaled_from):
            out = list(per_level[0])
            for n in range(len(out)):
                scales = level_scales if n >= scaled_from else (1.0,) * LEVELS
                out[n] = sum(scales[k] * per_level[k][n] for k in range(LEVELS))
            return out

        first_sums = add_levels(
            [gather([x * x, y * y] for x, y in pieces(b[k], rb[k])) for k in range(LEVELS)], 1
        )
        a0 = first_sums[0]
        a1 = first_sums[1] + gather([v * f * f] for v, f in pieces(w, sb))[0]
        top = jnp.sum(a0, keepdims=True)
        bottom = jnp.sum(a1, keepdims=True)
        tau = jnp.where(bottom > 0.0, top / jnp.where(bottom > 0.0, bottom, 1.0), 0.0)

        def residual_terms(x, ax, y, ay):
            r, rr = x - tau * ax, y - tau * ay
            return [r * r, r * ax, ax * ax, rr * rr, rr * ay, ay * ay, rr * y, ay * y]

        def field_terms(v, f, af):
            r = f - tau * af
            vr, va = v * r, v * af
            return [vr * r, vr * af, va * af, vr * f, va * f]

        later_sums = add_levels(
            [gather(residual_terms(*p) for p in pieces(b[k], ab[k], rb[k], rab[k])) for k in range(LEVELS)], 3
        )
        fields = gather(field_terms(*p) for p in pieces(w, sb, sab))
        blocks = [a0, a1, *later_sums[:3], *(x + y for x, y in zip(later_sums[3:], fields))]
        lines = [jnp.sum(block, axis=0, keepdims=True) for block in blocks]
        lane = lax.broadcasted_iota(jnp.int32, (1, LANES), 1)
        lines.append(jnp.where(lane == 0, tau, 0.0))
        lines.append(jnp.zeros((16 - len(lines), LANES), jnp.float32))
        sums = jnp.sum(jnp.concatenate(lines, axis=0), axis=1, keepdims=True)
        place = lax.broadcasted_iota(jnp.int32, (16, LANES), 0)
        lanes = lax.broadcasted_iota(jnp.int32, (16, LANES), 1)
        line = jnp.sum(jnp.where(place == lanes, sums, 0.0), axis=0, keepdims=True)
        part_ref[...] = jnp.broadcast_to(line, (n_dev, LANES))

    level_shapes = [(rows // s, cols // s) for s in SPACINGS]
    outs = level_shapes * 2 + [(2 * rows, cols)] + [(2 * sr, cols)] * (lon_total - 1) + [(n_dev, LANES)]
    results = call(kernel, outs, 24)(mid_surface, wt, side, near, following, tables, *mid, *mid_fine)
    return results[:LEVELS], results[LEVELS : 2 * LEVELS], results[2 * LEVELS : -1], results[-1]


def finish(plan, parts, base, image, own_surface, far_surfaces):
    rows, cols, sr, lon_total = plan.rows, plan.cols, plan.swath_rows, plan.lon_total

    def kernel(part_ref, *rest):
        base_refs, image_refs = rest[:LEVELS], rest[LEVELS : 2 * LEVELS]
        own_ref, far_refs = rest[2 * LEVELS], rest[2 * LEVELS + 1 : 2 * LEVELS + lon_total]
        out_refs, swath_ref = rest[-LEVELS - 1 : -1], rest[-1]
        lon = lax.axis_index("lon")
        part = part_ref[...]
        lane = lax.broadcasted_iota(jnp.int32, part.shape, 1)

        def column(n):
            return jnp.sum(jnp.where(lane == n, part, 0.0), axis=1, keepdims=True)

        def total(values):
            return jnp.sum(values, axis=0, keepdims=True)

        a0, a1, p1, p2, p3, c1, c2, c3, c4, c5, tau = [column(n) for n in range(11)]
        sum0, sum1 = total(a0), total(a1)
        step = sum0 / sum1
        gap = tau - step
        norm = total(p1 + 2.0 * gap * p2 + gap * gap * p3)
        curv_res = total(c1 + 2.0 * gap * c2 + gap * gap * c3)
        curv_mix = total(c4 + gap * c5)
        ratio = norm / sum0
        curv = curv_res + 2.0 * ratio * curv_mix + ratio * ratio * sum1
        next_step = norm / curv
        alpha = step + next_step * (1.0 + ratio)
        beta = -next_step * step
        for k in range(LEVELS):
            out_refs[k][...] = alpha * base_refs[k][...] + beta * image_refs[k][...]
        take = pl.ds(pl.multiple_of(lon * sr, sr), sr)
        later = pl.ds(pl.multiple_of(rows + lon * sr, sr), sr)
        fields = [(own_ref[take, :], own_ref[later, :])]
        fields += [(ref[0:sr, :], ref[sr:, :]) for ref in far_refs]
        for k in range(lon_total):
            here = pl.ds(pl.multiple_of((lon ^ k) * cols, LANES), cols)
            swath_ref[:, here] = alpha * fields[k][0] + beta * fields[k][1]

    outs = [(rows // s, cols // s) for s in SPACINGS] + [(sr, plan.width)]
    return call(kernel, outs, 8)(parts, *base, *image, own_surface, *far_surfaces)


def turn(x, axis, total, k):
    return lax.ppermute(x, axis, [(i, (i + k) % total) for i in range(total)])


def flip(x, axis, total, k):
    return lax.ppermute(x, axis, [(i, i ^ k) for i in range(total)])


def odd_swap(x, axis, total):
    pairs = [(i, i + 1) for i in range(1, total - 1, 2)]
    return lax.ppermute(x, axis, pairs + [(j, i) for i, j in pairs])


def body(observed, gauged):
    lat_total, lon_total = lax.axis_size("lat"), lax.axis_size("lon")
    plan = Plan(observed.shape, gauged.shape, lat_total, lon_total)
    weight, own, *windows = pack(plan, observed, gauged)
    tables = fetch(plan, own)
    right, *far, left = [turn(x, "lon", lon_total, k) for k, x in enumerate(windows, 1)]
    mis, side, near, following = misfit(plan, own, right, left, far, weight, tables)
    mid, mid_surface, mid_fine = inside(plan, mis, weight, side, tables)
    near = flip(near, "lat", lat_total, 1)
    following = odd_swap(following, "lat", lat_total)
    base, image, surfaces, parts = operate(plan, mid, mid_surface, mid_fine, weight, side, near, following, tables)
    far_surfaces = [flip(x, "lon", lon_total, k) for k, x in enumerate(surfaces[1:], 1)]
    parts = lax.all_to_all(parts, ("lat", "lon"), split_axis=0, concat_axis=0, tiled=True)
    return tuple(finish(plan, parts, base, image, surfaces[0], far_surfaces))


def solution(mesh):
    return jax.shard_map(
        body,
        mesh=mesh,
        in_specs=(P(("lat", "lon"), None), P("lat", "lon")),
        out_specs=(
            P("lat", "lon"),
            P("lat", "lon"),
            P("lat", "lon"),
            P("lat", "lon"),
            P(("lat", "lon"), None),
        ),
        check_vma=False,
    )
```

```python
import math

import jax
import jax.numpy as jnp
import numpy as np
from jax import lax
from jax.experimental import pallas as pl
from jax.experimental.pallas import tpu as pltpu
from jax.sharding import PartitionSpec as P

LEVELS = 4
SPACINGS = tuple(2 ** (LEVELS - 1 - k) for k in range(LEVELS))
COARSE = LEVELS - 1
HALO = 64
INNER = 32
RAW = 40
PART_ROWS = 8
EDGE = 32
NEAR = 8
LANES = 128

data_weight = 2.0
kappa_term = 5.0
level_scales = (0.02, 0.03, 0.05, 0.08)

MIB = 1024 * 1024


def wendland(distance, of=np):
    remain = of.maximum(1.0 - distance, 0.0)
    cube = remain * remain * remain
    return cube * cube * (35.0 * distance * distance + 18.0 * distance + 3.0) / 3.0


def frame_index(total, tile, halo):
    place = np.arange(total)
    index = np.where(place < tile + halo, place, place - total)
    return index, (place < tile + halo) | (place >= total - halo)


def basis(cells, nodes, spacing):
    (cell, cell_ok), (node, node_ok) = cells, nodes
    numerator = np.abs(2 * cell[:, None] - 2 * spacing * node[None, :] - (spacing - 1))
    table = wendland(numerator / (5.0 * spacing)) / math.sqrt(spacing)
    return np.where(cell_ok[:, None] & node_ok[None, :], table, 0.0).astype(np.float32)


def halves(table):
    high = table.astype(jnp.bfloat16)
    low = (table - high.astype(np.float32)).astype(jnp.bfloat16)
    return np.stack([high, low])


def split(x):
    high = x.astype(jnp.bfloat16)
    return high, (x - high.astype(jnp.float32)).astype(jnp.bfloat16)


def dot(a, b, contract):
    return lax.dot_general(a, b, ((contract[0:1], contract[1:2]), ((), ())), preferred_element_type=jnp.float32)


def dot3(a, b, contract=(1, 0)):
    (ah, al), (bh, bl) = a, b
    n = ah.shape[0]
    both = dot(jnp.concatenate([ah, al], axis=0), bh, contract)
    return both[0:n] + (both[n:] + dot(ah, bl, contract))


TAPS = (float(wendland(np.float64(0.4))), float(wendland(np.float64(0.8))))


def shift(x, step, axis):
    return pltpu.roll(x, step % x.shape[axis], axis)


def smooth(x):
    for axis in (0, 1):
        near = shift(x, 1, axis) + shift(x, -1, axis)
        far = shift(x, 2, axis) + shift(x, -2, axis)
        x = x + (TAPS[0] * near + TAPS[1] * far)
    return x


def autoreg(x):
    beside = shift(x, 1, 0) + shift(x, -1, 0) + shift(x, 1, 1) + shift(x, -1, 1)
    return kappa_term * x - beside


def side_mask(total, tile, halo, at, last, dim):
    shape = (total, 1) if dim == 0 else (1, total)
    place = lax.broadcasted_iota(jnp.int32, shape, dim)
    after = (place < tile + halo) & (at < last)
    before = (place >= total - halo) & (at > 0)
    return ((place < tile) | after | before).astype(jnp.float32)


class Plan:
    def __init__(self, swath_shape, tile_shape, lat_total, lon_total):
        self.swath_rows, self.width = swath_shape
        self.rows, self.cols = tile_shape
        self.lat_total, self.lon_total = lat_total, lon_total
        self.col_frame = self.cols + 2 * HALO
        self.outer_rows = self.rows + 2 * RAW
        self.inner_rows = self.rows + 2 * INNER
        wide = [-(-(self.rows // s + 2 * (INNER // s + 2)) // 16) * 16 for s in SPACINGS[:COARSE]]
        self.node_rows = wide + [self.outer_rows]
        self.near_rows = [min(w, self.rows // s + 2 * NEAR) for w, s in zip(wide, SPACINGS)]
        self.near_rows.append(self.rows + 2 * NEAR)
        self.near_starts = np.cumsum([0] + self.near_rows[:COARSE]).tolist()
        self.node_cols = [-(-self.col_frame // (s * LANES)) * LANES for s in SPACINGS]
        self.row_starts = np.cumsum([0] + self.node_rows[:COARSE]).tolist()
        self.col_starts = np.cumsum([0] + self.node_cols[:COARSE]).tolist()
        col_cells = frame_index(self.col_frame, self.cols, HALO)
        outer = frame_index(self.outer_rows, self.rows, RAW)
        inner = frame_index(self.inner_rows, self.rows, INNER)
        col_tables, outer_rows, inner_rows, wide_rows = [], [], [], []
        self.part_nodes, place_all = [], []
        for k in range(COARSE):
            s = SPACINGS[k]
            tile = self.rows // s
            col_nodes = frame_index(self.node_cols[k], self.cols // s, HALO // s)
            row_nodes = frame_index(self.node_rows[k], tile, (self.node_rows[k] - tile) // 2)
            near_nodes = frame_index(self.near_rows[k], tile, (self.near_rows[k] - tile) // 2)
            col_tables.append(basis(col_cells, col_nodes, s))
            outer_rows.append(basis(outer, row_nodes, s))
            wide_rows.append(basis(inner, row_nodes, s))
            inner_rows.append(basis(inner, near_nodes, s))
            for away in range((RAW - 2 * s) // s, INNER // s + 2):
                self.part_nodes.append((s, away))
                at = self.row_starts[k]
                place_all.append((at + tile + away, at + self.node_rows[k] - 1 - away))
        nodes = self.row_starts[-1]
        joins = np.zeros((2 * PART_ROWS, nodes), np.float32)
        for n, (after_at, before_at) in enumerate(place_all):
            joins[n, after_at] = 1.0
            joins[PART_ROWS + n, before_at] = 1.0
        outer_all = np.concatenate([np.concatenate(outer_rows, axis=1), joins], axis=0)
        inner_all = np.concatenate(inner_rows, axis=1)
        wide_all = np.concatenate(wide_rows, axis=1)
        self.edge_nodes, sel = [], []
        for k in range(COARSE):
            first, total = self.rows // SPACINGS[k] - NEAR, self.node_rows[k]
            self.edge_nodes.append(total - first + NEAR)
            sel += [self.row_starts[k] + at for at in (*range(first, total), *range(NEAR))]
        self.edge_starts = np.cumsum([0] + self.edge_nodes).tolist()
        edge_rows = [*range(self.rows - EDGE, self.inner_rows), *range(EDGE)]
        row_tables = [
            outer_all[: self.rows].T,
            outer_all[self.rows :].T[sel],
            inner_all.T,
            wide_all,
            wide_all[edge_rows][:, sel],
            inner_all[: self.rows],
        ]
        lanes = -(-max(t.shape[1] for t in row_tables) // LANES) * LANES
        self.row_places, ends = [], [0, 0]
        for table in row_tables:
            side = int(ends[1] < ends[0])
            self.row_places.append((ends[side], table.shape[0], self.col_starts[-1] + side * lanes, table.shape[1]))
            ends[side] += table.shape[0]
        at = max(ends)
        col_all = np.concatenate(col_tables, axis=1)
        self.turned_start = self.col_starts[-1] + 2 * lanes
        whole = np.zeros((max(at, *col_all.shape), self.turned_start + self.col_frame), np.float32)
        whole[: self.col_frame, : self.col_starts[-1]] = col_all
        whole[: self.col_starts[-1], self.turned_start :] = col_all.T
        for (start, height, lane, width), table in zip(self.row_places, row_tables):
            whole[start : start + height, lane : lane + width] = table
        self.tables = halves(whole)
        tiles = self.col_frame // LANES
        self.sums = len(self.part_nodes)
        self.letter_rows = -(-(self.letter()[-1] + tiles * self.sums) // 8) * 8

    def pick(self, table_ref):
        col_tables, turned_tables, row_tables = [], [], []
        for k in range(COARSE):
            places = slice(self.col_starts[k], self.col_starts[k + 1])
            turned_tables.append(tuple(table_ref[half, places, self.turned_start :] for half in (0, 1)))
            col_tables.append(tuple(table_ref[half, 0 : self.col_frame, places] for half in (0, 1)))
        for start, height, lane, width in self.row_places:
            rows, lanes = slice(start, start + height), slice(lane, lane + width)
            row_tables.append(tuple(table_ref[half, rows, lanes] for half in (0, 1)))
        return col_tables, turned_tables, row_tables

    def masks(self, heights):
        lat, lon = lax.axis_index("lat"), lax.axis_index("lon")
        out = []
        for k, s in enumerate(SPACINGS):
            tile = self.rows // s
            rows = side_mask(heights[k], tile, (heights[k] - tile) // 2, lat, self.lat_total - 1, 0)
            cols = side_mask(self.node_cols[k], self.cols // s, HALO // s, lon, self.lon_total - 1, 1)
            out.append(rows * cols)
        return out

    def letter(self):
        tiles = self.col_frame // LANES
        weights = tiles * RAW
        corner = weights + (tiles - 1) * INNER
        return 0, weights, corner, corner + INNER // 2


def call(kernel, outs, limit, scratch=(), spaces=None):
    def run(*operands):
        in_spaces = spaces or [pltpu.VMEM] * len(operands)
        return pl.pallas_call(
            kernel,
            out_shape=[jax.ShapeDtypeStruct(shape, jnp.float32) for shape in outs],
            in_specs=[pl.BlockSpec(memory_space=space) for space in in_spaces],
            out_specs=[pl.BlockSpec(memory_space=pltpu.VMEM)] * len(outs),
            scratch_shapes=list(scratch),
            compiler_params=pltpu.CompilerParams(vmem_limit_bytes=int(limit * MIB)),
        )(*operands)

    return run


def window(plan, obs_ref, to):
    sr, width, cols = plan.swath_rows, plan.width, plan.cols
    base = pl.multiple_of(to * cols, LANES)
    lane = lax.broadcasted_iota(jnp.int32, (sr, LANES), 1)
    before = obs_ref[:, pl.ds(pl.multiple_of(jnp.maximum(base - LANES, 0), LANES), LANES)]
    after = obs_ref[:, pl.ds(pl.multiple_of(jnp.minimum(base + cols, width - LANES), LANES), LANES)]
    before = jnp.where(to > 0, before, 0.0)
    after = jnp.where(to < plan.lon_total - 1, after, 0.0)
    return obs_ref[:, pl.ds(base, cols)], jnp.where(lane < HALO, after, before)


def pack(plan, observed, gauged):
    sr, width, cols, rows, n = plan.swath_rows, plan.width, plan.cols, plan.rows, plan.lon_total
    tiles = plan.col_frame // LANES

    def kernel(obs_hbm, gauge_hbm, *rest):
        wt_ref, out_refs, (obs_ref, gauge_ref, sems) = rest[0], rest[1 : n + 1], rest[n + 1 :]
        copies = [
            pltpu.make_async_copy(obs_hbm, obs_ref, sems.at[0]),
            pltpu.make_async_copy(gauge_hbm, gauge_ref, sems.at[1]),
        ]
        for copy in copies:
            copy.start()
        at = lax.axis_index("lon")
        half_lane = lax.broadcasted_iota(jnp.int32, (rows // 2, LANES), 1)
        copies[0].wait()
        for k, ref in enumerate(out_refs):
            main, sides = window(plan, obs_ref, lax.rem(at + k, n))
            if k in (1, n - 1):
                for t in range(tiles - 1):
                    ref[t * sr : (t + 1) * sr, :] = main[:, t * LANES : (t + 1) * LANES]
                ref[(tiles - 1) * sr : tiles * sr, :] = sides
            else:
                ref[:, 0:cols] = main
                ref[:, cols:] = sides
        copies[1].wait()
        wt_ref[...] = data_weight * gauge_ref[...].astype(jnp.float32)
        for k in (1, n - 1):
            edge = wt_ref[:, cols - LANES :] if k == 1 else wt_ref[:, 0:LANES]
            kept = (half_lane >= HALO) if k == 1 else (half_lane < HALO)
            turned = pltpu.roll(edge[rows // 2 :], HALO, 1)
            out_refs[k][tiles * sr :, :] = jnp.where(kept, edge[0 : rows // 2], turned)

    side = (tiles * sr + rows // 2, LANES)
    outs = [(rows, cols)] + [side if k in (1, n - 1) else (sr, plan.col_frame) for k in range(n)]
    scratch = [
        pltpu.VMEM((sr, width), jnp.float32),
        pltpu.VMEM((rows, cols), jnp.int32),
        pltpu.SemaphoreType.DMA((2,)),
    ]
    return call(kernel, outs, 53.25, scratch, [pltpu.HBM] * 2)(observed, gauged)


def misfit(plan, own, right, left, far, weight, tables):
    sr, cols, rows, n = plan.swath_rows, plan.cols, plan.rows, plan.lon_total
    tiles = plan.col_frame // LANES

    def kernel(own_ref, right_ref, left_ref, wt_ref, table_ref, *rest):
        far_refs, (mis_ref, side_ref, near_ref, next_ref) = rest[: n - 3], rest[n - 3 :]
        at = lax.axis_index("lon")
        lane = lax.broadcasted_iota(jnp.int32, (rows, LANES), 1)

        def side(ref, present):
            packed = ref[tiles * sr :, :]
            both = jnp.concatenate([packed, pltpu.roll(packed, HALO, 1)], axis=0)
            return jnp.where(present, both, 0.0)

        side_ref[...] = jnp.where(lane < HALO, side(left_ref, at < n - 1), side(right_ref, at > 0))

        for k, ref in enumerate((own_ref, right_ref, *far_refs, left_ref)):
            here = pl.ds(pl.multiple_of(lax.rem(at + (n - k), n) * sr, sr), sr)
            if k in (1, n - 1):
                for t in range(tiles - 1):
                    lanes = slice(t * LANES, (t + 1) * LANES)
                    mis_ref[here, lanes] = wt_ref[here, lanes] * ref[t * sr : (t + 1) * sr, :]
                mis_ref[here, cols:] = side_ref[here, :] * ref[(tiles - 1) * sr : tiles * sr, :]
            else:
                mis_ref[here, 0:cols] = wt_ref[here, :] * ref[:, 0:cols]
                mis_ref[here, cols:] = side_ref[here, :] * ref[:, cols:]

        up = lax.axis_index("lat") % 2
        depth = HALO - RAW
        shape = (PART_ROWS, depth)
        line = lax.broadcasted_iota(jnp.int32, shape, 0)
        cell = lax.broadcasted_iota(jnp.int32, shape, 1)
        for ref, low in ((near_ref, 1 - up), (next_ref, up)):
            far = mis_ref[pl.ds(pl.multiple_of(RAW + low * (rows - HALO - RAW), 8), depth), :]
            table = jnp.zeros(shape, jnp.float32)
            distance = jnp.where(low == 1, HALO - 1 - cell, RAW + cell)
            for m, (s, away) in enumerate(plan.part_nodes):
                numerator = jnp.abs(2 * distance - 2 * s * away - (s - 1)).astype(jnp.float32)
                table = jnp.where(line == m, wendland(numerator / (5.0 * s), jnp) / math.sqrt(s), table)
            edge = pl.ds(pl.multiple_of(low * (rows - INNER), 8), INNER)
            (th, tl), (fh, fl) = split(table), split(far)
            sums = dot(th, fh, (1, 0)) + (dot(th, fl, (1, 0)) + dot(tl, fh, (1, 0)))
            near = mis_ref[pl.ds(pl.multiple_of(low * (rows - RAW), 8), RAW), :]
            raw, weights, corner, parts = plan.letter()
            for t in range(tiles):
                lanes = slice(t * LANES, (t + 1) * LANES)
                ref[raw + t * RAW : raw + (t + 1) * RAW, :] = near[:, lanes]
                if t < tiles - 1:
                    ref[weights + t * INNER : weights + (t + 1) * INNER, :] = wt_ref[edge, lanes]
                ref[parts + t * plan.sums : parts + (t + 1) * plan.sums, :] = sums[0 : plan.sums, lanes]
            beside = side_ref[edge, :]
            turned = pltpu.roll(beside[INNER // 2 :], HALO, 1)
            some = lax.broadcasted_iota(jnp.int32, (INNER // 2, LANES), 1)
            outer = (some < INNER) | (some >= LANES - INNER)
            ref[corner : corner + INNER // 2, :] = jnp.where(outer, beside[0 : INNER // 2], turned)
            ref[parts + tiles * plan.sums :, :] = jnp.zeros((plan.letter_rows - parts - tiles * plan.sums, LANES), jnp.float32)

    outs = [(rows, plan.col_frame), (rows, LANES)] + [(plan.letter_rows, LANES)] * 2
    return call(kernel, outs, 4)(own, right, left, weight, tables, *far)


def open_letter(plan, letter):
    tiles = plan.col_frame // LANES
    raw, weights, corner, parts = plan.letter()
    near = [letter[raw + t * RAW : raw + (t + 1) * RAW] for t in range(tiles)]
    sums = [letter[parts + t * plan.sums : parts + (t + 1) * plan.sums] for t in range(tiles)]
    sums = jnp.concatenate(sums, axis=1)
    sums = jnp.concatenate([sums, jnp.zeros((PART_ROWS - plan.sums, plan.col_frame), jnp.float32)], axis=0)
    rows = [letter[weights + t * INNER : weights + (t + 1) * INNER] for t in range(tiles - 1)]
    both = letter[corner : corner + INNER // 2]
    some = lax.broadcasted_iota(jnp.int32, (INNER // 2, LANES), 1)
    outer = (some < INNER) | (some >= LANES - INNER)
    beside = [jnp.where(outer, x, 0.0) for x in (both, pltpu.roll(both, HALO, 1))]
    rows.append(jnp.concatenate(beside, axis=0))
    return jnp.concatenate(near, axis=1), sums, jnp.concatenate(rows, axis=1)


def fetch(plan, after):
    def kernel(table_ref, after_ref, out_ref, sem):
        copy = pltpu.make_async_copy(table_ref, out_ref, sem)
        copy.start()
        copy.wait()

    table = jnp.asarray(plan.tables)
    return pl.pallas_call(
        kernel,
        out_shape=jax.ShapeDtypeStruct(table.shape, table.dtype),
        in_specs=[pl.BlockSpec(memory_space=pltpu.HBM), pl.BlockSpec(memory_space=pltpu.VMEM)],
        out_specs=pl.BlockSpec(memory_space=pltpu.VMEM),
        scratch_shapes=[pltpu.SemaphoreType.DMA],
        compiler_params=pltpu.CompilerParams(vmem_limit_bytes=MIB),
        cost_estimate=pl.CostEstimate(flops=0, bytes_accessed=2 * table.nbytes, transcendentals=0),
    )(table, after)


def inside(plan, mis, wt, side, tables):
    rows, inner_rows = plan.rows, plan.inner_rows
    shapes = [(plan.node_rows[k], plan.node_cols[k]) for k in range(COARSE)] + [(rows + 2 * NEAR, plan.col_frame)]

    def kernel(mis_ref, wt_ref, side_ref, table_ref, *out_refs):
        base_refs, (surface_ref, once_ref, image_ref, rough_ref, second_ref) = out_refs[:LEVELS], out_refs[LEVELS:]
        col_tables, turned_tables, (own_t, _, _, wide_s, _, _) = plan.pick(table_ref)
        masks = plan.masks([height for height, _ in shapes])
        mis = mis_ref[...]
        gathered = dot3(own_t, split(mis))
        starts = plan.row_starts
        base = [dot3(split(gathered[starts[k] : starts[k + 1]]), col_tables[k]) * masks[k] for k in range(COARSE)]
        blank = jnp.zeros((2 * NEAR, plan.col_frame), jnp.float32)
        base.append(smooth(jnp.concatenate([mis, blank], axis=0)) * masks[COARSE])
        for k in range(LEVELS):
            base_refs[k][...] = base[k]
        once = autoreg(base[COARSE]) * masks[COARSE]
        once_ref[...] = once
        twice = level_scales[COARSE] * autoreg(once)
        fine = smooth(base[COARSE])
        blank = jnp.zeros((inner_rows - rows - 2 * NEAR, plan.col_frame), jnp.float32)
        fine = jnp.concatenate([fine[0 : rows + NEAR], blank, fine[rows + NEAR :]], axis=0)
        spread = jnp.concatenate([dot3(split(base[k]), turned_tables[k]) for k in range(COARSE)], axis=0)
        surface = fine + dot3(wide_s, split(spread))
        surface_ref[...] = surface
        again = jnp.concatenate([wt_ref[...], side_ref[...]], axis=1) * surface[0:rows]
        blank = jnp.zeros((2 * NEAR, plan.col_frame), jnp.float32)
        image = (smooth(jnp.concatenate([again, blank], axis=0)) + twice) * masks[COARSE]
        image_ref[...] = image
        rough_ref[...] = autoreg(image)
        second_ref[...] = smooth(image)[0:rows, 0 : plan.cols]

    outs = shapes + [(inner_rows, plan.col_frame)] + shapes[COARSE:] * 3 + [(rows, plan.cols)]
    results = call(kernel, outs, 24)(mis, wt, side, tables)
    return results[:LEVELS], results[LEVELS], results[LEVELS + 1 :]


def operate(plan, mid, mid_surface, mid_fine, wt, side, near, following, tables):
    rows, cols, sr, lon_total = plan.rows, plan.cols, plan.swath_rows, plan.lon_total
    n_dev = plan.lat_total * lon_total

    def kernel(mid_surface_ref, wt_ref, side_ref, near_ref, next_ref, table_ref, *out_refs):
        mid_refs, (once_ref, fine_ref, rough_ref, second_ref) = out_refs[:LEVELS], out_refs[LEVELS : LEVELS + 4]
        out_refs = out_refs[LEVELS + 4 :]
        base_refs, image_refs = out_refs[:LEVELS], out_refs[LEVELS : 2 * LEVELS]
        surface_refs, part_ref = out_refs[2 * LEVELS : -1], out_refs[-1]
        lat = lax.axis_index("lat")
        lon = lax.axis_index("lon")
        even = lat % 2 == 0
        col_tables, turned_tables, row_tables = plan.pick(table_ref)
        _, edge_t, inner_t, _, edge_s, tile_s = row_tables
        near_all, next_all = near_ref[...], next_ref[...]
        below = jnp.where(even, near_all, next_all)
        above = jnp.where(even, next_all, near_all)
        below, below_sums, below_wt = open_letter(plan, below)
        above, above_sums, above_wt = open_letter(plan, above)
        own_weight = jnp.concatenate([wt_ref[...], side_ref[...]], axis=1)
        weight = jnp.concatenate([own_weight, below_wt, above_wt], axis=0)

        masks = plan.masks(plan.node_rows)

        def collect(gathered, starts):
            return [dot3(split(gathered[starts[k] : starts[k + 1]]), col_tables[k]) for k in range(COARSE)]

        def spread(coeffs, width):
            turned = [tuple(part[:, 0:width] for part in table) for table in turned_tables]
            return split(jnp.concatenate([dot3(split(coeffs[k]), turned[k]) for k in range(COARSE)], axis=0))

        def cut(x, k, total):
            if x.shape[0] == total:
                return x
            side = (total - rows // SPACINGS[k]) // 2
            return jnp.concatenate([x[0 : total - side], x[x.shape[0] - side :]], axis=0)

        def blank(height, like):
            return jnp.zeros((height, like.shape[1]), jnp.float32)

        around = jnp.concatenate([below, above, below_sums, above_sums], axis=0)
        edge = collect(dot3(edge_t, split(around)), plan.edge_starts)
        base = []
        for k in range(COARSE):
            first = plan.edge_nodes[k] - NEAR
            tile = rows // SPACINGS[k]
            mask = jnp.concatenate([masks[k][tile - NEAR :], masks[k][0:NEAR]], axis=0)
            edge[k] = edge[k] * mask
            added = [edge[k][first:], edge[k][0:first]]
            if tile > 2 * NEAR:
                added.insert(1, blank(tile - 2 * NEAR, edge[k]))
            base.append(cut(mid_refs[k][...] + jnp.concatenate(added, axis=0), k, plan.near_rows[k]))
        strip = jnp.concatenate([blank(NEAR, below), below, above, blank(NEAR, above)], axis=0)
        fine_mask = masks[COARSE]
        strip_mask = jnp.concatenate([fine_mask[rows - NEAR :], fine_mask[0:NEAR]], axis=0)
        strip = smooth(strip) * strip_mask
        last = strip.shape[0] - NEAR
        added = [strip[last:], blank(rows - 2 * NEAR, strip), strip[0 : 2 * NEAR], strip[last - NEAR : last]]
        base.append(mid_refs[COARSE][...] + jnp.concatenate(added, axis=0))
        short, short_mask = [jnp.concatenate([x[0 : 3 * NEAR], x[last - 2 * NEAR :]], axis=0) for x in (strip, strip_mask)]
        once = autoreg(short) * short_mask

        def place(x):
            parts = [x[5 * NEAR :], blank(rows - 2 * NEAR, x), x[0 : 2 * NEAR], x[4 * NEAR : 5 * NEAR]]
            return jnp.concatenate(parts, axis=0)

        fine_once = once_ref[...] + place(once)
        twice_edge = level_scales[COARSE] * autoreg(once)
        fine = smooth(strip)
        added = [fine[last:], blank(rows - 2 * NEAR, fine), fine[0 : NEAR + INNER], fine[last - INNER : last]]
        extra = jnp.concatenate(added, axis=0)
        coarse = dot3(edge_s, spread(edge, plan.col_frame))
        body_rows = coarse.shape[0] - EDGE
        added = [coarse[body_rows:], blank(rows - 2 * EDGE, coarse), coarse[0:body_rows]]
        extra = extra + jnp.concatenate(added, axis=0)
        surface = mid_surface_ref[...] + extra
        masks = plan.masks(plan.near_rows)

        misfit_again = weight * surface
        image = collect(dot3(inner_t, split(misfit_again)), plan.near_starts)
        reach = EDGE + NEAR
        changed = [
            weight[rows - reach : rows] * extra[rows - reach : rows],
            misfit_again[rows : rows + NEAR],
            misfit_again[plan.inner_rows - NEAR :],
            weight[0:reach] * extra[0:reach],
        ]
        changed = smooth(jnp.concatenate(changed, axis=0))
        ends = [blank(EDGE, below), twice_edge[0 : 2 * NEAR], twice_edge[4 * NEAR :], blank(EDGE, below)]
        fine_mask = masks[COARSE]
        changed_mask = jnp.concatenate([fine_mask[rows - reach :], fine_mask[0:reach]], axis=0)
        changed = (changed + jnp.concatenate(ends, axis=0)) * changed_mask

        def spot(x):
            first = reach + 2 * NEAR
            return jnp.concatenate([x[first:], blank(rows - 2 * reach, x), x[0:first]], axis=0)

        rough_base, rough_image = [], []
        for k in range(COARSE):
            once = autoreg(base[k]) * masks[k]
            rough_base.append(once)
            image[k] = (image[k] + level_scales[k] * autoreg(once)) * masks[k]
            rough_image.append(autoreg(image[k]))
        rough_base.append(fine_once)
        image.append(fine_ref[...] + spot(changed))
        rough_image.append(rough_ref[...] + spot(autoreg(changed)))
        second_fine = second_ref[...] + spot(smooth(changed))[0:rows, 0:cols]
        second = dot3(tile_s, spread(image, cols)) + second_fine

        own = [(slice(0, rows // s), slice(0, cols // s)) for s in SPACINGS]
        b = [base[k][own[k]] for k in range(LEVELS)]
        ab = [image[k][own[k]] for k in range(LEVELS)]
        rb = [rough_base[k][own[k]] for k in range(LEVELS)]
        rab = [rough_image[k][own[k]] for k in range(LEVELS)]
        sb, sab = surface[0:rows, 0:cols], second[:, 0:cols]
        w = weight[0:rows, 0:cols]

        for k in range(LEVELS):
            base_refs[k][...] = b[k]
            image_refs[k][...] = ab[k]
        surface_refs[0][0:rows, :] = sb
        surface_refs[0][rows:, :] = sab
        for k in range(1, lon_total):
            take = pl.ds(pl.multiple_of((lon ^ k) * sr, sr), sr)
            surface_refs[k][0:sr, :] = surface_refs[0][take, :]
            take = pl.ds(pl.multiple_of(rows + (lon ^ k) * sr, sr), sr)
            surface_refs[k][sr:, :] = surface_refs[0][take, :]

        def pieces(*arrays):
            height, width = arrays[0].shape
            for at in range(0, height, 8):
                for lane in range(0, width, LANES):
                    yield [x[at : at + 8, lane : min(lane + LANES, width)] for x in arrays]

        def gather(terms):
            totals = None
            for values in terms:
                totals = values if totals is None else [t + v for t, v in zip(totals, values)]
            short = LANES - totals[0].shape[1]
            if short:
                totals = [jnp.concatenate([t, jnp.zeros((8, short), jnp.float32)], axis=1) for t in totals]
            return totals

        def add_levels(per_level, scaled_from):
            out = list(per_level[0])
            for n in range(len(out)):
                scales = level_scales if n >= scaled_from else (1.0,) * LEVELS
                out[n] = sum(scales[k] * per_level[k][n] for k in range(LEVELS))
            return out

        first_sums = add_levels(
            [gather([x * x, y * y] for x, y in pieces(b[k], rb[k])) for k in range(LEVELS)], 1
        )
        a0 = first_sums[0]
        a1 = first_sums[1] + gather([v * f * f] for v, f in pieces(w, sb))[0]
        top = jnp.sum(a0, keepdims=True)
        bottom = jnp.sum(a1, keepdims=True)
        tau = jnp.where(bottom > 0.0, top / jnp.where(bottom > 0.0, bottom, 1.0), 0.0)

        def residual_terms(x, ax, y, ay):
            r, rr = x - tau * ax, y - tau * ay
            return [r * r, r * ax, ax * ax, rr * rr, rr * ay, ay * ay, rr * y, ay * y]

        def field_terms(v, f, af):
            r = f - tau * af
            vr, va = v * r, v * af
            return [vr * r, vr * af, va * af, vr * f, va * f]

        later_sums = add_levels(
            [gather(residual_terms(*p) for p in pieces(b[k], ab[k], rb[k], rab[k])) for k in range(LEVELS)], 3
        )
        fields = gather(field_terms(*p) for p in pieces(w, sb, sab))
        blocks = [a0, a1, *later_sums[:3], *(x + y for x, y in zip(later_sums[3:], fields))]
        lines = [jnp.sum(block, axis=0, keepdims=True) for block in blocks]
        lane = lax.broadcasted_iota(jnp.int32, (1, LANES), 1)
        lines.append(jnp.where(lane == 0, tau, 0.0))
        lines.append(jnp.zeros((16 - len(lines), LANES), jnp.float32))
        sums = jnp.sum(jnp.concatenate(lines, axis=0), axis=1, keepdims=True)
        place = lax.broadcasted_iota(jnp.int32, (16, LANES), 0)
        lanes = lax.broadcasted_iota(jnp.int32, (16, LANES), 1)
        line = jnp.sum(jnp.where(place == lanes, sums, 0.0), axis=0, keepdims=True)
        part_ref[...] = jnp.broadcast_to(line, (n_dev, LANES))

    level_shapes = [(rows // s, cols // s) for s in SPACINGS]
    outs = level_shapes * 2 + [(2 * rows, cols)] + [(2 * sr, cols)] * (lon_total - 1) + [(n_dev, LANES)]
    results = call(kernel, outs, 24)(mid_surface, wt, side, near, following, tables, *mid, *mid_fine)
    return results[:LEVELS], results[LEVELS : 2 * LEVELS], results[2 * LEVELS : -1], results[-1]


def finish(plan, parts, base, image, own_surface, far_surfaces):
    rows, cols, sr, lon_total = plan.rows, plan.cols, plan.swath_rows, plan.lon_total

    def kernel(part_ref, *rest):
        base_refs, image_refs = rest[:LEVELS], rest[LEVELS : 2 * LEVELS]
        own_ref, far_refs = rest[2 * LEVELS], rest[2 * LEVELS + 1 : 2 * LEVELS + lon_total]
        out_refs, swath_ref = rest[-LEVELS - 1 : -1], rest[-1]
        lon = lax.axis_index("lon")
        part = part_ref[...]
        lane = lax.broadcasted_iota(jnp.int32, part.shape, 1)

        def column(n):
            return jnp.sum(jnp.where(lane == n, part, 0.0), axis=1, keepdims=True)

        def total(values):
            return jnp.sum(values, axis=0, keepdims=True)

        a0, a1, p1, p2, p3, c1, c2, c3, c4, c5, tau = [column(n) for n in range(11)]
        sum0, sum1 = total(a0), total(a1)
        step = sum0 / sum1
        gap = tau - step
        norm = total(p1 + 2.0 * gap * p2 + gap * gap * p3)
        curv_res = total(c1 + 2.0 * gap * c2 + gap * gap * c3)
        curv_mix = total(c4 + gap * c5)
        ratio = norm / sum0
        curv = curv_res + 2.0 * ratio * curv_mix + ratio * ratio * sum1
        next_step = norm / curv
        alpha = step + next_step * (1.0 + ratio)
        beta = -next_step * step
        for k in range(LEVELS):
            out_refs[k][...] = alpha * base_refs[k][...] + beta * image_refs[k][...]
        take = pl.ds(pl.multiple_of(lon * sr, sr), sr)
        later = pl.ds(pl.multiple_of(rows + lon * sr, sr), sr)
        fields = [(own_ref[take, :], own_ref[later, :])]
        fields += [(ref[0:sr, :], ref[sr:, :]) for ref in far_refs]
        for k in range(lon_total):
            here = pl.ds(pl.multiple_of((lon ^ k) * cols, LANES), cols)
            swath_ref[:, here] = alpha * fields[k][0] + beta * fields[k][1]

    outs = [(rows // s, cols // s) for s in SPACINGS] + [(sr, plan.width)]
    return call(kernel, outs, 8)(parts, *base, *image, own_surface, *far_surfaces)


def turn(x, axis, total, k):
    return lax.ppermute(x, axis, [(i, (i + k) % total) for i in range(total)])


def flip(x, axis, total, k):
    return lax.ppermute(x, axis, [(i, i ^ k) for i in range(total)])


def odd_swap(x, axis, total):
    pairs = [(i, i + 1) for i in range(1, total - 1, 2)]
    return lax.ppermute(x, axis, pairs + [(j, i) for i, j in pairs])


def body(observed, gauged):
    lat_total, lon_total = lax.axis_size("lat"), lax.axis_size("lon")
    plan = Plan(observed.shape, gauged.shape, lat_total, lon_total)
    weight, own, *windows = pack(plan, observed, gauged)
    tables = fetch(plan, own)
    right, *far, left = [turn(x, "lon", lon_total, k) for k, x in enumerate(windows, 1)]
    mis, side, near, following = misfit(plan, own, right, left, far, weight, tables)
    mid, mid_surface, mid_fine = inside(plan, mis, weight, side, tables)
    near = flip(near, "lat", lat_total, 1)
    following = odd_swap(following, "lat", lat_total)
    base, image, surfaces, parts = operate(plan, mid, mid_surface, mid_fine, weight, side, near, following, tables)
    far_surfaces = [flip(x, "lon", lon_total, k) for k, x in enumerate(surfaces[1:], 1)]
    parts = lax.all_to_all(parts, ("lat", "lon"), split_axis=0, concat_axis=0, tiled=True)
    return tuple(finish(plan, parts, base, image, surfaces[0], far_surfaces))


def solution(mesh):
    return jax.shard_map(
        body,
        mesh=mesh,
        in_specs=(P(("lat", "lon"), None), P("lat", "lon")),
        out_specs=(
            P("lat", "lon"),
            P("lat", "lon"),
            P("lat", "lon"),
            P("lat", "lon"),
            P(("lat", "lon"), None),
        ),
        check_vma=False,
    )
```
